32 devices in a mesh: space: 4 (over z), ens: 8 (over y, x, core).
Axes of the slice: x: 2, y: 2, z: 4, core: 2. Of those that a mesh axis runs over, the one named last changes fastest.
Arguments:
- log_perm: float32 [64, 8, 64, 512], P('ens', 'space'), may hold values from -4 to 4
- storage: float32 [8, 64, 512], P('space'), may hold values from 0.5 to 2
- head_init: float32 [8, 64, 512], P('space'), may hold values from -6 to 6
- well_cells: int32 [16], replicated, may hold values from 0 to 262143
- well_rates: float32 [16], replicated, may hold values from -12 to 12
- obs_cells: int32 [32], replicated, may hold values from 0 to 262143
- obs_values: float32 [32], replicated, may hold values from -6 to 6
- noise_var: float32 [32], replicated, may hold values from 0.05 to 0.5
- step_size: float32 [1], replicated, may hold values from 0.5 to 2
- perturb: float32 [64, 32], P('ens'), may hold values from -2 to 2
Outputs:
- head_field: float32 [64, 8, 64, 512], P('ens', 'space')
- updated: float32 [64, 8, 64, 512], P('ens', 'space')
The draws below stay inside these ranges and needn't reach their ends.
All inputs are finite; a program needn't handle non-finite values.
Results may differ from the reference program's by a relative error of at most 0.00025.
Values sent between devices are 32-bit elements; how exact they have to be, the bound alone decides.
No kernel may reach another device: no remote copies, remote signals or barrier semaphores. Data moves between devices by JAX's collectives and lax.ppermute only.
A program may use at most 192 MiB of HBM per device.

```python
import math
import jax
import jax.numpy as jnp
from jax import lax

NZ = 64
NY = 512
SWEEPS = 3
NOBS = 32
NWELL = 16
NX = 8
PARTICLES = 64
NCELLS = 262144


def plant(entries, rng, low, high):
    longest = entries.shape.index(max(entries.shape))
    spots = []
    for shift in (0, 1):
        where = [jax.random.randint(jax.random.fold_in(rng, axis), (), 0, length) for axis, length in enumerate(entries.shape)]
        where[longest] = (where[longest] + shift) % entries.shape[longest]
        spots.append(tuple(where))
    return entries.at[spots[0]].set(low).at[spots[1]].set(high)


def steps_of(rng, dims, shards, least, high):
    gain, own = 1.0, jax.random.fold_in(rng, 6)
    for position, blocks in shards:
        draws = jnp.exp(jax.random.uniform(jax.random.fold_in(own, position), (blocks,), jnp.float32, least / len(shards), high / len(shards)))
        gain = gain * jnp.repeat(draws, dims[position] // blocks).reshape([-1 if axis == position else 1 for axis in range(len(dims))])
    return gain


def normal_values(rng, dims, spread, most, pieces=(), kind=jnp.bfloat16):
    values = spread * jax.random.normal(rng, dims, jnp.float32)
    if pieces:
        values = values * steps_of(rng, dims, pieces, -0.22, 0.18)
    return jnp.clip(values, -most, most).astype(kind)


def setup_inputs(seed: int = 0) -> dict:
    splits = jax.random.split(jax.random.key(seed), 11)
    return {
        "log_perm": normal_values(splits[0], (PARTICLES, NX, NZ, NY), 1.0, 4.0, ((0, 8), (1, 4)), jnp.float32),
        "storage": jnp.clip(jnp.exp(math.log(2.0) - 1.3862944 * jax.random.uniform(splits[1], (NX, NZ, NY), jnp.float32) ** steps_of(splits[1], (NX, NZ, NY), ((0, 4),), -0.2, 0.2)), 0.5, 2.0),
        "head_init": normal_values(splits[2], (NX, NZ, NY), 1.0, 6.0, ((0, 4),), jnp.float32),
        "well_cells": plant(jax.random.randint(splits[3], (NWELL,), 0, NCELLS), jax.random.fold_in(splits[3], 1), 0, NCELLS - 1).astype(jnp.int32),
        "well_rates": normal_values(splits[4], (NWELL,), 3.0, 12.0, (), jnp.float32),
        "obs_cells": plant(jax.random.randint(splits[5], (NOBS,), 0, NCELLS), jax.random.fold_in(splits[5], 1), 0, NCELLS - 1).astype(jnp.int32),
        "obs_values": normal_values(splits[6], (NOBS,), 1.0, 6.0, (), jnp.float32),
        "noise_var": jnp.clip(jnp.exp(jax.random.uniform(splits[7], (NOBS,), jnp.float32, math.log(0.05), math.log(0.5))), 0.05, 0.5),
        "step_size": jnp.clip(jax.random.uniform(splits[8], (1,), jnp.float32, 0.5, 2.0), 0.5, 2.0),
        "perturb": normal_values(splits[9], (PARTICLES, NOBS), 0.3, 2.0, ((0, 8),), jnp.float32),
    }


OMEGA = 0.8
HIGHEST = lax.Precision.HIGHEST
DIRECTIONS = [(a, b, c) for a in (-1, 0, 1) for b in (-1, 0, 1) for c in (-1, 0, 1) if (a, b, c) != (0, 0, 0)]

def shifted(padded, a, b, c, planes, depth, across):
    return padded[..., 1 + a:1 + a + planes, 1 + b:1 + b + depth, 1 + c:1 + c + across]

def forward(log_row, storage, head_init, source):
    planes, depth, across = log_row.shape
    permeability = jnp.exp(log_row)
    padded = jnp.pad(permeability, 1)
    transmit = []
    for a, b, c in DIRECTIONS:
        factor = 2.0 ** (1 - abs(a) - abs(b) - abs(c))
        neighbour = shifted(padded, a, b, c, planes, depth, across)
        transmit.append(factor * 2.0 * permeability * neighbour / (permeability + neighbour))
    diagonal = storage + sum(transmit)
    forcing = storage * head_init + source
    head_field = head_init
    for sweep_index in range(SWEEPS):
        padded_head = jnp.pad(head_field, 1)
        gathered = sum((transmit[i] * shifted(padded_head, a, b, c, planes, depth, across) for i, (a, b, c) in enumerate(DIRECTIONS)))
        head_field = (1.0 - OMEGA) * head_field + OMEGA * (forcing + gathered) / diagonal
    return head_field

def solve_pair(factor, residual):
    first = lax.linalg.triangular_solve(factor, residual.T, left_side=True, lower=True)
    second = lax.linalg.triangular_solve(factor, first, left_side=True, lower=True, transpose_a=True)
    return second.T

def reference(log_perm, storage, head_init, well_cells, well_rates, obs_cells, obs_values, noise_var, step_size, perturb):
    source = jnp.zeros((NX * NZ * NY,), jnp.float32).at[well_cells].add(well_rates).reshape(NX, NZ, NY)

    def member(log_row):
        field = forward(log_row, storage, head_init, source)
        return (field, field.reshape(-1)[obs_cells])
    head_field, observed = lax.map(member, log_perm)
    members = log_perm.shape[0]
    deviation = observed - jnp.mean(observed, axis=0)
    covariance = jnp.dot(deviation.T, deviation, precision=HIGHEST) / (members - 1)
    system = covariance + jnp.diag(noise_var / step_size[0])
    factor = jnp.linalg.cholesky(system)
    gain_rows = solve_pair(factor, obs_values[None, :] + perturb - observed)
    flat = log_perm.reshape(members, -1)
    centred = flat - jnp.mean(flat, axis=0)
    cross = jnp.dot(deviation.T, centred, precision=HIGHEST)
    change = jnp.dot(gain_rows, cross, precision=HIGHEST) / (members - 1)
    updated = (flat + change).reshape(log_perm.shape)
    return (head_field, updated)
```

```python
import functools

import jax
import jax.numpy as jnp
from jax import lax
from jax.experimental import pallas as pl
from jax.experimental.pallas import tpu as pltpu
from jax.sharding import PartitionSpec as P

OMEGA = 0.8
HIGHEST = lax.Precision.HIGHEST
F32 = jnp.float32
MIB = 1 << 20
VMEM = pl.BlockSpec(memory_space=pltpu.VMEM)
SMEM = pl.BlockSpec(memory_space=pltpu.SMEM)
ANY = pl.BlockSpec(memory_space=pl.ANY)
REACH = 3
DEEP = 3
MICROSECOND = 3.0e6
EXPECTED = dict(planes=4, gather=5, sweep=13, local_heads=5, solve=5, mix=4, update=4)
SLOT = 8
SIDE = 2 * REACH + 1


def spot():
    slab = lax.axis_index("space")
    return lax.rem(slab, 2), lax.axis_index("ens"), slab


def recip(x):
    return pltpu.reciprocal(x, approx=True)


def call(kernel, name, out_shape, in_specs, out_specs, scratch=(), after=(), alias={}):
    tokens = len(after)

    def entry(*refs):
        kernel(*refs[tokens:])

    run = pl.pallas_call(
        entry,
        name=name,
        out_shape=out_shape,
        in_specs=[ANY] * tokens + list(in_specs),
        out_specs=out_specs,
        scratch_shapes=list(scratch),
        input_output_aliases={k + tokens: v for k, v in alias.items()},
        compiler_params=pltpu.CompilerParams(vmem_limit_bytes=64 * MIB),
        cost_estimate=pl.CostEstimate(
            flops=0, bytes_accessed=int(EXPECTED[name] * MICROSECOND), transcendentals=0
        ),
    )
    return functools.partial(run, *after)


def row_spans(depth, cut):
    return [(0, depth)] if cut is None else [(0, cut), (cut, depth)]


def planes_kernel(step, cut, lp, head, *refs):
    members, planes, depth, across = lp.shape
    spans = row_spans(depth, cut)
    parts = len(spans)
    sides = (refs[:parts], refs[parts : 2 * parts])
    own, raw, turned, perm, sem_in, sem_out = refs[2 * parts :]
    count = depth // step
    lines = depth // 8
    ins = []
    for b in range(count):
        rows = pl.ds(b * step, step)
        ins.append(
            pltpu.make_async_copy(lp.at[:, :, rows, :], raw.at[:, :, rows, :], sem_in.at[b])
        )
        ins[-1].start()
    odd, _, _ = spot()
    outs = []

    def send(src, dst):
        copy = pltpu.make_async_copy(src, dst, sem_out.at[len(outs)])
        copy.start()
        outs.append(copy)

    for i in range(planes):
        for k in range(lines):
            perm[i, depth + k] = head[i, pl.ds(8 * k, 8), :]
    plane = (1 - odd, odd)
    for s in range(2):
        send(
            perm.at[plane[s], pl.ds(depth, lines)],
            sides[s][0].at[pl.ds(spans[0][1], lines)],
        )
    sent = 0
    for b in range(count):
        ins[b].wait()

        def turn(k, carry):
            some = pl.ds(pl.multiple_of(b * step + 8 * k, 8), 8)
            for i in range(planes):
                x = jnp.swapaxes(raw[:, i, some, :], 0, 1)
                turned[i, some] = x
                perm[i, some] = jnp.exp(x)
            return carry

        lax.fori_loop(0, step // 8, turn, 0)
        rows = pl.ds(b * step, step)
        send(turned.at[:, rows], own.at[:, rows])
        while sent < parts and spans[sent][1] <= (b + 1) * step:
            lo, hi = spans[sent]
            for s in range(2):
                send(perm.at[plane[s], pl.ds(lo, hi - lo)], sides[s][sent].at[pl.ds(0, hi - lo)])
            sent += 1
    for copy in outs:
        copy.wait()


def planes_of(lp, head, cut, after=()):
    members, planes, depth, across = lp.shape
    step = 16
    lines = depth // 8
    spans = row_spans(depth, cut)
    sides = [
        jax.ShapeDtypeStruct((hi - lo + (lines if lo == 0 else 0), members, across), F32)
        for lo, hi in spans
    ]
    turned = (planes, depth, members, across)
    out = call(
        functools.partial(planes_kernel, step, cut),
        "planes",
        sides * 2 + [jax.ShapeDtypeStruct(turned, F32)],
        [ANY, VMEM],
        [ANY] * (2 * len(spans) + 1),
        [
            pltpu.VMEM(lp.shape, F32),
            pltpu.VMEM(turned, F32),
            pltpu.VMEM((planes, depth + lines, members, across), F32),
            pltpu.SemaphoreType.DMA((depth // step,)),
            pltpu.SemaphoreType.DMA((2 * len(spans) + depth // step + 2,)),
        ],
        after=after,
    )(lp, head)
    parts = len(spans)
    return out[:parts], out[parts : 2 * parts], out[2 * parts]


def sweep_kernel(cfg, *refs):
    first, last, za, zb, depth, members, across, pieces = cfg
    refs = list(refs)
    odd, _, _ = spot()
    lines = {"f": refs.pop(0)}
    if first:
        lines["s"] = refs.pop(0)
        lines["d"] = refs.pop(0)
    named = {}
    for key, spans in pieces:
        named[key] = [(refs.pop(0), lo, hi) for lo, hi in spans]
    if last:
        refs.pop(0)
        natural = refs.pop(0)
    else:
        outs = [refs.pop(0), refs.pop(0)]
        w_out = refs.pop(0) if first else None
    R, RP, H, HP, S, A, O, W, forcing = refs[:9]
    refs = refs[9:]
    dests = {"p": R, "h": H, "f": forcing}
    if first:
        DS, DA, HH, storage, head = refs[:5]
        refs = refs[5:]
        dests.update({"s": storage, "d": head})
    if last:
        NAT = refs.pop(0)
    sem_in, sem_out = refs
    zlo = max(za - 1, 0)
    zhi = min(zb, depth - 1)
    own = (1, 2)
    tiles = across // 128
    slots = {"a": 2 - odd, "b": 1 + odd, "ra": 3 - 3 * odd, "rb": 3 * odd}

    ends = []
    at = zlo
    for width in (4, 8, 12, 12, 12, 12, 12):
        if at >= zhi + 1:
            break
        ends.append(min(at + width, zhi + 1))
        at = ends[-1]
    if len(ends) > 1 and ends[-1] - ends[-2] < 4:
        ends.pop(-2)
    groups = []
    used = 0

    def copy_in(batch, src, dst):
        batch.append(pltpu.make_async_copy(src, dst, sem_in.at[len(batch) + used]))

    start = zlo
    for end in ends:
        batch = []
        for (kind, name), spans in named.items():
            low_row = za if kind == "w" else zlo
            high_row = zb if kind == "w" else zhi + 1
            for ref, lo, hi in spans:
                s, e = max(start, lo, low_row), min(end, hi, high_row)
                if s < e:
                    src, dst = pl.ds(s - lo, e - s), pl.ds(s - low_row, e - s)
                    if kind == "w":
                        copy_in(batch, ref.at[:, src], W.at[:, dst])
                    else:
                        copy_in(batch, ref.at[src], dests[kind].at[slots[name], dst])
        if start == zlo:
            for kind, ref in lines.items():
                copy_in(batch, ref, dests[kind])
            if first:
                for q, name in enumerate(("ra", "rb")):
                    ref, lo, hi = named["p", name][0]
                    some = pl.ds(hi - lo, depth // 8)
                    copy_in(batch, ref.at[some], HH.at[odd if q == 1 else 1 - odd])
        groups.append(batch)
        used += len(batch)
        start = end
    for batch in groups[:DEEP]:
        for copy in batch:
            copy.start()

    lane = lax.broadcasted_iota(jnp.int32, (members, 128), 1)
    final_lane = lane == 127
    first_lane = lane == 0

    def ahead(parts, beyond):
        turned = [pltpu.roll(x, 127, 1) for x in parts]
        out = [jnp.where(final_lane, turned[t + 1], turned[t]) for t in range(tiles - 1)]
        last_part = turned[-1]
        if beyond is not None:
            last_part = jnp.where(final_lane, beyond, last_part)
        return out + [last_part]

    def behind(parts):
        turned = [pltpu.roll(x, 1, 1) for x in parts]
        out = [jnp.where(first_lane, 0.0, turned[0])]
        return out + [jnp.where(first_lane, turned[t - 1], turned[t]) for t in range(1, tiles)]

    tile = [pl.ds(t * 128, 128) for t in range(tiles)]

    def load_row(z, chosen=range(4)):
        q = z - zlo
        for i in chosen:
            r = [recip(R[i, q, :, ys]) for ys in tile]
            rp = ahead(r, jnp.inf)
            for t, ys in enumerate(tile):
                R[i, q, :, ys] = r[t]
                RP[i, q, :, ys] = rp[t]
            if first:
                if i in own:
                    row = head[i - 1, pl.ds(z, 1), :]
                else:
                    row = HH[i // 3, z // 8, pl.ds(lax.rem(z, 8), 1), :]
                row = jnp.broadcast_to(row, (members, across))
                h = [row[:, t * 128 : (t + 1) * 128] for t in range(tiles)]
            else:
                h = [H[i, q, :, ys] for ys in tile]
            hp = ahead(h, None)
            for t, ys in enumerate(tile):
                if first:
                    H[i, q, :, ys] = h[t]
                HP[i, q, :, ys] = hp[t]

    def process(z, emit=True, inner=True, load=False):
        c = z - zlo
        both = (c, c + 1) if inner else (c,)
        done = {}
        for t, ys in enumerate(tile):

            def get(ref):
                return [[ref[i, q, :, ys] for q in both] for i in range(4)]

            r, rp, h, hp = get(R), get(RP), get(H), get(HP)
            total = {}
            for k, i in enumerate(own):
                total["s", i, 0] = S[k, :, ys]
                total["a", i, 0] = A[k, :, ys]
                if first:
                    total["ds", i, 0] = DS[k, :, ys]
                    total["da", i, 0] = DA[k, :, ys]

            def add(key, value):
                total[key] = total[key] + value if key in total else value

            def pair(scale, i, q, j, p, ahead):
                x = r[i][q] + (rp[j][p] if ahead else r[j][p])
                u = recip(x if scale == 1.0 else x * scale)
                if i in own:
                    add(("s", i, q), u * (hp[j][p] if ahead else h[j][p]))
                    if first:
                        add(("ds", i, q), u)
                if j in own:
                    add(("a" if ahead else "s", j, p), u * h[i][q])
                    if first:
                        add(("da" if ahead else "ds", j, p), u)

            w1, w2, w3 = 0.5, 1.0, 2.0
            sides = ((0, 1), (1, 2), (2, 3))
            for i in own:
                pair(w1, i, 0, i, 0, True)
            for i, j in sides:
                pair(w1, i, 0, j, 0, False)
                pair(w2, i, 0, j, 0, True)
                pair(w2, j, 0, i, 0, True)
            if inner:
                for i in own:
                    pair(w1, i, 0, i, 1, False)
                    pair(w2, i, 0, i, 1, True)
                    pair(w2, i, 1, i, 0, True)
                for i, j in sides:
                    pair(w2, i, 0, j, 1, False)
                    pair(w2, i, 1, j, 0, False)
                    pair(w3, i, 0, j, 1, True)
                    pair(w3, i, 1, j, 0, True)
                    pair(w3, j, 0, i, 1, True)
                    pair(w3, j, 1, i, 0, True)
                for k, i in enumerate(own):
                    S[k, :, ys] = total["s", i, 1]
                    A[k, :, ys] = total["a", i, 1]
                    if first:
                        DS[k, :, ys] = total["ds", i, 1]
                        DA[k, :, ys] = total["da", i, 1]
            for key, value in total.items():
                if key[2] == 0:
                    done.setdefault(key[:2], []).append(value)
            if load:
                load_row(z + 2, range(t * 4 // tiles, (t + 1) * 4 // tiles))
        if not emit:
            return
        o = z - za
        for k, i in enumerate(own):
            moved = behind(done["a", i])
            source = forcing[k, pl.ds(z, 1), :]
            if first:
                store = storage[k, pl.ds(z, 1), :]
            if first:
                da = behind(done["da", i])
            for t, ys in enumerate(tile):
                cut = slice(t * 128, (t + 1) * 128)
                gathered = done["s", i][t] + moved[t]
                if first:
                    diagonal = store[:, cut] + (done["ds", i][t] + da[t])
                    w = OMEGA * recip(diagonal)
                    W[k, o, :, ys] = w
                else:
                    w = W[k, o, :, ys]
                old = H[i, c, :, ys]
                O[k, o, :, ys] = (1.0 - OMEGA) * old + w * (source[:, cut] + gathered)

    results = []

    def start_out(src, dst):
        copy = pltpu.make_async_copy(src, dst, sem_out.at[len(results)])
        copy.start()
        results.append(copy)

    progress = [za]

    def flush(upto):
        if last:
            upto = upto // 8 * 8
        begin = progress[0]
        if upto <= begin:
            return
        progress[0] = upto
        rows = pl.ds(begin - za, upto - begin)
        if last:

            def turn(b, carry):
                some = pl.ds(pl.multiple_of(b * 8, 8), 8)
                for k in range(2):
                    NAT[:, k, some, :] = jnp.swapaxes(O[k, some], 0, 1)
                return carry

            lax.fori_loop((begin - za) // 8, (upto - za) // 8, turn, 0)
            start_out(
                NAT.at[:, :, rows, :], natural.at[:, :, pl.ds(begin, upto - begin), :]
            )
            return
        start_out(O.at[1 - odd, rows], outs[0].at[rows])
        start_out(O.at[odd, rows], outs[1].at[rows])
        if first:
            start_out(W.at[:, rows], w_out.at[:, rows])

    S[...] = jnp.zeros_like(S)
    A[...] = jnp.zeros_like(A)
    if first:
        DS[...] = jnp.zeros_like(DS)
        DA[...] = jnp.zeros_like(DA)
    at = zlo
    for g, end in enumerate(ends):
        for copy in groups[g]:
            copy.wait()
        if g + DEEP < len(groups):
            for copy in groups[g + DEEP]:
                copy.start()
        if g == 0:
            load_row(zlo)
            load_row(zlo + 1)
            if zlo < za:
                load_row(zlo + 2)
                process(zlo, emit=False)
                at = za

        def body(z, carry):
            process(z, load=True)
            return carry

        lax.fori_loop(at, end - 2, body, 0, unroll=2)
        at = end - 2
        flush(at)
    process(zhi - 1)
    if zb == depth:
        process(zhi, inner=False)
    flush(zb)
    for copy in results:
        copy.wait()


def sweep_of(first, last, za, zb, shape, lines, fields, into=None, after=()):
    members, planes, depth, across = shape
    zlo = max(za - 1, 0)
    zhi = min(zb, depth - 1)
    rows = zb - za
    pieces = tuple((key, tuple((lo, hi) for _, lo, hi in spans)) for key, spans in fields.items())
    operands = list(lines)
    for spans in fields.values():
        operands += [ref for ref, _, _ in spans]
    copies = sum(len(spans) for spans in fields.values()) * 7 + 8
    field = pltpu.VMEM((4, zhi + 1 - zlo, members, across), F32)
    line = pltpu.VMEM((2, members, across), F32)
    flat = pltpu.VMEM((2, depth, across), F32)
    both = pltpu.VMEM((2, rows, members, across), F32)
    scratch = [field] * 4 + [line] * 2 + [both] * 2 + [flat]
    if first:
        scratch += [line] * 2 + [pltpu.VMEM((2, depth // 8, 8, across), F32)] + [flat] * 2
    alias = {}
    if last:
        scratch += [pltpu.VMEM((members, 2, rows, across), F32)]
        out_shape = [jax.ShapeDtypeStruct(shape, F32)]
        operands.append(lines[0] if into is None else into)
        if into is not None:
            alias = {len(operands) - 1: 0}
    else:
        out_shape = [jax.ShapeDtypeStruct((rows, members, across), F32)] * 2
        if first:
            out_shape += [jax.ShapeDtypeStruct((2, rows, members, across), F32)]
    scratch += [pltpu.SemaphoreType.DMA((copies,)), pltpu.SemaphoreType.DMA((32,))]
    cfg = (first, last, za, zb, depth, members, across, pieces)
    cells = 2 * rows * members * across
    return call(
        functools.partial(sweep_kernel, cfg),
        "sweep",
        out_shape,
        [ANY] * len(operands),
        [ANY] * len(out_shape),
        scratch,
        alias=alias,
        after=after,
    )(*operands)


WAITS = {(1, 1): ("patches",), (2, 1): ("summed",)}
CUTS = (35, 34, 33, 32)
ORDER = (
    "planes",
    "gather",
    (1, 0),
    (1, 1),
    "local",
    (2, 0),
    (2, 1),
    "solve",
    (3, 0),
    (3, 1),
    "update",
)


def exact_pick(x, onehot):
    top = x.astype(jnp.bfloat16)
    rest = x - top.astype(F32)
    mid = rest.astype(jnp.bfloat16)
    low = (rest - mid.astype(F32)).astype(jnp.bfloat16)
    out = jnp.dot(low, onehot, preferred_element_type=F32)
    out = out + jnp.dot(mid, onehot, preferred_element_type=F32)
    return out + jnp.dot(top, onehot, preferred_element_type=F32)


def columns_of(cells, start, count, width, lanes, depth, across):
    lane = lax.broadcasted_iota(jnp.int32, (1, lanes), 1)
    at = lax.rem(lane, width)
    cell = jnp.zeros((1, lanes), jnp.int32)
    for o in range(count):
        cell = jnp.where((at >= o * SLOT) & (at < (o + 1) * SLOT), cells[start + o], cell)
    slot = lax.rem(lane, SLOT)
    y = lax.rem(cell, across) + slot - REACH
    y = jnp.where((slot < SIDE) & (at < count * SLOT), y, -1)
    line = lax.div(cell, across)
    return lax.div(line, depth), lax.rem(line, depth), y


def gather_kernel(spans, slabs, wells, rates, cells, head, storage, *refs):
    parts = len(spans)
    sides = (refs[:parts], refs[parts : 2 * parts])
    outs = refs[2 * parts : 2 * parts + slabs]
    forcing, field, picked, held_p, held_e, packed, sems, sem_out = refs[2 * parts + slabs :]
    out = held_p
    planes, depth, across = head.shape
    members, lanes = picked.shape[2:]
    odd, _, slab = spot()
    step = 16
    copies = {}
    for b in range(depth // step):
        for lo, hi in spans:
            s, e = max(lo, b * step), min(hi, (b + 1) * step)
            if s >= e:
                continue
            for side, plane in enumerate((1 - odd, odd)):
                ref = sides[side][spans.index((lo, hi))]
                batch = copies.setdefault(b, [])
                copy = pltpu.make_async_copy(
                    ref.at[pl.ds(s - lo, e - s)],
                    field.at[plane, pl.ds(s, e - s)],
                    sems.at[b, len(batch)],
                )
                copy.start()
                batch.append(copy)

    forcing[...] = storage[...] * head[...]
    lane = lax.broadcasted_iota(jnp.int32, (1, across), 1)

    def add_well(k, carry):
        cell = wells[k] - slab * (planes * depth * across)

        @pl.when((cell >= 0) & (cell < planes * depth * across))
        def _():
            line = lax.div(cell, across)
            x = lax.div(line, depth)
            z = lax.rem(line, depth)
            row = forcing[x, pl.ds(z, 1), :]
            here = lane == lax.rem(cell, across)
            forcing[x, pl.ds(z, 1), :] = row + jnp.where(here, rates[k], 0.0)

        return carry

    lax.fori_loop(0, wells.shape[0], add_well, 0)
    _, zcol, ycol = columns_of(cells, 0, lanes // SLOT, lanes, lanes, depth, across)
    across_ids = lax.broadcasted_iota(jnp.int32, (across, lanes), 0)
    onehot = jnp.where(across_ids == ycol, 1.0, 0.0).astype(jnp.bfloat16)
    held_p[...] = jnp.zeros_like(held_p)
    held_e[...] = jnp.zeros_like(held_e)
    depth_ids = lax.broadcasted_iota(jnp.int32, (depth, lanes), 0)
    for a, ref in enumerate((head, storage, forcing)):
        for i in range(planes):
            lines = exact_pick(ref[i], onehot)
            for d in range(SIDE):
                here = zcol + (d - REACH) == depth_ids
                line = jnp.sum(jnp.where(here, lines, 0.0), axis=0, keepdims=True)
                held_e[i, d, pl.ds(a, 1), :] = line
    for b in range(depth // step):
        for copy in copies[b]:
            copy.wait()
        some = pl.ds(step * b, step)
        for i in range(planes):
            rows = field[i, some].reshape(step * members, across)
            picked[i, some] = exact_pick(rows, onehot).reshape(step, members, lanes)

        def body(k, carry):
            for i in range(planes):
                held = [out[i, d, pl.ds(0, members), :] for d in range(SIDE)]
                for e in range(8):
                    z = b * step + k * 8 + e
                    value = picked[i, z]
                    for d in range(SIDE):
                        held[d] = jnp.where(zcol + (d - REACH) == z, value, held[d])
                for d in range(SIDE):
                    out[i, d, pl.ds(0, members), :] = held[d]
            return carry

        lax.fori_loop(0, step // 8, body, 0)

    width = lanes // slabs
    first = lax.broadcasted_iota(jnp.int32, (members, 128), 1) < 64
    for t in range(slabs):
        tile = pl.ds(width * t // 128 * 128, 128)
        shift = width * t % 128
        for i in range(planes):
            for d in range(SIDE):
                p = pltpu.roll(held_p[i, d, :, tile], (128 - shift) % 128, 1)
                e = pltpu.roll(held_e[i, d, :, tile], (192 - shift) % 128, 1)
                packed[t, i, d] = jnp.where(first, p, e)
    results = []
    for k in range(slabs):
        copy = pltpu.make_async_copy(packed.at[slab ^ k], outs[k], sem_out.at[k])
        copy.start()
        results.append(copy)
    for copy in results:
        copy.wait()


def gather_of(wells, rates, cells, head, storage, spans, slabs, side_a, side_b, after=()):
    planes, depth, across = head.shape
    members = side_a[0].shape[1]
    lanes = cells.shape[0] * SLOT
    held = (planes, SIDE, members, lanes)
    packed = (planes, SIDE, members, 128)
    return call(
        functools.partial(gather_kernel, spans, slabs),
        "gather",
        [jax.ShapeDtypeStruct(packed, F32)] * slabs + [jax.ShapeDtypeStruct(head.shape, F32)],
        [SMEM] * 3 + [VMEM] * 2 + [ANY] * (2 * len(spans)),
        [ANY] * slabs + [VMEM],
        [
            pltpu.VMEM((planes, depth, members, across), F32),
            pltpu.VMEM((planes, depth, members, lanes), F32),
            pltpu.VMEM(held, F32),
            pltpu.VMEM(held, F32),
            pltpu.VMEM((slabs,) + packed, F32),
            pltpu.SemaphoreType.DMA((depth // 16, 4)),
            pltpu.SemaphoreType.DMA((slabs,)),
        ],
        after=after,
    )(wells, rates, cells, head, storage, *side_a, *side_b)


def local_kernel(nz, ny, nobs, slabs, cells, perturb, *refs):
    blocks = refs[:slabs]
    out, R, RM, RP, H, HM, HP, ST, FO, W, NEW = refs[slabs:]
    members, lanes = R.shape[2:]
    _, _, slab = spot()
    share = nobs // slabs
    x0, zcol, ycol = columns_of(cells, slab * share, share, 64, lanes, nz, ny)

    def spread(ref, minus, plus, i, d, value):
        ref[i, d] = value
        minus[i, d] = pltpu.roll(value, 1, 1)
        plus[i, d] = pltpu.roll(value, lanes - 1, 1)

    def select(i, carry):
        x = x0 + (i - REACH)
        masks = [x == 2 * (slab ^ (g // 2)) + g % 2 for g in range(2 * slabs)]
        for d in range(SIDE):
            z = zcol + (d - REACH)
            inside = (x >= 0) & (x < 2 * slabs) & (z >= 0) & (z < nz)
            inside = inside & (ycol >= 0) & (ycol < ny)
            both = jnp.zeros((members, lanes), F32)
            for g in range(2 * slabs):
                both = jnp.where(masks[g], blocks[g // 2][g % 2, d], both)
            perm = both
            rest = pltpu.roll(both, 64, 1)
            r = jnp.where(inside, recip(perm), jnp.inf)
            spread(R, RM, RP, i, d, r)
            head = jnp.broadcast_to(jnp.where(inside, rest[0:1], 0.0), (members, lanes))
            spread(H, HM, HP, i, d, head)
            ST[i, d] = jnp.where(inside, rest[1:2], 1.0)
            FO[i, d] = jnp.where(inside, rest[2:3], 0.0)
        return carry

    lax.fori_loop(0, SIDE, select, 0)
    rs, hs = (RM, R, RP), (HM, H, HP)

    def update(i, d, first):
        mine = R[i, d]
        total = {}
        weight = {}
        for a in (-1, 0, 1):
            for b in (-1, 0, 1):
                for c in (-1, 0, 1):
                    n = abs(a) + abs(b) + abs(c)
                    if n == 0:
                        continue
                    u = recip(mine + rs[c + 1][i + a, d + b])
                    t = u * hs[c + 1][i + a, d + b]
                    total[n] = total[n] + t if n in total else t
                    if first:
                        weight[n] = weight[n] + u if n in weight else u
        gathered = 2.0 * total[1] + total[2] + 0.5 * total[3]
        if first:
            diagonal = ST[i, d] + (2.0 * weight[1] + weight[2] + 0.5 * weight[3])
            w = OMEGA * recip(diagonal)
            W[i, d] = w
        else:
            w = W[i, d]
        return (1.0 - OMEGA) * H[i, d] + w * (FO[i, d] + gathered)

    for sweep in range(1, REACH):
        width = SIDE - 2 * sweep

        def body(i, carry):
            for d in range(sweep, SIDE - sweep):
                NEW[i, d] = update(i, d, sweep == 1)
            return carry

        lax.fori_loop(sweep, SIDE - sweep, body, 0)
        for i in range(sweep, SIDE - sweep):
            for d in range(sweep, SIDE - sweep):
                spread(H, HM, HP, i, d, NEW[i, d])
    final = update(REACH, REACH, False)
    lane = lax.broadcasted_iota(jnp.int32, (lanes, 128), 0)
    target = lax.broadcasted_iota(jnp.int32, (lanes, 128), 1) - slab * share
    onehot = (lane == target * SLOT + REACH) & (target >= 0) & (target < share)
    observed = exact_pick(final, jnp.where(onehot, 1.0, 0.0).astype(jnp.bfloat16))
    rest = jnp.zeros((members, 128 - 2 * nobs), F32)
    part = perturb[...] * (1.0 / slabs)
    out[...] = jnp.concatenate([observed[:, :nobs], part, rest], 1)


def local_of(nz, ny, cells, perturb, blocks, after=()):
    nobs = cells.shape[0]
    lanes = 128
    members = perturb.shape[0]
    slabs = len(blocks)
    full = pltpu.VMEM((SIDE, SIDE, members, lanes), F32)
    line = pltpu.VMEM((SIDE, SIDE, 1, lanes), F32)
    return call(
        functools.partial(local_kernel, nz, ny, nobs, slabs),
        "local_heads",
        jax.ShapeDtypeStruct((members, 128), F32),
        [SMEM] + [VMEM] * (1 + slabs),
        VMEM,
        [full] * 6 + [line] * 2 + [full] * 2,
        after=after,
    )(cells, perturb, *blocks)


def solve_kernel(nobs, peers, values, noise, step, seen, out, aug):
    every = seen[...]
    total = every.shape[0]
    heads = every[:, :nobs]
    mean = jnp.sum(heads, axis=0, keepdims=True) * (1.0 / total)
    dev = heads - mean
    contract = (((0,), (0,)), ((), ()))
    cov = lax.dot_general(dev, dev, contract, precision=HIGHEST, preferred_element_type=F32)
    cov = cov * (1.0 / (total - 1))
    row = lax.broadcasted_iota(jnp.int32, (nobs, nobs), 0)
    col = lax.broadcasted_iota(jnp.int32, (nobs, nobs), 1)
    system = cov + jnp.where(row == col, noise[...] * (1.0 / step[0]), 0.0)
    identity = jnp.where(row == col, 1.0, 0.0)
    work = jnp.concatenate([system, identity], 1)
    line = lax.broadcasted_iota(jnp.int32, work.shape, 0)
    for k in range(nobs):
        pivot = work[k : k + 1, :] * (1.0 / work[k : k + 1, k : k + 1])
        work = jnp.where(line == k, pivot, work - work[:, k : k + 1] * pivot)
    aug[...] = work
    inverse = aug[:, pl.ds(nobs, nobs)]
    mine = every[: every.shape[0] // peers]
    residual = values[...] + mine[:, nobs : 2 * nobs] - mine[:, :nobs]
    gain = jnp.dot(residual, inverse, precision=HIGHEST, preferred_element_type=F32)
    nt = (((1,), (1,)), ((), ()))
    mixing = lax.dot_general(gain, dev, nt, precision=HIGHEST, preferred_element_type=F32)
    out[...] = mixing * (1.0 / (total - 1))


def solve_of(seen, peers, values, noise, step, after=()):
    nobs = values.shape[0]
    total = seen.shape[0]
    return call(
        functools.partial(solve_kernel, nobs, peers),
        "solve",
        jax.ShapeDtypeStruct((total // peers, total), F32),
        [VMEM, VMEM, SMEM, VMEM],
        VMEM,
        [pltpu.VMEM((nobs, 2 * nobs), F32)],
        after=after,
    )(values[None], noise[None], step, seen)


def update_kernel(step, mixing, lp, every, out, x, a, sem_lp, sem_in, sem_out):
    members, planes, depth, across = lp.shape
    peers = every.shape[0]
    _, me, _ = spot()
    blocks = [(b, i) for b in range(depth // step) for i in range(planes)]
    ahead = a.shape[0]
    ins, outs, fields = [], [], []
    for n, (b, i) in enumerate(blocks):
        rows = pl.ds(b * step, step)
        ins.append(
            pltpu.make_async_copy(every.at[:, i, rows], a.at[n % ahead], sem_in.at[n])
        )
        fields.append(
            pltpu.make_async_copy(lp.at[:, i, rows, :], x.at[:, i, rows, :], sem_lp.at[n])
        )
        outs.append(
            pltpu.make_async_copy(x.at[:, i, rows, :], out.at[:, i, rows, :], sem_out.at[n])
        )
    for n in range(ahead):
        ins[n].start()
        fields[n].start()
    m = mixing[...]
    m_top = m.astype(jnp.bfloat16)
    m_low = (m - m_top.astype(F32)).astype(jnp.bfloat16)
    left = jnp.concatenate([m_top, m_top], 1)
    right = jnp.concatenate([m_low, jnp.zeros_like(m_low)], 1)
    left = jnp.concatenate([left, right], 0)
    for n, (b, i) in enumerate(blocks):
        ins[n].wait()
        fields[n].wait()
        for g in range(step // 8):
            lines = []
            for z in range(8 * g, 8 * g + 8):
                f = jnp.concatenate([a[n % ahead, me ^ k, z] for k in range(peers)], 0)
                top = f.astype(jnp.bfloat16)
                low = (f - top.astype(F32)).astype(jnp.bfloat16)
                both = jnp.concatenate([top, low], 0)
                y = jnp.dot(left, both, preferred_element_type=F32)
                lines.append(y[:members] + y[members:])
            change = jnp.stack(lines, 0)
            some = pl.ds(b * step + 8 * g, 8)
            x[:, i, some, :] = x[:, i, some, :] + jnp.swapaxes(change, 0, 1)
        outs[n].start()
        if n + ahead < len(blocks):
            ins[n + ahead].start()
            fields[n + ahead].start()
    for copy in outs:
        copy.wait()


def update_of(mixing, lp, every, after=()):
    members, planes, depth, across = lp.shape
    peers = every.shape[0]
    step = 8
    ahead = 6
    count = planes * depth // step
    return call(
        functools.partial(update_kernel, step),
        "update",
        jax.ShapeDtypeStruct(lp.shape, F32),
        [VMEM, ANY, ANY],
        ANY,
        [
            pltpu.VMEM(lp.shape, F32),
            pltpu.VMEM((ahead, peers, step, members, across), F32),
            pltpu.SemaphoreType.DMA((count,)),
            pltpu.SemaphoreType.DMA((count,)),
            pltpu.SemaphoreType.DMA((count,)),
        ],
        after=after,
    )(mixing, lp, every)


def swap(x, axis, bit):
    return lax.ppermute(x, axis, [(i, i ^ bit) for i in range(lax.axis_size(axis))])


def swaps(parts, axis):
    return [parts[0]] + [swap(parts[k], axis, k) for k in range(1, lax.axis_size(axis))]


def gather_by_swaps(x, axis, token):
    x = lax.optimization_barrier((x, *token))[0]
    bit = 1
    while bit < lax.axis_size(axis):
        x = jnp.concatenate([x, swap(x, axis, bit)], 0)
        bit *= 2
    return x


def halo(x, side):
    pairs = [(i, i + 1) for i in range(side, lax.axis_size("space") - 1, 2)]
    return lax.ppermute(x, "space", pairs + [(b, a) for a, b in pairs])


def shards(
    log_perm,
    storage,
    head_init,
    well_cells,
    well_rates,
    obs_cells,
    obs_values,
    noise_var,
    step_size,
    perturb,
):
    shape = log_perm.shape
    members, planes, depth, across = shape
    slabs = lax.axis_size("space")
    peers = lax.axis_size("ens")
    spans = row_spans(depth, CUTS[0])
    names = ("a", "b", "ra", "rb")
    state = {"token": ()}

    def after(*refs):
        state["token"] = refs

    def span(parts, cut):
        return [(x, lo, hi) for x, (lo, hi) in zip(parts, row_spans(depth, cut))]

    def planes_step():
        side_a, side_b, own = planes_of(log_perm, head_init, CUTS[0])
        state["a"], state["b"], state["own"] = side_a, side_b, own
        far_a = [halo(x, 0) for x in side_a]
        far_b = [halo(x, 1) for x in side_b]
        state["far"] = [v for v in zip(far_a, far_b)]
        sides = (side_a, side_b, far_a, far_b)
        state["perms"] = {("p", n): span(v, CUTS[0]) for n, v in zip(names, sides)}
        state["new"] = {1: [], 2: []}
        state["every"] = lax.all_gather(own, "ens", axis=0)
        after(own)

    def gather_step():
        *patch, state["forcing"] = gather_of(
            well_cells,
            well_rates,
            obs_cells,
            head_init,
            storage,
            spans,
            slabs,
            state["a"],
            state["b"],
            after=state["token"],
        )
        state["patches"] = swaps(patch, "space")
        after(patch[0])

    def local_step():
        seen = local_of(
            depth, across, obs_cells, perturb, state["patches"], after=state["token"]
        )
        state["local"] = seen
        seen = sum(swaps([seen] * slabs, "space"))
        state["summed"] = [seen]
        after(state["local"])

    def solve_step():
        seen = gather_by_swaps(state["summed"][0], "ens", state["token"])
        state["mixing"] = solve_of(
            seen, peers, obs_values, noise_var, step_size, after=state["token"]
        )
        after(state["mixing"])

    def update_step():
        state["updated"] = update_of(
            state["mixing"], log_perm, state["every"], after=state["token"]
        )
        after(state["updated"])

    def sweep_step(sweep, part):
        first, last = sweep == 1, sweep == 3
        lo, hi = row_spans(depth, CUTS[sweep])[part]
        lines = [state["forcing"]] + ([storage, head_init] if first else [])
        fields = {k: v[: part + 1] if k[1][0] == "r" else v for k, v in state["perms"].items()}
        if not first:
            columns = list(zip(*state["new"][sweep - 1]))
            for k, n in enumerate(names):
                fields["h", n] = span(columns[k], CUTS[sweep - 1])
            weights = list(zip(*state["new"][1]))[4]
            fields["w", "w"] = span(weights, CUTS[1])
        token = () if "head" in state else state["token"]
        for key in WAITS.get((sweep, part), ()):
            token = token + tuple(state[key])
        out = sweep_of(first, last, lo, hi, shape, lines, fields, state.get("head"), after=token)
        if last:
            state["head"] = out[0]
        else:
            far = (halo(out[0], 0), halo(out[1], 1))
            state["new"][sweep].append((out[0], out[1]) + far + tuple(out[2:]))
        after(out[0])

    steps = dict(
        planes=planes_step,
        gather=gather_step,
        local=local_step,
        solve=solve_step,
        update=update_step,
    )
    for step in ORDER:
        if isinstance(step, tuple):
            sweep_step(*step)
        else:
            steps[step]()
    return (state["head"], state["updated"])


def solution(mesh):
    return jax.shard_map(
        shards,
        mesh=mesh,
        in_specs=(
            P("ens", "space", None, None),
            P("space", None, None),
            P("space", None, None),
            P(),
            P(),
            P(),
            P(),
            P(),
            P(),
            P("ens", None),
        ),
        out_specs=(P("ens", "space", None, None), P("ens", "space", None, None)),
        check_vma=False,
    )
```

```python
import functools

import jax
import jax.numpy as jnp
from jax import lax
from jax.experimental import pallas as pl
from jax.experimental.pallas import tpu as pltpu
from jax.sharding import PartitionSpec as P

OMEGA = 0.8
HIGHEST = lax.Precision.HIGHEST
F32 = jnp.float32
MIB = 1 << 20
VMEM = pl.BlockSpec(memory_space=pltpu.VMEM)
SMEM = pl.BlockSpec(memory_space=pltpu.SMEM)
ANY = pl.BlockSpec(memory_space=pl.ANY)
REACH = 3
DEEP = 3
MICROSECOND = 3.0e6
EXPECTED = dict(planes=4, gather=6, sweep=13, local_heads=5, solve=5, mix=4, update=4)
SLOT = 8
SIDE = 2 * REACH + 1


def spot():
    slab = lax.axis_index("space")
    return lax.rem(slab, 2), lax.axis_index("ens"), slab


def recip(x):
    return pltpu.reciprocal(x, approx=True)


def call(kernel, name, out_shape, in_specs, out_specs, scratch=(), after=(), alias={}):
    tokens = len(after)

    def entry(*refs):
        kernel(*refs[tokens:])

    run = pl.pallas_call(
        entry,
        name=name,
        out_shape=out_shape,
        in_specs=[ANY] * tokens + list(in_specs),
        out_specs=out_specs,
        scratch_shapes=list(scratch),
        input_output_aliases={k + tokens: v for k, v in alias.items()},
        compiler_params=pltpu.CompilerParams(vmem_limit_bytes=64 * MIB),
        cost_estimate=pl.CostEstimate(
            flops=0, bytes_accessed=int(EXPECTED[name] * MICROSECOND), transcendentals=0
        ),
    )
    return functools.partial(run, *after)


def row_spans(depth, cut):
    return [(0, depth)] if cut is None else [(0, cut), (cut, depth)]


def planes_kernel(step, cut, lp, head, *refs):
    members, planes, depth, across = lp.shape
    spans = row_spans(depth, cut)
    parts = len(spans)
    sides = (refs[:parts], refs[parts : 2 * parts])
    own, raw, turned, perm, sem_in, sem_out = refs[2 * parts :]
    count = depth // step
    lines = depth // 8
    ins = []
    for b in range(count):
        rows = pl.ds(b * step, step)
        ins.append(
            pltpu.make_async_copy(lp.at[:, :, rows, :], raw.at[:, :, rows, :], sem_in.at[b])
        )
        ins[-1].start()
    odd, _, _ = spot()
    outs = []

    def send(src, dst):
        copy = pltpu.make_async_copy(src, dst, sem_out.at[len(outs)])
        copy.start()
        outs.append(copy)

    for i in range(planes):
        for k in range(lines):
            perm[i, depth + k] = head[i, pl.ds(8 * k, 8), :]
    plane = (1 - odd, odd)
    for s in range(2):
        send(
            perm.at[plane[s], pl.ds(depth, lines)],
            sides[s][0].at[pl.ds(spans[0][1], lines)],
        )
    sent = 0
    for b in range(count):
        ins[b].wait()

        def turn(k, carry):
            some = pl.ds(pl.multiple_of(b * step + 8 * k, 8), 8)
            for i in range(planes):
                x = jnp.swapaxes(raw[:, i, some, :], 0, 1)
                turned[i, some] = x
                perm[i, some] = jnp.exp(x)
            return carry

        lax.fori_loop(0, step // 8, turn, 0)
        rows = pl.ds(b * step, step)
        send(turned.at[:, rows], own.at[:, rows])
        while sent < parts and spans[sent][1] <= (b + 1) * step:
            lo, hi = spans[sent]
            for s in range(2):
                send(perm.at[plane[s], pl.ds(lo, hi - lo)], sides[s][sent].at[pl.ds(0, hi - lo)])
            sent += 1
    for copy in outs:
        copy.wait()


def planes_of(lp, head, cut, after=()):
    members, planes, depth, across = lp.shape
    step = 16
    lines = depth // 8
    spans = row_spans(depth, cut)
    sides = [
        jax.ShapeDtypeStruct((hi - lo + (lines if lo == 0 else 0), members, across), F32)
        for lo, hi in spans
    ]
    turned = (planes, depth, members, across)
    out = call(
        functools.partial(planes_kernel, step, cut),
        "planes",
        sides * 2 + [jax.ShapeDtypeStruct(turned, F32)],
        [ANY, VMEM],
        [ANY] * (2 * len(spans) + 1),
        [
            pltpu.VMEM(lp.shape, F32),
            pltpu.VMEM(turned, F32),
            pltpu.VMEM((planes, depth + lines, members, across), F32),
            pltpu.SemaphoreType.DMA((depth // step,)),
            pltpu.SemaphoreType.DMA((2 * len(spans) + depth // step + 2,)),
        ],
        after=after,
    )(lp, head)
    parts = len(spans)
    return out[:parts], out[parts : 2 * parts], out[2 * parts]


def sweep_kernel(cfg, *refs):
    first, last, za, zb, depth, members, across, pieces = cfg
    refs = list(refs)
    odd, _, _ = spot()
    lines = {"f": refs.pop(0)}
    if first:
        lines["s"] = refs.pop(0)
        lines["d"] = refs.pop(0)
    named = {}
    for key, spans in pieces:
        named[key] = [(refs.pop(0), lo, hi) for lo, hi in spans]
    if last:
        refs.pop(0)
        natural = refs.pop(0)
    else:
        outs = [refs.pop(0), refs.pop(0)]
        w_out = refs.pop(0) if first else None
    R, RP, H, HP, S, A, O, W, forcing = refs[:9]
    refs = refs[9:]
    dests = {"p": R, "h": H, "f": forcing}
    if first:
        DS, DA, HH, storage, head = refs[:5]
        refs = refs[5:]
        dests.update({"s": storage, "d": head})
    if last:
        NAT = refs.pop(0)
    sem_in, sem_out = refs
    zlo = max(za - 1, 0)
    zhi = min(zb, depth - 1)
    own = (1, 2)
    tiles = across // 128
    slots = {"a": 2 - odd, "b": 1 + odd, "ra": 3 - 3 * odd, "rb": 3 * odd}

    ends = []
    at = zlo
    for width in (4, 8, 12, 12, 12, 12, 12):
        if at >= zhi + 1:
            break
        ends.append(min(at + width, zhi + 1))
        at = ends[-1]
    if len(ends) > 1 and ends[-1] - ends[-2] < 4:
        ends.pop(-2)
    groups = []
    used = 0

    def copy_in(batch, src, dst):
        batch.append(pltpu.make_async_copy(src, dst, sem_in.at[len(batch) + used]))

    start = zlo
    for end in ends:
        batch = []
        for (kind, name), spans in named.items():
            low_row = za if kind == "w" else zlo
            high_row = zb if kind == "w" else zhi + 1
            for ref, lo, hi in spans:
                s, e = max(start, lo, low_row), min(end, hi, high_row)
                if s < e:
                    src, dst = pl.ds(s - lo, e - s), pl.ds(s - low_row, e - s)
                    if kind == "w":
                        copy_in(batch, ref.at[:, src], W.at[:, dst])
                    else:
                        copy_in(batch, ref.at[src], dests[kind].at[slots[name], dst])
        if start == zlo:
            for kind, ref in lines.items():
                copy_in(batch, ref, dests[kind])
            if first:
                for q, name in enumerate(("ra", "rb")):
                    ref, lo, hi = named["p", name][0]
                    some = pl.ds(hi - lo, depth // 8)
                    copy_in(batch, ref.at[some], HH.at[odd if q == 1 else 1 - odd])
        groups.append(batch)
        used += len(batch)
        start = end
    for batch in groups[:DEEP]:
        for copy in batch:
            copy.start()

    lane = lax.broadcasted_iota(jnp.int32, (members, 128), 1)
    final_lane = lane == 127
    first_lane = lane == 0

    def ahead(parts, beyond):
        turned = [pltpu.roll(x, 127, 1) for x in parts]
        out = [jnp.where(final_lane, turned[t + 1], turned[t]) for t in range(tiles - 1)]
        last_part = turned[-1]
        if beyond is not None:
            last_part = jnp.where(final_lane, beyond, last_part)
        return out + [last_part]

    def behind(parts):
        turned = [pltpu.roll(x, 1, 1) for x in parts]
        out = [jnp.where(first_lane, 0.0, turned[0])]
        return out + [jnp.where(first_lane, turned[t - 1], turned[t]) for t in range(1, tiles)]

    tile = [pl.ds(t * 128, 128) for t in range(tiles)]

    def load_row(z, chosen=range(4)):
        q = z - zlo
        for i in chosen:
            r = [recip(R[i, q, :, ys]) for ys in tile]
            rp = ahead(r, jnp.inf)
            for t, ys in enumerate(tile):
                R[i, q, :, ys] = r[t]
                RP[i, q, :, ys] = rp[t]
            if first:
                if i in own:
                    row = head[i - 1, pl.ds(z, 1), :]
                else:
                    row = HH[i // 3, z // 8, pl.ds(lax.rem(z, 8), 1), :]
                row = jnp.broadcast_to(row, (members, across))
                h = [row[:, t * 128 : (t + 1) * 128] for t in range(tiles)]
            else:
                h = [H[i, q, :, ys] for ys in tile]
            hp = ahead(h, None)
            for t, ys in enumerate(tile):
                if first:
                    H[i, q, :, ys] = h[t]
                HP[i, q, :, ys] = hp[t]

    def process(z, emit=True, inner=True, load=False):
        c = z - zlo
        both = (c, c + 1) if inner else (c,)
        done = {}
        for t, ys in enumerate(tile):

            def get(ref):
                return [[ref[i, q, :, ys] for q in both] for i in range(4)]

            r, rp, h, hp = get(R), get(RP), get(H), get(HP)
            total = {}
            for k, i in enumerate(own):
                total["s", i, 0] = S[k, :, ys]
                total["a", i, 0] = A[k, :, ys]
                if first:
                    total["ds", i, 0] = DS[k, :, ys]
                    total["da", i, 0] = DA[k, :, ys]

            def add(key, value):
                total[key] = total[key] + value if key in total else value

            def pair(scale, i, q, j, p, ahead):
                x = r[i][q] + (rp[j][p] if ahead else r[j][p])
                u = recip(x if scale == 1.0 else x * scale)
                if i in own:
                    add(("s", i, q), u * (hp[j][p] if ahead else h[j][p]))
                    if first:
                        add(("ds", i, q), u)
                if j in own:
                    add(("a" if ahead else "s", j, p), u * h[i][q])
                    if first:
                        add(("da" if ahead else "ds", j, p), u)

            w1, w2, w3 = 0.5, 1.0, 2.0
            sides = ((0, 1), (1, 2), (2, 3))
            for i in own:
                pair(w1, i, 0, i, 0, True)
            for i, j in sides:
                pair(w1, i, 0, j, 0, False)
                pair(w2, i, 0, j, 0, True)
                pair(w2, j, 0, i, 0, True)
            if inner:
                for i in own:
                    pair(w1, i, 0, i, 1, False)
                    pair(w2, i, 0, i, 1, True)
                    pair(w2, i, 1, i, 0, True)
                for i, j in sides:
                    pair(w2, i, 0, j, 1, False)
                    pair(w2, i, 1, j, 0, False)
                    pair(w3, i, 0, j, 1, True)
                    pair(w3, i, 1, j, 0, True)
                    pair(w3, j, 0, i, 1, True)
                    pair(w3, j, 1, i, 0, True)
                for k, i in enumerate(own):
                    S[k, :, ys] = total["s", i, 1]
                    A[k, :, ys] = total["a", i, 1]
                    if first:
                        DS[k, :, ys] = total["ds", i, 1]
                        DA[k, :, ys] = total["da", i, 1]
            for key, value in total.items():
                if key[2] == 0:
                    done.setdefault(key[:2], []).append(value)
            if load:
                load_row(z + 2, range(t * 4 // tiles, (t + 1) * 4 // tiles))
        if not emit:
            return
        o = z - za
        for k, i in enumerate(own):
            moved = behind(done["a", i])
            source = forcing[k, pl.ds(z, 1), :]
            if first:
                store = storage[k, pl.ds(z, 1), :]
            if first:
                da = behind(done["da", i])
            for t, ys in enumerate(tile):
                cut = slice(t * 128, (t + 1) * 128)
                gathered = done["s", i][t] + moved[t]
                if first:
                    diagonal = store[:, cut] + (done["ds", i][t] + da[t])
                    w = OMEGA * recip(diagonal)
                    W[k, o, :, ys] = w
                else:
                    w = W[k, o, :, ys]
                old = H[i, c, :, ys]
                O[k, o, :, ys] = (1.0 - OMEGA) * old + w * (source[:, cut] + gathered)

    results = []

    def start_out(src, dst):
        copy = pltpu.make_async_copy(src, dst, sem_out.at[len(results)])
        copy.start()
        results.append(copy)

    progress = [za]

    def flush(upto):
        if last:
            upto = upto // 8 * 8
        begin = progress[0]
        if upto <= begin:
            return
        progress[0] = upto
        rows = pl.ds(begin - za, upto - begin)
        if last:

            def turn(b, carry):
                some = pl.ds(pl.multiple_of(b * 8, 8), 8)
                for k in range(2):
                    NAT[:, k, some, :] = jnp.swapaxes(O[k, some], 0, 1)
                return carry

            lax.fori_loop((begin - za) // 8, (upto - za) // 8, turn, 0)
            start_out(
                NAT.at[:, :, rows, :], natural.at[:, :, pl.ds(begin, upto - begin), :]
            )
            return
        start_out(O.at[1 - odd, rows], outs[0].at[rows])
        start_out(O.at[odd, rows], outs[1].at[rows])
        if first:
            start_out(W.at[:, rows], w_out.at[:, rows])

    S[...] = jnp.zeros_like(S)
    A[...] = jnp.zeros_like(A)
    if first:
        DS[...] = jnp.zeros_like(DS)
        DA[...] = jnp.zeros_like(DA)
    at = zlo
    for g, end in enumerate(ends):
        for copy in groups[g]:
            copy.wait()
        if g + DEEP < len(groups):
            for copy in groups[g + DEEP]:
                copy.start()
        if g == 0:
            load_row(zlo)
            load_row(zlo + 1)
            if zlo < za:
                load_row(zlo + 2)
                process(zlo, emit=False)
                at = za

        def body(z, carry):
            process(z, load=True)
            return carry

        lax.fori_loop(at, end - 2, body, 0, unroll=2)
        at = end - 2
        flush(at)
    process(zhi - 1)
    if zb == depth:
        process(zhi, inner=False)
    flush(zb)
    for copy in results:
        copy.wait()


def sweep_of(first, last, za, zb, shape, lines, fields, into=None, after=()):
    members, planes, depth, across = shape
    zlo = max(za - 1, 0)
    zhi = min(zb, depth - 1)
    rows = zb - za
    pieces = tuple((key, tuple((lo, hi) for _, lo, hi in spans)) for key, spans in fields.items())
    operands = list(lines)
    for spans in fields.values():
        operands += [ref for ref, _, _ in spans]
    copies = sum(len(spans) for spans in fields.values()) * 7 + 8
    field = pltpu.VMEM((4, zhi + 1 - zlo, members, across), F32)
    line = pltpu.VMEM((2, members, across), F32)
    flat = pltpu.VMEM((2, depth, across), F32)
    both = pltpu.VMEM((2, rows, members, across), F32)
    scratch = [field] * 4 + [line] * 2 + [both] * 2 + [flat]
    if first:
        scratch += [line] * 2 + [pltpu.VMEM((2, depth // 8, 8, across), F32)] + [flat] * 2
    alias = {}
    if last:
        scratch += [pltpu.VMEM((members, 2, rows, across), F32)]
        out_shape = [jax.ShapeDtypeStruct(shape, F32)]
        operands.append(lines[0] if into is None else into)
        if into is not None:
            alias = {len(operands) - 1: 0}
    else:
        out_shape = [jax.ShapeDtypeStruct((rows, members, across), F32)] * 2
        if first:
            out_shape += [jax.ShapeDtypeStruct((2, rows, members, across), F32)]
    scratch += [pltpu.SemaphoreType.DMA((copies,)), pltpu.SemaphoreType.DMA((32,))]
    cfg = (first, last, za, zb, depth, members, across, pieces)
    cells = 2 * rows * members * across
    return call(
        functools.partial(sweep_kernel, cfg),
        "sweep",
        out_shape,
        [ANY] * len(operands),
        [ANY] * len(out_shape),
        scratch,
        alias=alias,
        after=after,
    )(*operands)


WAITS = {(1, 0): ("patches",), (2, 0): ("partial",)}
CUTS = (None, None, None, None)
ORDER = (
    "planes",
    "gather",
    (1, 0),
    "local",
    (2, 0),
    "solve",
    "update",
    (3, 0),
)


def exact_pick(x, onehot):
    top = x.astype(jnp.bfloat16)
    rest = x - top.astype(F32)
    mid = rest.astype(jnp.bfloat16)
    low = (rest - mid.astype(F32)).astype(jnp.bfloat16)
    out = jnp.dot(low, onehot, preferred_element_type=F32)
    out = out + jnp.dot(mid, onehot, preferred_element_type=F32)
    return out + jnp.dot(top, onehot, preferred_element_type=F32)


def columns_of(cells, start, count, width, lanes, depth, across):
    lane = lax.broadcasted_iota(jnp.int32, (1, lanes), 1)
    at = lax.rem(lane, width)
    cell = jnp.zeros((1, lanes), jnp.int32)
    for o in range(count):
        cell = jnp.where((at >= o * SLOT) & (at < (o + 1) * SLOT), cells[start + o], cell)
    slot = lax.rem(lane, SLOT)
    y = lax.rem(cell, across) + slot - REACH
    y = jnp.where((slot < SIDE) & (at < count * SLOT), y, -1)
    line = lax.div(cell, across)
    return lax.div(line, depth), lax.rem(line, depth), y


def gather_kernel(slabs, wells, rates, cells, head, storage, own, *refs):
    outs = refs[:slabs]
    forcing, field, picked, held_p, held_e, packed, sems, sem_out = refs[slabs:]
    out = held_p
    planes, depth, across = head.shape
    members, lanes = picked.shape[2:]
    _, _, slab = spot()
    step = 16
    copies = []
    for b in range(depth // step):
        rows = pl.ds(b * step, step)
        copy = pltpu.make_async_copy(own.at[:, rows], field.at[:, rows], sems.at[b])
        copy.start()
        copies.append(copy)

    forcing[...] = storage[...] * head[...]
    lane = lax.broadcasted_iota(jnp.int32, (1, across), 1)

    def add_well(k, carry):
        cell = wells[k] - slab * (planes * depth * across)

        @pl.when((cell >= 0) & (cell < planes * depth * across))
        def _():
            line = lax.div(cell, across)
            x = lax.div(line, depth)
            z = lax.rem(line, depth)
            row = forcing[x, pl.ds(z, 1), :]
            here = lane == lax.rem(cell, across)
            forcing[x, pl.ds(z, 1), :] = row + jnp.where(here, rates[k], 0.0)

        return carry

    lax.fori_loop(0, wells.shape[0], add_well, 0)
    _, zcol, ycol = columns_of(cells, 0, lanes // SLOT, lanes, lanes, depth, across)
    across_ids = lax.broadcasted_iota(jnp.int32, (across, lanes), 0)
    onehot = jnp.where(across_ids == ycol, 1.0, 0.0).astype(jnp.bfloat16)
    held_p[...] = jnp.zeros_like(held_p)
    held_e[...] = jnp.zeros_like(held_e)
    depth_ids = lax.broadcasted_iota(jnp.int32, (depth, lanes), 0)
    for a, ref in enumerate((head, storage, forcing)):
        for i in range(planes):
            lines = exact_pick(ref[i], onehot)
            for d in range(SIDE):
                here = zcol + (d - REACH) == depth_ids
                line = jnp.sum(jnp.where(here, lines, 0.0), axis=0, keepdims=True)
                held_e[i, d, pl.ds(a, 1), :] = line
    results = []
    for b in range(depth // step):
        copies[b].wait()
        some = pl.ds(step * b, step)
        for i in range(planes):
            rows = field[i, some].reshape(step * members, across)
            picked[i, some] = exact_pick(rows, onehot).reshape(step, members, lanes)

        def body(k, carry):
            for i in range(planes):
                held = [out[i, d, pl.ds(0, members), :] for d in range(SIDE)]
                for e in range(8):
                    z = b * step + k * 8 + e
                    value = picked[i, z]
                    for d in range(SIDE):
                        held[d] = jnp.where(zcol + (d - REACH) == z, value, held[d])
                for d in range(SIDE):
                    out[i, d, pl.ds(0, members), :] = held[d]
            return carry

        lax.fori_loop(0, step // 8, body, 0)

    width = lanes // slabs
    first = lax.broadcasted_iota(jnp.int32, (members, 128), 1) < 64
    for t in range(slabs):
        tile = pl.ds(width * t // 128 * 128, 128)
        shift = width * t % 128
        for i in range(planes):
            for d in range(SIDE):
                p = pltpu.roll(held_p[i, d, :, tile], (128 - shift) % 128, 1)
                e = pltpu.roll(held_e[i, d, :, tile], (192 - shift) % 128, 1)
                packed[t, i, d] = jnp.where(first, p, e)
    for k in range(slabs):
        copy = pltpu.make_async_copy(packed.at[slab ^ k], outs[k], sem_out.at[k])
        copy.start()
        results.append(copy)
    for copy in results:
        copy.wait()


def gather_of(wells, rates, cells, head, storage, own, slabs, after=()):
    planes, depth, members, across = own.shape
    lanes = cells.shape[0] * SLOT
    held = (planes, SIDE, members, lanes)
    packed = (planes, SIDE, members, 128)
    return call(
        functools.partial(gather_kernel, slabs),
        "gather",
        [jax.ShapeDtypeStruct(packed, F32)] * slabs
        + [jax.ShapeDtypeStruct(head.shape, F32)],
        [SMEM] * 3 + [VMEM] * 2 + [ANY],
        [ANY] * slabs + [VMEM],
        [
            pltpu.VMEM(own.shape, F32),
            pltpu.VMEM((planes, depth, members, lanes), F32),
            pltpu.VMEM(held, F32),
            pltpu.VMEM(held, F32),
            pltpu.VMEM((slabs,) + packed, F32),
            pltpu.SemaphoreType.DMA((depth // 16,)),
            pltpu.SemaphoreType.DMA((slabs,)),
        ],
        after=after,
    )(wells, rates, cells, head, storage, own)


def local_kernel(nz, ny, nobs, slabs, peers, cells, *refs):
    blocks = refs[:slabs]
    out, R, RM, RP, H, HM, HP, ST, FO, W, NEW = refs[slabs:]
    members, lanes = R.shape[2:]
    _, block, slab = spot()
    share = nobs // slabs
    x0, zcol, ycol = columns_of(cells, slab * share, share, 64, lanes, nz, ny)

    def spread(ref, minus, plus, i, d, value):
        ref[i, d] = value
        minus[i, d] = pltpu.roll(value, 1, 1)
        plus[i, d] = pltpu.roll(value, lanes - 1, 1)

    def select(i, carry):
        x = x0 + (i - REACH)
        masks = [x == 2 * (slab ^ (g // 2)) + g % 2 for g in range(2 * slabs)]
        for d in range(SIDE):
            z = zcol + (d - REACH)
            inside = (x >= 0) & (x < 2 * slabs) & (z >= 0) & (z < nz)
            inside = inside & (ycol >= 0) & (ycol < ny)
            both = jnp.zeros((members, lanes), F32)
            for g in range(2 * slabs):
                both = jnp.where(masks[g], blocks[g // 2][g % 2, d], both)
            perm = both
            rest = pltpu.roll(both, 64, 1)
            r = jnp.where(inside, jnp.exp(-perm), jnp.inf)
            spread(R, RM, RP, i, d, r)
            head = jnp.broadcast_to(jnp.where(inside, rest[0:1], 0.0), (members, lanes))
            spread(H, HM, HP, i, d, head)
            ST[i, d] = jnp.where(inside, rest[1:2], 1.0)
            FO[i, d] = jnp.where(inside, rest[2:3], 0.0)
        return carry

    lax.fori_loop(0, SIDE, select, 0)
    rs, hs = (RM, R, RP), (HM, H, HP)

    def update(i, d, first):
        mine = R[i, d]
        total = {}
        weight = {}
        for a in (-1, 0, 1):
            for b in (-1, 0, 1):
                for c in (-1, 0, 1):
                    n = abs(a) + abs(b) + abs(c)
                    if n == 0:
                        continue
                    u = recip(mine + rs[c + 1][i + a, d + b])
                    t = u * hs[c + 1][i + a, d + b]
                    total[n] = total[n] + t if n in total else t
                    if first:
                        weight[n] = weight[n] + u if n in weight else u
        gathered = 2.0 * total[1] + total[2] + 0.5 * total[3]
        if first:
            diagonal = ST[i, d] + (2.0 * weight[1] + weight[2] + 0.5 * weight[3])
            w = OMEGA * recip(diagonal)
            W[i, d] = w
        else:
            w = W[i, d]
        return (1.0 - OMEGA) * H[i, d] + w * (FO[i, d] + gathered)

    for sweep in range(1, REACH):
        width = SIDE - 2 * sweep

        def body(i, carry):
            for d in range(sweep, SIDE - sweep):
                NEW[i, d] = update(i, d, sweep == 1)
            return carry

        lax.fori_loop(sweep, SIDE - sweep, body, 0)
        for i in range(sweep, SIDE - sweep):
            for d in range(sweep, SIDE - sweep):
                spread(H, HM, HP, i, d, NEW[i, d])
    final = update(REACH, REACH, False)
    lane = lax.broadcasted_iota(jnp.int32, (lanes, 128), 0)
    target = lax.broadcasted_iota(jnp.int32, (lanes, 128), 1) - block * (128 // peers)
    onehot = (lane == target * SLOT + REACH) & (target >= 0) & (target < share)
    out[...] = exact_pick(final, jnp.where(onehot, 1.0, 0.0).astype(jnp.bfloat16))


def local_of(nz, ny, cells, peers, blocks, after=()):
    nobs = cells.shape[0]
    lanes = 128
    members = blocks[0].shape[2]
    slabs = len(blocks)
    full = pltpu.VMEM((SIDE, SIDE, members, lanes), F32)
    line = pltpu.VMEM((SIDE, SIDE, 1, lanes), F32)
    return call(
        functools.partial(local_kernel, nz, ny, nobs, slabs, peers),
        "local_heads",
        jax.ShapeDtypeStruct((members, 128), F32),
        [SMEM] + [VMEM] * slabs,
        VMEM,
        [full] * 6 + [line] * 2 + [full] * 2,
        after=after,
    )(cells, *blocks)


def solve_kernel(nobs, peers, values, noise, step, perturb, *refs):
    *seen, out, aug = refs
    _, block, slab = spot()
    members = perturb.shape[0]
    total = peers * members
    width = 128 // peers
    share = nobs // len(seen)
    row = lax.broadcasted_iota(jnp.int32, (total, 128), 0)
    lane = lax.broadcasted_iota(jnp.int32, (total, 128), 1)
    mine = lax.div(row, members) == lax.div(lane, width)
    source = lax.broadcasted_iota(jnp.int32, (128, nobs), 0)
    target = lax.broadcasted_iota(jnp.int32, (128, nobs), 1)
    spot_of = lax.rem(source, width)
    heads = jnp.zeros((total, nobs), F32)
    for k, ref in enumerate(seen):
        line = jnp.where(mine, jnp.concatenate([ref[...]] * peers, 0), 0.0)
        onehot = (spot_of < share) & (target == (slab ^ k) * share + spot_of)
        heads = heads + exact_pick(line, jnp.where(onehot, 1.0, 0.0).astype(jnp.bfloat16))
    aug[pl.ds(0, total), pl.ds(0, nobs)] = heads
    mean = jnp.sum(heads, axis=0, keepdims=True) * (1.0 / total)
    dev = heads - mean
    contract = (((0,), (0,)), ((), ()))
    cov = lax.dot_general(dev, dev, contract, precision=HIGHEST, preferred_element_type=F32)
    cov = cov * (1.0 / (total - 1))
    row = lax.broadcasted_iota(jnp.int32, (nobs, nobs), 0)
    col = lax.broadcasted_iota(jnp.int32, (nobs, nobs), 1)
    system = cov + jnp.where(row == col, noise[...] * (1.0 / step[0]), 0.0)
    identity = jnp.where(row == col, 1.0, 0.0)
    work = jnp.concatenate([system, identity], 1)
    line = lax.broadcasted_iota(jnp.int32, work.shape, 0)
    for k in range(nobs):
        pivot = work[k : k + 1, :] * (1.0 / work[k : k + 1, k : k + 1])
        work = jnp.where(line == k, pivot, work - work[:, k : k + 1] * pivot)
    own = aug[pl.ds(pl.multiple_of(block * members, members), members), pl.ds(0, nobs)]
    inverse = work[:, nobs:]
    residual = values[...] + perturb[...] - own
    gain = jnp.dot(residual, inverse, precision=HIGHEST, preferred_element_type=F32)
    nt = (((1,), (1,)), ((), ()))
    mixing = lax.dot_general(gain, dev, nt, precision=HIGHEST, preferred_element_type=F32)
    out[...] = mixing * (1.0 / (total - 1))


def solve_of(seen, peers, values, noise, step, perturb, after=()):
    nobs = values.shape[0]
    members = perturb.shape[0]
    total = members * peers
    return call(
        functools.partial(solve_kernel, nobs, peers),
        "solve",
        jax.ShapeDtypeStruct((members, total), F32),
        [VMEM, VMEM, SMEM] + [VMEM] * (1 + len(seen)),
        VMEM,
        [pltpu.VMEM((total, 128), F32)],
        after=after,
    )(values[None], noise[None], step, perturb, *seen)


def update_kernel(step, mixing, lp, every, out, x, a, sem_lp, sem_in, sem_out):
    members, planes, depth, across = lp.shape
    peers = every.shape[0]
    blocks = [(b, i) for b in range(depth // step) for i in range(planes)]
    ahead = a.shape[0]
    ins, outs, fields = [], [], []
    for n, (b, i) in enumerate(blocks):
        rows = pl.ds(b * step, step)
        ins.append(
            pltpu.make_async_copy(every.at[:, i, rows], a.at[n % ahead], sem_in.at[n])
        )
        fields.append(
            pltpu.make_async_copy(lp.at[:, i, rows, :], x.at[:, i, rows, :], sem_lp.at[n])
        )
        outs.append(
            pltpu.make_async_copy(x.at[:, i, rows, :], out.at[:, i, rows, :], sem_out.at[n])
        )
    for n in range(ahead):
        ins[n].start()
        fields[n].start()
    m = mixing[...]
    m_top = m.astype(jnp.bfloat16)
    m_low = (m - m_top.astype(F32)).astype(jnp.bfloat16)
    left = jnp.concatenate([m_top, m_top], 1)
    right = jnp.concatenate([m_low, jnp.zeros_like(m_low)], 1)
    left = jnp.concatenate([left, right], 0)
    for n, (b, i) in enumerate(blocks):
        ins[n].wait()
        fields[n].wait()
        for g in range(step // 8):
            lines = []
            for z in range(8 * g, 8 * g + 8):
                f = jnp.concatenate([a[n % ahead, k, z] for k in range(peers)], 0)
                top = f.astype(jnp.bfloat16)
                low = (f - top.astype(F32)).astype(jnp.bfloat16)
                both = jnp.concatenate([top, low], 0)
                y = jnp.dot(left, both, preferred_element_type=F32)
                lines.append(y[:members] + y[members:])
            change = jnp.stack(lines, 0)
            some = pl.ds(b * step + 8 * g, 8)
            x[:, i, some, :] = x[:, i, some, :] + jnp.swapaxes(change, 0, 1)
        outs[n].start()
        if n + ahead < len(blocks):
            ins[n + ahead].start()
            fields[n + ahead].start()
    for copy in outs:
        copy.wait()


def update_of(mixing, lp, every, after=()):
    members, planes, depth, across = lp.shape
    peers = every.shape[0]
    step = 8
    ahead = 6
    count = planes * depth // step
    return call(
        functools.partial(update_kernel, step),
        "update",
        jax.ShapeDtypeStruct(lp.shape, F32),
        [VMEM, ANY, ANY],
        ANY,
        [
            pltpu.VMEM(lp.shape, F32),
            pltpu.VMEM((ahead, peers, step, members, across), F32),
            pltpu.SemaphoreType.DMA((count,)),
            pltpu.SemaphoreType.DMA((count,)),
            pltpu.SemaphoreType.DMA((count,)),
        ],
        after=after,
    )(mixing, lp, every)


def swap(x, axis, bit):
    return lax.ppermute(x, axis, [(i, i ^ bit) for i in range(lax.axis_size(axis))])


def swaps(parts, axis):
    return [parts[0]] + [swap(parts[k], axis, k) for k in range(1, lax.axis_size(axis))]


def halo(x, side):
    pairs = [(i, i + 1) for i in range(side, lax.axis_size("space") - 1, 2)]
    return lax.ppermute(x, "space", pairs + [(b, a) for a, b in pairs])


def shards(
    log_perm,
    storage,
    head_init,
    well_cells,
    well_rates,
    obs_cells,
    obs_values,
    noise_var,
    step_size,
    perturb,
):
    shape = log_perm.shape
    members, planes, depth, across = shape
    slabs = lax.axis_size("space")
    peers = lax.axis_size("ens")
    names = ("a", "b", "ra", "rb")
    state = {"token": ()}

    def after(*refs):
        state["token"] = refs

    def span(parts, cut):
        return [(x, lo, hi) for x, (lo, hi) in zip(parts, row_spans(depth, cut))]

    def planes_step():
        side_a, side_b, own = planes_of(log_perm, head_init, CUTS[0])
        far_a = [halo(x, 0) for x in side_a]
        far_b = [halo(x, 1) for x in side_b]
        sides = (side_a, side_b, far_a, far_b)
        state["perms"] = {("p", n): span(v, CUTS[0]) for n, v in zip(names, sides)}
        state["new"] = {1: [], 2: []}
        state["own"] = own
        state["every"] = lax.all_gather(own, "ens", axis=0)

    def gather_step():
        *patch, state["forcing"] = gather_of(
            well_cells, well_rates, obs_cells, head_init, storage, state["own"], slabs
        )
        state["patches"] = swaps(patch, "space")
        after(patch[0])

    def local_step():
        seen = local_of(
            depth, across, obs_cells, peers, state["patches"], after=state["token"]
        )
        after(seen)
        bit = 1
        while bit < peers:
            seen = seen + swap(seen, "ens", bit)
            bit *= 2
        state["partial"] = swaps([seen] * slabs, "space")

    def solve_step():
        state["mixing"] = solve_of(
            state["partial"], peers, obs_values, noise_var, step_size, perturb, after=state["token"]
        )
        after(state["mixing"])

    def update_step():
        state["updated"] = update_of(
            state["mixing"], log_perm, state["every"], after=state["token"]
        )
        after(state["updated"])

    def sweep_step(sweep, part):
        first, last = sweep == 1, sweep == 3
        lo, hi = row_spans(depth, CUTS[sweep])[part]
        lines = [state["forcing"]] + ([storage, head_init] if first else [])
        fields = {k: v[: part + 1] if k[1][0] == "r" else v for k, v in state["perms"].items()}
        if not first:
            columns = list(zip(*state["new"][sweep - 1]))
            for k, n in enumerate(names):
                fields["h", n] = span(columns[k], CUTS[sweep - 1])
            weights = list(zip(*state["new"][1]))[4]
            fields["w", "w"] = span(weights, CUTS[1])
        token = () if "head" in state else state["token"]
        for key in WAITS.get((sweep, part), ()):
            token = token + tuple(state[key])
        out = sweep_of(first, last, lo, hi, shape, lines, fields, state.get("head"), after=token)
        if last:
            state["head"] = out[0]
        else:
            far = (halo(out[0], 0), halo(out[1], 1))
            state["new"][sweep].append((out[0], out[1]) + far + tuple(out[2:]))
        after(out[0])

    steps = dict(
        planes=planes_step,
        gather=gather_step,
        local=local_step,
        solve=solve_step,
        update=update_step,
    )
    for step in ORDER:
        if isinstance(step, tuple):
            sweep_step(*step)
        else:
            steps[step]()
    return (state["head"], state["updated"])


def solution(mesh):
    return jax.shard_map(
        shards,
        mesh=mesh,
        in_specs=(
            P("ens", "space", None, None),
            P("space", None, None),
            P("space", None, None),
            P(),
            P(),
            P(),
            P(),
            P(),
            P(),
            P("ens", None),
        ),
        out_specs=(P("ens", "space", None, None), P("ens", "space", None, None)),
        check_vma=False,
    )
```

```python
import functools

import jax
import jax.numpy as jnp
from jax import lax
from jax.experimental import pallas as pl
from jax.experimental.pallas import tpu as pltpu
from jax.sharding import PartitionSpec as P

OMEGA = 0.8
HIGHEST = lax.Precision.HIGHEST
F32 = jnp.float32
MIB = 1 << 20
VMEM = pl.BlockSpec(memory_space=pltpu.VMEM)
SMEM = pl.BlockSpec(memory_space=pltpu.SMEM)
ANY = pl.BlockSpec(memory_space=pl.ANY)
REACH = 3
DEEP = 3
MICROSECOND = 3.0e6
EXPECTED = dict(planes=4, gather=6, sweep=13, local_heads=5, solve=5, mix=4, update=4)
SLOT = 8
SIDE = 2 * REACH + 1


def spot():
    slab = lax.axis_index("space")
    return lax.rem(slab, 2), lax.axis_index("ens"), slab


def recip(x):
    return pltpu.reciprocal(x, approx=True)


def call(kernel, name, out_shape, in_specs, out_specs, scratch=(), after=(), alias={}):
    tokens = len(after)

    def entry(*refs):
        kernel(*refs[tokens:])

    run = pl.pallas_call(
        entry,
        name=name,
        out_shape=out_shape,
        in_specs=[ANY] * tokens + list(in_specs),
        out_specs=out_specs,
        scratch_shapes=list(scratch),
        input_output_aliases={k + tokens: v for k, v in alias.items()},
        compiler_params=pltpu.CompilerParams(vmem_limit_bytes=64 * MIB),
        cost_estimate=pl.CostEstimate(
            flops=0, bytes_accessed=int(EXPECTED[name] * MICROSECOND), transcendentals=0
        ),
    )
    return functools.partial(run, *after)


def row_spans(depth, cut):
    return [(0, depth)] if cut is None else [(0, cut), (cut, depth)]


def planes_kernel(step, cut, lp, head, *refs):
    members, planes, depth, across = lp.shape
    spans = row_spans(depth, cut)
    parts = len(spans)
    sides = (refs[:parts], refs[parts : 2 * parts])
    own, raw, turned, perm, sem_in, sem_out = refs[2 * parts :]
    count = depth // step
    lines = depth // 8
    ins = []
    for b in range(count):
        rows = pl.ds(b * step, step)
        ins.append(
            pltpu.make_async_copy(lp.at[:, :, rows, :], raw.at[:, :, rows, :], sem_in.at[b])
        )
        ins[-1].start()
    odd, _, _ = spot()
    outs = []

    def send(src, dst):
        copy = pltpu.make_async_copy(src, dst, sem_out.at[len(outs)])
        copy.start()
        outs.append(copy)

    for i in range(planes):
        for k in range(lines):
            perm[i, depth + k] = head[i, pl.ds(8 * k, 8), :]
    plane = (1 - odd, odd)
    for s in range(2):
        send(
            perm.at[plane[s], pl.ds(depth, lines)],
            sides[s][0].at[pl.ds(spans[0][1], lines)],
        )
    sent = 0
    for b in range(count):
        ins[b].wait()

        def turn(k, carry):
            some = pl.ds(pl.multiple_of(b * step + 8 * k, 8), 8)
            for i in range(planes):
                x = jnp.swapaxes(raw[:, i, some, :], 0, 1)
                turned[i, some] = x
                perm[i, some] = jnp.exp(x)
            return carry

        lax.fori_loop(0, step // 8, turn, 0)
        rows = pl.ds(b * step, step)
        send(turned.at[:, rows], own.at[:, rows])
        while sent < parts and spans[sent][1] <= (b + 1) * step:
            lo, hi = spans[sent]
            for s in range(2):
                send(perm.at[plane[s], pl.ds(lo, hi - lo)], sides[s][sent].at[pl.ds(0, hi - lo)])
            sent += 1
    for copy in outs:
        copy.wait()


def planes_of(lp, head, cut, after=()):
    members, planes, depth, across = lp.shape
    step = 16
    lines = depth // 8
    spans = row_spans(depth, cut)
    sides = [
        jax.ShapeDtypeStruct((hi - lo + (lines if lo == 0 else 0), members, across), F32)
        for lo, hi in spans
    ]
    turned = (planes, depth, members, across)
    out = call(
        functools.partial(planes_kernel, step, cut),
        "planes",
        sides * 2 + [jax.ShapeDtypeStruct(turned, F32)],
        [ANY, VMEM],
        [ANY] * (2 * len(spans) + 1),
        [
            pltpu.VMEM(lp.shape, F32),
            pltpu.VMEM(turned, F32),
            pltpu.VMEM((planes, depth + lines, members, across), F32),
            pltpu.SemaphoreType.DMA((depth // step,)),
            pltpu.SemaphoreType.DMA((2 * len(spans) + depth // step + 2,)),
        ],
        after=after,
    )(lp, head)
    parts = len(spans)
    return out[:parts], out[parts : 2 * parts], out[2 * parts]


def sweep_kernel(cfg, *refs):
    mode, first, last, za, zb, depth, members, across, pieces = cfg
    pre, post = mode == "pre", mode == "post"
    refs = list(refs)
    odd, _, _ = spot()
    lines = {}
    if first:
        lines["d"] = refs.pop(0)
    if not (pre and first or post and not first):
        lines["f"] = refs.pop(0)
    if first and not pre:
        lines["s"] = refs.pop(0)
    named = {}
    for key, spans in pieces:
        named[key] = [(refs.pop(0), lo, hi) for lo, hi in spans]
    if pre:
        outs = [refs.pop(0)]
        w_out = refs.pop(0) if first else None
    elif last:
        refs.pop(0)
        natural = refs.pop(0)
    else:
        outs = [refs.pop(0), refs.pop(0)]
        w_out = refs.pop(0) if first else None
    R, RP, H, HP, S, A, O, W, forcing = refs[:9]
    refs = refs[9:]
    dests = {"p": R, "h": H, "f": forcing}
    flat = {"w": W}
    if post:
        flat["t"] = refs.pop(0)
        flat["u"] = refs.pop(0)
    if first:
        DS, DA, HH, storage, head = refs[:5]
        refs = refs[5:]
        dests.update({"s": storage, "d": head})
    if last and not pre:
        NAT = refs.pop(0)
    sem_in, sem_out = refs
    zlo = max(za - 1, 0)
    zhi = min(zb, depth - 1)
    own = (1, 2)
    tiles = across // 128
    slots = {"a": 2 - odd, "b": 1 + odd, "ra": 3 - 3 * odd, "rb": 3 * odd}

    ends = []
    at = zlo
    for width in (4, 8, 12, 12, 12, 12, 12):
        if at >= zhi + 1:
            break
        ends.append(min(at + width, zhi + 1))
        at = ends[-1]
    if len(ends) > 1 and ends[-1] - ends[-2] < 4:
        ends.pop(-2)
    groups = []
    used = 0

    def copy_in(batch, src, dst):
        batch.append(pltpu.make_async_copy(src, dst, sem_in.at[len(batch) + used]))

    start = zlo
    for end in ends:
        batch = []
        for (kind, name), spans in named.items():
            low_row = za if kind in flat else zlo
            high_row = zb if kind in flat else zhi + 1
            for ref, lo, hi in spans:
                s, e = max(start, lo, low_row), min(end, hi, high_row)
                if s < e:
                    src, dst = pl.ds(s - lo, e - s), pl.ds(s - low_row, e - s)
                    if kind in flat:
                        copy_in(batch, ref.at[:, src], flat[kind].at[:, dst])
                    else:
                        copy_in(batch, ref.at[src], dests[kind].at[slots[name], dst])
        if start == zlo:
            for kind, ref in lines.items():
                copy_in(batch, ref, dests[kind])
            if first and not pre:
                for q, name in enumerate(("ra", "rb")):
                    ref, lo, hi = named["p", name][0]
                    some = pl.ds(hi - lo, depth // 8)
                    copy_in(batch, ref.at[some], HH.at[odd if q == 1 else 1 - odd])
        groups.append(batch)
        used += len(batch)
        start = end
    for batch in groups[:DEEP]:
        for copy in batch:
            copy.start()

    lane = lax.broadcasted_iota(jnp.int32, (members, 128), 1)
    final_lane = lane == 127
    first_lane = lane == 0

    def ahead(parts, beyond):
        turned = [pltpu.roll(x, 127, 1) for x in parts]
        out = [jnp.where(final_lane, turned[t + 1], turned[t]) for t in range(tiles - 1)]
        last_part = turned[-1]
        if beyond is not None:
            last_part = jnp.where(final_lane, beyond, last_part)
        return out + [last_part]

    def behind(parts):
        turned = [pltpu.roll(x, 1, 1) for x in parts]
        out = [jnp.where(first_lane, 0.0, turned[0])]
        return out + [jnp.where(first_lane, turned[t - 1], turned[t]) for t in range(1, tiles)]

    tile = [pl.ds(t * 128, 128) for t in range(tiles)]

    used_planes = own if pre else range(4)

    def load_row(z, chosen=used_planes):
        q = z - zlo
        for i in chosen:
            r = [recip(R[i, q, :, ys]) for ys in tile]
            rp = ahead(r, jnp.inf)
            for t, ys in enumerate(tile):
                R[i, q, :, ys] = r[t]
                RP[i, q, :, ys] = rp[t]
            if post and i in own:
                continue
            if first:
                if i in own:
                    row = head[i - 1, pl.ds(z, 1), :]
                else:
                    row = HH[i // 3, z // 8, pl.ds(lax.rem(z, 8), 1), :]
                row = jnp.broadcast_to(row, (members, across))
                h = [row[:, t * 128 : (t + 1) * 128] for t in range(tiles)]
            else:
                h = [H[i, q, :, ys] for ys in tile]
            hp = ahead(h, None)
            for t, ys in enumerate(tile):
                if first:
                    H[i, q, :, ys] = h[t]
                HP[i, q, :, ys] = hp[t]

    def process(z, emit=True, inner=True, load=False):
        c = z - zlo
        both = (c, c + 1) if inner else (c,)
        done = {}
        for t, ys in enumerate(tile):

            def get(ref):
                return {i: [ref[i, q, :, ys] for q in both] for i in used_planes}

            r, rp = get(R), get(RP)
            h, hp = ({}, {}) if post else (get(H), get(HP))
            if post:
                for i in (0, 3):
                    h[i] = [H[i, q, :, ys] for q in both]
                    hp[i] = [HP[i, q, :, ys] for q in both]
            total = {}
            for k, i in enumerate(own):
                total["s", i, 0] = S[k, :, ys]
                total["a", i, 0] = A[k, :, ys]
                if first:
                    total["ds", i, 0] = DS[k, :, ys]
                    total["da", i, 0] = DA[k, :, ys]

            def add(key, value):
                total[key] = total[key] + value if key in total else value

            def pair(scale, i, q, j, p, ahead):
                x = r[i][q] + (rp[j][p] if ahead else r[j][p])
                u = recip(x if scale == 1.0 else x * scale)
                if i in own:
                    add(("s", i, q), u * (hp[j][p] if ahead else h[j][p]))
                    if first:
                        add(("ds", i, q), u)
                if j in own:
                    add(("a" if ahead else "s", j, p), u * h[i][q])
                    if first:
                        add(("da" if ahead else "ds", j, p), u)

            w1, w2, w3 = 0.5, 1.0, 2.0
            sides = ((0, 1), (1, 2), (2, 3))
            if mode != "full":
                sides = sides[1:2] if pre else sides[::2]
            inside = () if post else own
            for i in inside:
                pair(w1, i, 0, i, 0, True)
            for i, j in sides:
                pair(w1, i, 0, j, 0, False)
                pair(w2, i, 0, j, 0, True)
                pair(w2, j, 0, i, 0, True)
            if inner:
                for i in inside:
                    pair(w1, i, 0, i, 1, False)
                    pair(w2, i, 0, i, 1, True)
                    pair(w2, i, 1, i, 0, True)
                for i, j in sides:
                    pair(w2, i, 0, j, 1, False)
                    pair(w2, i, 1, j, 0, False)
                    pair(w3, i, 0, j, 1, True)
                    pair(w3, i, 1, j, 0, True)
                    pair(w3, j, 0, i, 1, True)
                    pair(w3, j, 1, i, 0, True)
                for k, i in enumerate(own):
                    S[k, :, ys] = total["s", i, 1]
                    A[k, :, ys] = total["a", i, 1]
                    if first:
                        DS[k, :, ys] = total["ds", i, 1]
                        DA[k, :, ys] = total["da", i, 1]
            for key, value in total.items():
                if key[2] == 0:
                    done.setdefault(key[:2], []).append(value)
            if load:
                count = len(used_planes)
                load_row(z + 2, used_planes[t * count // tiles : (t + 1) * count // tiles])
        if not emit:
            return
        o = z - za
        for k, i in enumerate(own):
            moved = behind(done["a", i])
            if "f" in lines:
                source = forcing[k, pl.ds(z, 1), :]
            if first:
                da = behind(done["da", i])
                old_row = head[k, pl.ds(z, 1), :]
                if not pre:
                    store = storage[k, pl.ds(z, 1), :]
            for t, ys in enumerate(tile):
                cut = slice(t * 128, (t + 1) * 128)
                gathered = done["s", i][t] + moved[t]
                if first:
                    weight = done["ds", i][t] + da[t]
                    old = old_row[:, cut]
                elif not post:
                    old = H[i, c, :, ys]
                if pre and first:
                    O[k, o, :, ys] = gathered
                    W[k, o, :, ys] = weight
                    continue
                if first:
                    if post:
                        gathered = gathered + flat["t"][k, o, :, ys]
                        weight = weight + flat["u"][k, o, :, ys]
                    w = OMEGA * recip(store[:, cut] + weight)
                    W[k, o, :, ys] = w
                else:
                    w = W[k, o, :, ys]
                if post and not first:
                    O[k, o, :, ys] = flat["t"][k, o, :, ys] + w * gathered
                else:
                    O[k, o, :, ys] = (1.0 - OMEGA) * old + w * (source[:, cut] + gathered)

    results = []

    def start_out(src, dst):
        copy = pltpu.make_async_copy(src, dst, sem_out.at[len(results)])
        copy.start()
        results.append(copy)

    progress = [za]

    def flush(upto):
        if last and not pre:
            upto = upto // 8 * 8
        begin = progress[0]
        if upto <= begin:
            return
        progress[0] = upto
        rows = pl.ds(begin - za, upto - begin)
        if pre:
            start_out(O.at[:, rows], outs[0].at[:, rows])
            if first:
                start_out(W.at[:, rows], w_out.at[:, rows])
            return
        if last:

            def turn(b, carry):
                some = pl.ds(pl.multiple_of(b * 8, 8), 8)
                for k in range(2):
                    NAT[:, k, some, :] = jnp.swapaxes(O[k, some], 0, 1)
                return carry

            lax.fori_loop((begin - za) // 8, (upto - za) // 8, turn, 0)
            start_out(
                NAT.at[:, :, rows, :], natural.at[:, :, pl.ds(begin, upto - begin), :]
            )
            return
        start_out(O.at[1 - odd, rows], outs[0].at[rows])
        start_out(O.at[odd, rows], outs[1].at[rows])
        if first:
            start_out(W.at[:, rows], w_out.at[:, rows])

    S[...] = jnp.zeros_like(S)
    A[...] = jnp.zeros_like(A)
    if first:
        DS[...] = jnp.zeros_like(DS)
        DA[...] = jnp.zeros_like(DA)
    at = zlo
    for g, end in enumerate(ends):
        for copy in groups[g]:
            copy.wait()
        if g + DEEP < len(groups):
            for copy in groups[g + DEEP]:
                copy.start()
        if g == 0:
            load_row(zlo)
            load_row(zlo + 1)
            if zlo < za:
                load_row(zlo + 2)
                process(zlo, emit=False)
                at = za

        def body(z, carry):
            process(z, load=True)
            return carry

        lax.fori_loop(at, end - 2, body, 0, unroll=2)
        at = end - 2
        flush(at)
    process(zhi - 1)
    if zb == depth:
        process(zhi, inner=False)
    flush(zb)
    for copy in results:
        copy.wait()


def sweep_of(mode, first, last, shape, lines, fields, after=()):
    members, planes, depth, across = shape
    za, zb = 0, depth
    pieces = tuple((key, tuple((lo, hi) for _, lo, hi in spans)) for key, spans in fields.items())
    operands = list(lines)
    for spans in fields.values():
        operands += [ref for ref, _, _ in spans]
    copies = sum(len(spans) for spans in fields.values()) * 8 + 8
    field = pltpu.VMEM((4, depth, members, across), F32)
    line = pltpu.VMEM((2, members, across), F32)
    flat = pltpu.VMEM((2, depth, across), F32)
    both = pltpu.VMEM((2, depth, members, across), F32)
    scratch = [field] * 4 + [line] * 2 + [both] * 2 + [flat]
    if mode == "post":
        scratch += [both] * 2
    if first:
        scratch += [line] * 2 + [pltpu.VMEM((2, depth // 8, 8, across), F32)] + [flat] * 2
    pair = jax.ShapeDtypeStruct((2, depth, members, across), F32)
    if mode == "pre":
        out_shape = [pair] * (2 if first else 1)
    elif last:
        scratch += [pltpu.VMEM((members, 2, depth, across), F32)]
        out_shape = [jax.ShapeDtypeStruct(shape, F32)]
        operands.append(operands[0])
    else:
        out_shape = [jax.ShapeDtypeStruct((depth, members, across), F32)] * 2
        if first:
            out_shape += [pair]
    scratch += [pltpu.SemaphoreType.DMA((copies,)), pltpu.SemaphoreType.DMA((32,))]
    cfg = (mode, first, last, za, zb, depth, members, across, pieces)
    return call(
        functools.partial(sweep_kernel, cfg),
        "sweep",
        out_shape,
        [ANY] * len(operands),
        [ANY] * len(out_shape),
        scratch,
        after=after,
    )(*operands)


WAITS = {1: ("patches",), 2: ("partial",)}
CUTS = (None,)
ORDER = (
    "planes",
    "gather",
    (1,),
    (1, "post"),
    "local",
    (2,),
    (2, "post"),
    "solve",
    "update",
    (3,),
    (3, "post"),
)


def exact_pick(x, onehot):
    top = x.astype(jnp.bfloat16)
    rest = x - top.astype(F32)
    mid = rest.astype(jnp.bfloat16)
    low = (rest - mid.astype(F32)).astype(jnp.bfloat16)
    out = jnp.dot(low, onehot, preferred_element_type=F32)
    out = out + jnp.dot(mid, onehot, preferred_element_type=F32)
    return out + jnp.dot(top, onehot, preferred_element_type=F32)


def columns_of(cells, start, count, width, lanes, depth, across):
    lane = lax.broadcasted_iota(jnp.int32, (1, lanes), 1)
    at = lax.rem(lane, width)
    cell = jnp.zeros((1, lanes), jnp.int32)
    for o in range(count):
        cell = jnp.where((at >= o * SLOT) & (at < (o + 1) * SLOT), cells[start + o], cell)
    slot = lax.rem(lane, SLOT)
    y = lax.rem(cell, across) + slot - REACH
    y = jnp.where((slot < SIDE) & (at < count * SLOT), y, -1)
    line = lax.div(cell, across)
    return lax.div(line, depth), lax.rem(line, depth), y


def gather_kernel(slabs, wells, rates, cells, head, storage, own, *refs):
    outs = refs[:slabs]
    forcing, field, picked, held_p, held_e, packed, sems, sem_out = refs[slabs:]
    out = held_p
    planes, depth, across = head.shape
    members, lanes = picked.shape[2:]
    _, _, slab = spot()
    step = 16
    copies = []
    for b in range(depth // step):
        rows = pl.ds(b * step, step)
        copy = pltpu.make_async_copy(own.at[:, rows], field.at[:, rows], sems.at[b])
        copy.start()
        copies.append(copy)

    forcing[...] = storage[...] * head[...]
    lane = lax.broadcasted_iota(jnp.int32, (1, across), 1)

    def add_well(k, carry):
        cell = wells[k] - slab * (planes * depth * across)

        @pl.when((cell >= 0) & (cell < planes * depth * across))
        def _():
            line = lax.div(cell, across)
            x = lax.div(line, depth)
            z = lax.rem(line, depth)
            row = forcing[x, pl.ds(z, 1), :]
            here = lane == lax.rem(cell, across)
            forcing[x, pl.ds(z, 1), :] = row + jnp.where(here, rates[k], 0.0)

        return carry

    lax.fori_loop(0, wells.shape[0], add_well, 0)
    _, zcol, ycol = columns_of(cells, 0, lanes // SLOT, lanes, lanes, depth, across)
    across_ids = lax.broadcasted_iota(jnp.int32, (across, lanes), 0)
    onehot = jnp.where(across_ids == ycol, 1.0, 0.0).astype(jnp.bfloat16)
    held_p[...] = jnp.zeros_like(held_p)
    held_e[...] = jnp.zeros_like(held_e)
    depth_ids = lax.broadcasted_iota(jnp.int32, (depth, lanes), 0)
    for a, ref in enumerate((head, storage, forcing)):
        for i in range(planes):
            lines = exact_pick(ref[i], onehot)
            for d in range(SIDE):
                here = zcol + (d - REACH) == depth_ids
                line = jnp.sum(jnp.where(here, lines, 0.0), axis=0, keepdims=True)
                held_e[i, d, pl.ds(a, 1), :] = line
    results = []
    for b in range(depth // step):
        copies[b].wait()
        some = pl.ds(step * b, step)
        for i in range(planes):
            rows = field[i, some].reshape(step * members, across)
            picked[i, some] = exact_pick(rows, onehot).reshape(step, members, lanes)

        def body(k, carry):
            for i in range(planes):
                held = [out[i, d, pl.ds(0, members), :] for d in range(SIDE)]
                for e in range(8):
                    z = b * step + k * 8 + e
                    value = picked[i, z]
                    for d in range(SIDE):
                        held[d] = jnp.where(zcol + (d - REACH) == z, value, held[d])
                for d in range(SIDE):
                    out[i, d, pl.ds(0, members), :] = held[d]
            return carry

        lax.fori_loop(0, step // 8, body, 0)

    width = lanes // slabs
    first = lax.broadcasted_iota(jnp.int32, (members, 128), 1) < 64
    for t in range(slabs):
        tile = pl.ds(width * t // 128 * 128, 128)
        shift = width * t % 128
        for i in range(planes):
            for d in range(SIDE):
                p = pltpu.roll(held_p[i, d, :, tile], (128 - shift) % 128, 1)
                e = pltpu.roll(held_e[i, d, :, tile], (192 - shift) % 128, 1)
                packed[t, i, d] = jnp.where(first, p, e)
    for k in range(slabs):
        copy = pltpu.make_async_copy(packed.at[slab ^ k], outs[k], sem_out.at[k])
        copy.start()
        results.append(copy)
    for copy in results:
        copy.wait()


def gather_of(wells, rates, cells, head, storage, own, slabs, after=()):
    planes, depth, members, across = own.shape
    lanes = cells.shape[0] * SLOT
    held = (planes, SIDE, members, lanes)
    packed = (planes, SIDE, members, 128)
    return call(
        functools.partial(gather_kernel, slabs),
        "gather",
        [jax.ShapeDtypeStruct(packed, F32)] * slabs
        + [jax.ShapeDtypeStruct(head.shape, F32)],
        [SMEM] * 3 + [VMEM] * 2 + [ANY],
        [ANY] * slabs + [VMEM],
        [
            pltpu.VMEM(own.shape, F32),
            pltpu.VMEM((planes, depth, members, lanes), F32),
            pltpu.VMEM(held, F32),
            pltpu.VMEM(held, F32),
            pltpu.VMEM((slabs,) + packed, F32),
            pltpu.SemaphoreType.DMA((depth // 16,)),
            pltpu.SemaphoreType.DMA((slabs,)),
        ],
        after=after,
    )(wells, rates, cells, head, storage, own)


def local_kernel(nz, ny, nobs, slabs, peers, cells, *refs):
    blocks = refs[:slabs]
    out, R, RM, RP, H, HM, HP, ST, FO, W, NEW = refs[slabs:]
    members, lanes = R.shape[2:]
    _, block, slab = spot()
    share = nobs // slabs
    x0, zcol, ycol = columns_of(cells, slab * share, share, 64, lanes, nz, ny)

    def spread(ref, minus, plus, i, d, value):
        ref[i, d] = value
        minus[i, d] = pltpu.roll(value, 1, 1)
        plus[i, d] = pltpu.roll(value, lanes - 1, 1)

    def select(i, carry):
        x = x0 + (i - REACH)
        masks = [x == 2 * (slab ^ (g // 2)) + g % 2 for g in range(2 * slabs)]
        for d in range(SIDE):
            z = zcol + (d - REACH)
            inside = (x >= 0) & (x < 2 * slabs) & (z >= 0) & (z < nz)
            inside = inside & (ycol >= 0) & (ycol < ny)
            both = jnp.zeros((members, lanes), F32)
            for g in range(2 * slabs):
                both = jnp.where(masks[g], blocks[g // 2][g % 2, d], both)
            perm = both
            rest = pltpu.roll(both, 64, 1)
            r = jnp.where(inside, jnp.exp(-perm), jnp.inf)
            spread(R, RM, RP, i, d, r)
            head = jnp.broadcast_to(jnp.where(inside, rest[0:1], 0.0), (members, lanes))
            spread(H, HM, HP, i, d, head)
            ST[i, d] = jnp.where(inside, rest[1:2], 1.0)
            FO[i, d] = jnp.where(inside, rest[2:3], 0.0)
        return carry

    lax.fori_loop(0, SIDE, select, 0)
    rs, hs = (RM, R, RP), (HM, H, HP)

    def update(i, d, first):
        mine = R[i, d]
        total = {}
        weight = {}
        for a in (-1, 0, 1):
            for b in (-1, 0, 1):
                for c in (-1, 0, 1):
                    n = abs(a) + abs(b) + abs(c)
                    if n == 0:
                        continue
                    u = recip(mine + rs[c + 1][i + a, d + b])
                    t = u * hs[c + 1][i + a, d + b]
                    total[n] = total[n] + t if n in total else t
                    if first:
                        weight[n] = weight[n] + u if n in weight else u
        gathered = 2.0 * total[1] + total[2] + 0.5 * total[3]
        if first:
            diagonal = ST[i, d] + (2.0 * weight[1] + weight[2] + 0.5 * weight[3])
            w = OMEGA * recip(diagonal)
            W[i, d] = w
        else:
            w = W[i, d]
        return (1.0 - OMEGA) * H[i, d] + w * (FO[i, d] + gathered)

    for sweep in range(1, REACH):
        width = SIDE - 2 * sweep

        def body(i, carry):
            for d in range(sweep, SIDE - sweep):
                NEW[i, d] = update(i, d, sweep == 1)
            return carry

        lax.fori_loop(sweep, SIDE - sweep, body, 0)
        for i in range(sweep, SIDE - sweep):
            for d in range(sweep, SIDE - sweep):
                spread(H, HM, HP, i, d, NEW[i, d])
    final = update(REACH, REACH, False)
    lane = lax.broadcasted_iota(jnp.int32, (lanes, 128), 0)
    target = lax.broadcasted_iota(jnp.int32, (lanes, 128), 1) - block * (128 // peers)
    onehot = (lane == target * SLOT + REACH) & (target >= 0) & (target < share)
    out[...] = exact_pick(final, jnp.where(onehot, 1.0, 0.0).astype(jnp.bfloat16))


def local_of(nz, ny, cells, peers, blocks, after=()):
    nobs = cells.shape[0]
    lanes = 128
    members = blocks[0].shape[2]
    slabs = len(blocks)
    full = pltpu.VMEM((SIDE, SIDE, members, lanes), F32)
    line = pltpu.VMEM((SIDE, SIDE, 1, lanes), F32)
    return call(
        functools.partial(local_kernel, nz, ny, nobs, slabs, peers),
        "local_heads",
        jax.ShapeDtypeStruct((members, 128), F32),
        [SMEM] + [VMEM] * slabs,
        VMEM,
        [full] * 6 + [line] * 2 + [full] * 2,
        after=after,
    )(cells, *blocks)


def solve_kernel(nobs, peers, values, noise, step, perturb, *refs):
    *seen, out, aug = refs
    _, block, slab = spot()
    members = perturb.shape[0]
    total = peers * members
    width = 128 // peers
    share = nobs // len(seen)
    row = lax.broadcasted_iota(jnp.int32, (total, 128), 0)
    lane = lax.broadcasted_iota(jnp.int32, (total, 128), 1)
    mine = lax.div(row, members) == lax.div(lane, width)
    source = lax.broadcasted_iota(jnp.int32, (128, nobs), 0)
    target = lax.broadcasted_iota(jnp.int32, (128, nobs), 1)
    spot_of = lax.rem(source, width)
    heads = jnp.zeros((total, nobs), F32)
    for k, ref in enumerate(seen):
        line = jnp.where(mine, jnp.concatenate([ref[...]] * peers, 0), 0.0)
        onehot = (spot_of < share) & (target == (slab ^ k) * share + spot_of)
        heads = heads + exact_pick(line, jnp.where(onehot, 1.0, 0.0).astype(jnp.bfloat16))
    aug[pl.ds(0, total), pl.ds(0, nobs)] = heads
    mean = jnp.sum(heads, axis=0, keepdims=True) * (1.0 / total)
    dev = heads - mean
    contract = (((0,), (0,)), ((), ()))
    cov = lax.dot_general(dev, dev, contract, precision=HIGHEST, preferred_element_type=F32)
    cov = cov * (1.0 / (total - 1))
    row = lax.broadcasted_iota(jnp.int32, (nobs, nobs), 0)
    col = lax.broadcasted_iota(jnp.int32, (nobs, nobs), 1)
    system = cov + jnp.where(row == col, noise[...] * (1.0 / step[0]), 0.0)
    identity = jnp.where(row == col, 1.0, 0.0)
    work = jnp.concatenate([system, identity], 1)
    line = lax.broadcasted_iota(jnp.int32, work.shape, 0)
    for k in range(nobs):
        pivot = work[k : k + 1, :] * (1.0 / work[k : k + 1, k : k + 1])
        work = jnp.where(line == k, pivot, work - work[:, k : k + 1] * pivot)
    own = aug[pl.ds(pl.multiple_of(block * members, members), members), pl.ds(0, nobs)]
    inverse = work[:, nobs:]
    residual = values[...] + perturb[...] - own
    gain = jnp.dot(residual, inverse, precision=HIGHEST, preferred_element_type=F32)
    nt = (((1,), (1,)), ((), ()))
    mixing = lax.dot_general(gain, dev, nt, precision=HIGHEST, preferred_element_type=F32)
    out[...] = mixing * (1.0 / (total - 1))


def solve_of(seen, peers, values, noise, step, perturb, after=()):
    nobs = values.shape[0]
    members = perturb.shape[0]
    total = members * peers
    return call(
        functools.partial(solve_kernel, nobs, peers),
        "solve",
        jax.ShapeDtypeStruct((members, total), F32),
        [VMEM, VMEM, SMEM] + [VMEM] * (1 + len(seen)),
        VMEM,
        [pltpu.VMEM((total, 128), F32)],
        after=after,
    )(values[None], noise[None], step, perturb, *seen)


def update_kernel(step, mixing, lp, every, out, x, a, sem_lp, sem_in, sem_out):
    members, planes, depth, across = lp.shape
    peers = every.shape[0]
    blocks = [(b, i) for b in range(depth // step) for i in range(planes)]
    ahead = a.shape[0]
    ins, outs, fields = [], [], []
    for n, (b, i) in enumerate(blocks):
        rows = pl.ds(b * step, step)
        ins.append(
            pltpu.make_async_copy(every.at[:, i, rows], a.at[n % ahead], sem_in.at[n])
        )
        fields.append(
            pltpu.make_async_copy(lp.at[:, i, rows, :], x.at[:, i, rows, :], sem_lp.at[n])
        )
        outs.append(
            pltpu.make_async_copy(x.at[:, i, rows, :], out.at[:, i, rows, :], sem_out.at[n])
        )
    for n in range(ahead):
        ins[n].start()
        fields[n].start()
    m = mixing[...]
    m_top = m.astype(jnp.bfloat16)
    m_low = (m - m_top.astype(F32)).astype(jnp.bfloat16)
    left = jnp.concatenate([m_top, m_top], 1)
    right = jnp.concatenate([m_low, jnp.zeros_like(m_low)], 1)
    left = jnp.concatenate([left, right], 0)
    for n, (b, i) in enumerate(blocks):
        ins[n].wait()
        fields[n].wait()
        for g in range(step // 8):
            lines = []
            for z in range(8 * g, 8 * g + 8):
                f = jnp.concatenate([a[n % ahead, k, z] for k in range(peers)], 0)
                top = f.astype(jnp.bfloat16)
                low = (f - top.astype(F32)).astype(jnp.bfloat16)
                both = jnp.concatenate([top, low], 0)
                y = jnp.dot(left, both, preferred_element_type=F32)
                lines.append(y[:members] + y[members:])
            change = jnp.stack(lines, 0)
            some = pl.ds(b * step + 8 * g, 8)
            x[:, i, some, :] = x[:, i, some, :] + jnp.swapaxes(change, 0, 1)
        outs[n].start()
        if n + ahead < len(blocks):
            ins[n + ahead].start()
            fields[n + ahead].start()
    for copy in outs:
        copy.wait()


def update_of(mixing, lp, every, after=()):
    members, planes, depth, across = lp.shape
    peers = every.shape[0]
    step = 8
    ahead = 6
    count = planes * depth // step
    return call(
        functools.partial(update_kernel, step),
        "update",
        jax.ShapeDtypeStruct(lp.shape, F32),
        [VMEM, ANY, ANY],
        ANY,
        [
            pltpu.VMEM(lp.shape, F32),
            pltpu.VMEM((ahead, peers, step, members, across), F32),
            pltpu.SemaphoreType.DMA((count,)),
            pltpu.SemaphoreType.DMA((count,)),
            pltpu.SemaphoreType.DMA((count,)),
        ],
        after=after,
    )(mixing, lp, every)


def swap(x, axis, bit):
    return lax.ppermute(x, axis, [(i, i ^ bit) for i in range(lax.axis_size(axis))])


def swaps(parts, axis):
    return [parts[0]] + [swap(parts[k], axis, k) for k in range(1, lax.axis_size(axis))]


def halo(x, side):
    pairs = [(i, i + 1) for i in range(side, lax.axis_size("space") - 1, 2)]
    return lax.ppermute(x, "space", pairs + [(b, a) for a, b in pairs])


def shards(
    log_perm,
    storage,
    head_init,
    well_cells,
    well_rates,
    obs_cells,
    obs_values,
    noise_var,
    step_size,
    perturb,
):
    shape = log_perm.shape
    members, planes, depth, across = shape
    slabs = lax.axis_size("space")
    peers = lax.axis_size("ens")
    names = ("a", "b", "ra", "rb")
    state = {"token": ()}

    def after(*refs):
        state["token"] = refs

    def span(parts, cut):
        return [(x, lo, hi) for x, (lo, hi) in zip(parts, row_spans(depth, cut))]

    def planes_step():
        side_a, side_b, own = planes_of(log_perm, head_init, CUTS[0])
        far_a = [halo(x, 0) for x in side_a]
        far_b = [halo(x, 1) for x in side_b]
        sides = (side_a, side_b, far_a, far_b)
        state["perms"] = {("p", n): span(v, CUTS[0]) for n, v in zip(names, sides)}
        state["own"] = own
        state["every"] = lax.all_gather(own, "ens", axis=0)

    def gather_step():
        *patch, state["forcing"] = gather_of(
            well_cells, well_rates, obs_cells, head_init, storage, state["own"], slabs
        )
        state["patches"] = swaps(patch, "space")
        after(patch[0])

    def local_step():
        seen = local_of(
            depth, across, obs_cells, peers, state["patches"], after=state["token"]
        )
        after(seen)
        bit = 1
        while bit < peers:
            seen = seen + swap(seen, "ens", bit)
            bit *= 2
        state["partial"] = swaps([seen] * slabs, "space")

    def solve_step():
        state["mixing"] = solve_of(
            state["partial"], peers, obs_values, noise_var, step_size, perturb, after=state["token"]
        )
        after(state["mixing"])

    def update_step():
        state["updated"] = update_of(
            state["mixing"], log_perm, state["every"], after=state["token"]
        )
        after(state["updated"])

    def whole(ref):
        return [(ref, 0, depth)]

    def pre_step(sweep):
        first = sweep == 1
        perms = state["perms"]
        fields = {k: perms[k] for k in (("p", "a"), ("p", "b"))}
        if first:
            lines = [head_init]
        else:
            lines = [state["forcing"]]
            fields["h", "a"], fields["h", "b"] = (whole(x) for x in state["new"][:2])
            fields["w", "w"] = whole(state["weights"])
        state["pre"] = sweep_of(
            "pre", first, sweep == 3, shape, lines, fields, after=state["token"]
        )
        after(state["pre"][0])

    def sweep_step(sweep, mode):
        first, last = sweep == 1, sweep == 3
        post = mode == "post"
        lines = [head_init] if first else []
        if first or not post:
            lines.append(state["forcing"])
        if first:
            lines.append(storage)
        fields = dict(state["perms"])
        if not first:
            fields["w", "w"] = whole(state["weights"])
            for k, n in enumerate(names):
                if k >= 2 or not post:
                    fields["h", n] = whole(state["new"][k])
        if post:
            fields["t", "t"] = whole(state["pre"][0])
            if first:
                fields["u", "u"] = whole(state["pre"][1])
        token = state["token"]
        for key in WAITS.get(sweep, ()):
            token = token + tuple(state[key])
        out = sweep_of(mode, first, last, shape, lines, fields, after=token)
        if last:
            state["head"] = out[0]
        else:
            if first:
                state["weights"] = out[2]
            state["new"] = (out[0], out[1], halo(out[0], 0), halo(out[1], 1))
        after(out[0])

    steps = dict(
        planes=planes_step,
        gather=gather_step,
        local=local_step,
        solve=solve_step,
        update=update_step,
    )
    for step in ORDER:
        if isinstance(step, tuple):
            (pre_step if len(step) == 1 else sweep_step)(*step)
        else:
            steps[step]()
    return (state["head"], state["updated"])


def solution(mesh):
    return jax.shard_map(
        shards,
        mesh=mesh,
        in_specs=(
            P("ens", "space", None, None),
            P("space", None, None),
            P("space", None, None),
            P(),
            P(),
            P(),
            P(),
            P(),
            P(),
            P("ens", None),
        ),
        out_specs=(P("ens", "space", None, None), P("ens", "space", None, None)),
        check_vma=False,
    )
```

```python
import functools

import jax
import jax.numpy as jnp
from jax import lax
from jax.experimental import pallas as pl
from jax.experimental.pallas import tpu as pltpu
from jax.sharding import PartitionSpec as P

OMEGA = 0.8
HIGHEST = lax.Precision.HIGHEST
F32 = jnp.float32
MIB = 1 << 20
VMEM = pl.BlockSpec(memory_space=pltpu.VMEM)
SMEM = pl.BlockSpec(memory_space=pltpu.SMEM)
ANY = pl.BlockSpec(memory_space=pl.ANY)
REACH = 3
DEEP = 3
MICROSECOND = 3.0e6
EXPECTED = dict(planes=4, gather=6, sweep=13, local_heads=5, solve=5, mix=4, update=4)
SLOT = 8
SIDE = 2 * REACH + 1


def spot():
    slab = lax.axis_index("space")
    return lax.rem(slab, 2), lax.axis_index("ens"), slab


def recip(x):
    return pltpu.reciprocal(x, approx=True)


def call(kernel, name, out_shape, in_specs, out_specs, scratch=(), after=(), alias={}):
    tokens = len(after)

    def entry(*refs):
        kernel(*refs[tokens:])

    run = pl.pallas_call(
        entry,
        name=name,
        out_shape=out_shape,
        in_specs=[ANY] * tokens + list(in_specs),
        out_specs=out_specs,
        scratch_shapes=list(scratch),
        input_output_aliases={k + tokens: v for k, v in alias.items()},
        compiler_params=pltpu.CompilerParams(vmem_limit_bytes=64 * MIB),
        cost_estimate=pl.CostEstimate(
            flops=0, bytes_accessed=int(EXPECTED[name] * MICROSECOND), transcendentals=0
        ),
    )
    return functools.partial(run, *after)


def row_spans(depth, cut):
    return [(0, depth)] if cut is None else [(0, cut), (cut, depth)]


def planes_kernel(step, cut, lp, head, *refs):
    members, planes, depth, across = lp.shape
    spans = row_spans(depth, cut)
    parts = len(spans)
    sides = (refs[:parts], refs[parts : 2 * parts])
    own, raw, turned, perm, sem_in, sem_out = refs[2 * parts :]
    count = depth // step
    lines = depth // 8
    ins = []
    for b in range(count):
        rows = pl.ds(b * step, step)
        ins.append(
            pltpu.make_async_copy(lp.at[:, :, rows, :], raw.at[:, :, rows, :], sem_in.at[b])
        )
        ins[-1].start()
    odd, _, _ = spot()
    outs = []

    def send(src, dst):
        copy = pltpu.make_async_copy(src, dst, sem_out.at[len(outs)])
        copy.start()
        outs.append(copy)

    for i in range(planes):
        for k in range(lines):
            perm[i, depth + k] = head[i, pl.ds(8 * k, 8), :]
    plane = (1 - odd, odd)
    for s in range(2):
        send(
            perm.at[plane[s], pl.ds(depth, lines)],
            sides[s][0].at[pl.ds(spans[0][1], lines)],
        )
    sent = 0
    for b in range(count):
        ins[b].wait()

        def turn(k, carry):
            some = pl.ds(pl.multiple_of(b * step + 8 * k, 8), 8)
            for i in range(planes):
                x = jnp.swapaxes(raw[:, i, some, :], 0, 1)
                turned[i, some] = x
                perm[i, some] = jnp.exp(x)
            return carry

        lax.fori_loop(0, step // 8, turn, 0)
        rows = pl.ds(b * step, step)
        send(turned.at[:, rows], own.at[:, rows])
        while sent < parts and spans[sent][1] <= (b + 1) * step:
            lo, hi = spans[sent]
            for s in range(2):
                send(perm.at[plane[s], pl.ds(lo, hi - lo)], sides[s][sent].at[pl.ds(0, hi - lo)])
            sent += 1
    for copy in outs:
        copy.wait()


def planes_of(lp, head, cut, after=()):
    members, planes, depth, across = lp.shape
    step = 16
    lines = depth // 8
    spans = row_spans(depth, cut)
    sides = [
        jax.ShapeDtypeStruct((hi - lo + (lines if lo == 0 else 0), members, across), F32)
        for lo, hi in spans
    ]
    turned = (planes, depth, members, across)
    out = call(
        functools.partial(planes_kernel, step, cut),
        "planes",
        sides * 2 + [jax.ShapeDtypeStruct(turned, F32)],
        [ANY, VMEM],
        [ANY] * (2 * len(spans) + 1),
        [
            pltpu.VMEM(lp.shape, F32),
            pltpu.VMEM(turned, F32),
            pltpu.VMEM((planes, depth + lines, members, across), F32),
            pltpu.SemaphoreType.DMA((depth // step,)),
            pltpu.SemaphoreType.DMA((2 * len(spans) + depth // step + 2,)),
        ],
        after=after,
    )(lp, head)
    parts = len(spans)
    return out[:parts], out[parts : 2 * parts], out[2 * parts]


def sweep_kernel(cfg, *refs):
    mode, first, last, za, zb, depth, members, across, pieces = cfg
    pre, post = mode == "pre", mode == "post"
    refs = list(refs)
    odd, _, _ = spot()
    lines = {}
    if first:
        lines["d"] = refs.pop(0)
    if not (pre and first or post and not first):
        lines["f"] = refs.pop(0)
    if first and not pre:
        lines["s"] = refs.pop(0)
    named = {}
    for key, spans in pieces:
        named[key] = [(refs.pop(0), lo, hi) for lo, hi in spans]
    if pre:
        outs = [refs.pop(0)]
        w_out = refs.pop(0) if first else None
    elif last:
        refs.pop(0)
        natural = refs.pop(0)
    else:
        outs = [refs.pop(0), refs.pop(0)]
        w_out = refs.pop(0) if first else None
    R, RP, H, HP, S, A, O, W, forcing = refs[:9]
    refs = refs[9:]
    dests = {"p": R, "h": H, "f": forcing}
    flat = {"w": W}
    if post:
        flat["t"] = refs.pop(0)
        flat["u"] = refs.pop(0)
    if first:
        DS, DA, HH, storage, head = refs[:5]
        refs = refs[5:]
        dests.update({"s": storage, "d": head})
    if last and not pre:
        NAT = refs.pop(0)
    sem_in, sem_out = refs
    zlo = max(za - 1, 0)
    zhi = min(zb, depth - 1)
    own = (1, 2)
    tiles = across // 128
    slots = {"a": 2 - odd, "b": 1 + odd, "ra": 3 - 3 * odd, "rb": 3 * odd}

    ends = []
    at = zlo
    for width in (4, 8, 12, 12, 12, 12, 12):
        if at >= zhi + 1:
            break
        ends.append(min(at + width, zhi + 1))
        at = ends[-1]
    if len(ends) > 1 and ends[-1] - ends[-2] < 4:
        ends.pop(-2)
    groups = []
    used = 0

    def copy_in(batch, src, dst):
        batch.append(pltpu.make_async_copy(src, dst, sem_in.at[len(batch) + used]))

    start = zlo
    for end in ends:
        batch = []
        for (kind, name), spans in named.items():
            low_row = za if kind in flat else zlo
            high_row = zb if kind in flat else zhi + 1
            for ref, lo, hi in spans:
                s, e = max(start, lo, low_row), min(end, hi, high_row)
                if s < e:
                    src, dst = pl.ds(s - lo, e - s), pl.ds(s - low_row, e - s)
                    if kind in flat:
                        copy_in(batch, ref.at[:, src], flat[kind].at[:, dst])
                    else:
                        copy_in(batch, ref.at[src], dests[kind].at[slots[name], dst])
        if start == zlo:
            for kind, ref in lines.items():
                copy_in(batch, ref, dests[kind])
            if first and not pre:
                for q, name in enumerate(("ra", "rb")):
                    ref, lo, hi = named["p", name][0]
                    some = pl.ds(hi - lo, depth // 8)
                    copy_in(batch, ref.at[some], HH.at[odd if q == 1 else 1 - odd])
        groups.append(batch)
        used += len(batch)
        start = end
    for batch in groups[:DEEP]:
        for copy in batch:
            copy.start()

    lane = lax.broadcasted_iota(jnp.int32, (members, 128), 1)
    final_lane = lane == 127
    first_lane = lane == 0

    def ahead(parts, beyond):
        turned = [pltpu.roll(x, 127, 1) for x in parts]
        out = [jnp.where(final_lane, turned[t + 1], turned[t]) for t in range(tiles - 1)]
        last_part = turned[-1]
        if beyond is not None:
            last_part = jnp.where(final_lane, beyond, last_part)
        return out + [last_part]

    def behind(parts):
        turned = [pltpu.roll(x, 1, 1) for x in parts]
        out = [jnp.where(first_lane, 0.0, turned[0])]
        return out + [jnp.where(first_lane, turned[t - 1], turned[t]) for t in range(1, tiles)]

    tile = [pl.ds(t * 128, 128) for t in range(tiles)]

    used_planes = own if pre else range(4)

    def load_row(z, chosen=used_planes):
        q = z - zlo
        for i in chosen:
            r = [recip(R[i, q, :, ys]) for ys in tile]
            rp = ahead(r, jnp.inf)
            for t, ys in enumerate(tile):
                R[i, q, :, ys] = r[t]
                RP[i, q, :, ys] = rp[t]
            if post and i in own:
                continue
            if first:
                if i in own:
                    row = head[i - 1, pl.ds(z, 1), :]
                else:
                    row = HH[i // 3, z // 8, pl.ds(lax.rem(z, 8), 1), :]
                row = jnp.broadcast_to(row, (members, across))
                h = [row[:, t * 128 : (t + 1) * 128] for t in range(tiles)]
            else:
                h = [H[i, q, :, ys] for ys in tile]
            hp = ahead(h, None)
            for t, ys in enumerate(tile):
                if first:
                    H[i, q, :, ys] = h[t]
                HP[i, q, :, ys] = hp[t]

    def process(z, emit=True, inner=True, load=False):
        c = z - zlo
        both = (c, c + 1) if inner else (c,)
        done = {}
        for t, ys in enumerate(tile):

            def get(ref):
                return {i: [ref[i, q, :, ys] for q in both] for i in used_planes}

            r, rp = get(R), get(RP)
            h, hp = ({}, {}) if post else (get(H), get(HP))
            if post:
                for i in (0, 3):
                    h[i] = [H[i, q, :, ys] for q in both]
                    hp[i] = [HP[i, q, :, ys] for q in both]
            total = {}
            for k, i in enumerate(own):
                total["s", i, 0] = S[k, :, ys]
                total["a", i, 0] = A[k, :, ys]
                if first:
                    total["ds", i, 0] = DS[k, :, ys]
                    total["da", i, 0] = DA[k, :, ys]

            def add(key, value):
                total[key] = total[key] + value if key in total else value

            def pair(scale, i, q, j, p, ahead):
                x = r[i][q] + (rp[j][p] if ahead else r[j][p])
                u = recip(x if scale == 1.0 else x * scale)
                if i in own:
                    add(("s", i, q), u * (hp[j][p] if ahead else h[j][p]))
                    if first:
                        add(("ds", i, q), u)
                if j in own:
                    add(("a" if ahead else "s", j, p), u * h[i][q])
                    if first:
                        add(("da" if ahead else "ds", j, p), u)

            w1, w2, w3 = 0.5, 1.0, 2.0
            sides = ((0, 1), (1, 2), (2, 3))
            if mode != "full":
                sides = sides[1:2] if pre else sides[::2]
            inside = () if post else own
            for i in inside:
                pair(w1, i, 0, i, 0, True)
            for i, j in sides:
                pair(w1, i, 0, j, 0, False)
                pair(w2, i, 0, j, 0, True)
                pair(w2, j, 0, i, 0, True)
            if inner:
                for i in inside:
                    pair(w1, i, 0, i, 1, False)
                    pair(w2, i, 0, i, 1, True)
                    pair(w2, i, 1, i, 0, True)
                for i, j in sides:
                    pair(w2, i, 0, j, 1, False)
                    pair(w2, i, 1, j, 0, False)
                    pair(w3, i, 0, j, 1, True)
                    pair(w3, i, 1, j, 0, True)
                    pair(w3, j, 0, i, 1, True)
                    pair(w3, j, 1, i, 0, True)
                for k, i in enumerate(own):
                    S[k, :, ys] = total["s", i, 1]
                    A[k, :, ys] = total["a", i, 1]
                    if first:
                        DS[k, :, ys] = total["ds", i, 1]
                        DA[k, :, ys] = total["da", i, 1]
            for key, value in total.items():
                if key[2] == 0:
                    done.setdefault(key[:2], []).append(value)
            if load:
                count = len(used_planes)
                load_row(z + 2, used_planes[t * count // tiles : (t + 1) * count // tiles])
        if not emit:
            return
        o = z - za
        for k, i in enumerate(own):
            moved = behind(done["a", i])
            if "f" in lines:
                source = forcing[k, pl.ds(z, 1), :]
            if first:
                da = behind(done["da", i])
                old_row = head[k, pl.ds(z, 1), :]
                if not pre:
                    store = storage[k, pl.ds(z, 1), :]
            for t, ys in enumerate(tile):
                cut = slice(t * 128, (t + 1) * 128)
                gathered = done["s", i][t] + moved[t]
                if first:
                    weight = done["ds", i][t] + da[t]
                    old = old_row[:, cut]
                elif not post:
                    old = H[i, c, :, ys]
                if pre and first:
                    O[k, o, :, ys] = gathered
                    W[k, o, :, ys] = weight
                    continue
                if first:
                    if post:
                        gathered = gathered + flat["t"][k, o, :, ys]
                        weight = weight + flat["u"][k, o, :, ys]
                    w = OMEGA * recip(store[:, cut] + weight)
                    W[k, o, :, ys] = w
                else:
                    w = W[k, o, :, ys]
                if post and not first:
                    O[k, o, :, ys] = flat["t"][k, o, :, ys] + w * gathered
                else:
                    O[k, o, :, ys] = (1.0 - OMEGA) * old + w * (source[:, cut] + gathered)

    results = []

    def start_out(src, dst):
        copy = pltpu.make_async_copy(src, dst, sem_out.at[len(results)])
        copy.start()
        results.append(copy)

    progress = [za]

    def flush(upto):
        if last and not pre:
            upto = upto // 8 * 8
        begin = progress[0]
        if upto <= begin:
            return
        progress[0] = upto
        rows = pl.ds(begin - za, upto - begin)
        if pre:
            start_out(O.at[:, rows], outs[0].at[:, rows])
            if first:
                start_out(W.at[:, rows], w_out.at[:, rows])
            return
        if last:

            def turn(b, carry):
                some = pl.ds(pl.multiple_of(b * 8, 8), 8)
                for k in range(2):
                    NAT[:, k, some, :] = jnp.swapaxes(O[k, some], 0, 1)
                return carry

            lax.fori_loop((begin - za) // 8, (upto - za) // 8, turn, 0)
            start_out(
                NAT.at[:, :, rows, :], natural.at[:, :, pl.ds(begin, upto - begin), :]
            )
            return
        start_out(O.at[1 - odd, rows], outs[0].at[rows])
        start_out(O.at[odd, rows], outs[1].at[rows])
        if first:
            start_out(W.at[:, rows], w_out.at[:, rows])

    S[...] = jnp.zeros_like(S)
    A[...] = jnp.zeros_like(A)
    if first:
        DS[...] = jnp.zeros_like(DS)
        DA[...] = jnp.zeros_like(DA)
    at = zlo
    for g, end in enumerate(ends):
        for copy in groups[g]:
            copy.wait()
        if g + DEEP < len(groups):
            for copy in groups[g + DEEP]:
                copy.start()
        if g == 0:
            load_row(zlo)
            load_row(zlo + 1)
            if zlo < za:
                load_row(zlo + 2)
                process(zlo, emit=False)
                at = za

        def body(z, carry):
            process(z, load=True)
            return carry

        lax.fori_loop(at, end - 2, body, 0, unroll=2)
        at = end - 2
        flush(at)
    process(zhi - 1)
    if zb == depth:
        process(zhi, inner=False)
    flush(zb)
    for copy in results:
        copy.wait()


def sweep_of(mode, first, last, shape, lines, fields, after=()):
    members, planes, depth, across = shape
    za, zb = 0, depth
    pieces = tuple((key, tuple((lo, hi) for _, lo, hi in spans)) for key, spans in fields.items())
    operands = list(lines)
    for spans in fields.values():
        operands += [ref for ref, _, _ in spans]
    copies = sum(len(spans) for spans in fields.values()) * 8 + 8
    field = pltpu.VMEM((4, depth, members, across), F32)
    line = pltpu.VMEM((2, members, across), F32)
    flat = pltpu.VMEM((2, depth, across), F32)
    both = pltpu.VMEM((2, depth, members, across), F32)
    scratch = [field] * 4 + [line] * 2 + [both] * 2 + [flat]
    if mode == "post":
        scratch += [both] * 2
    if first:
        scratch += [line] * 2 + [pltpu.VMEM((2, depth // 8, 8, across), F32)] + [flat] * 2
    pair = jax.ShapeDtypeStruct((2, depth, members, across), F32)
    if mode == "pre":
        out_shape = [pair] * (2 if first else 1)
    elif last:
        scratch += [pltpu.VMEM((members, 2, depth, across), F32)]
        out_shape = [jax.ShapeDtypeStruct(shape, F32)]
        operands.append(operands[0])
    else:
        out_shape = [jax.ShapeDtypeStruct((depth, members, across), F32)] * 2
        if first:
            out_shape += [pair]
    scratch += [pltpu.SemaphoreType.DMA((copies,)), pltpu.SemaphoreType.DMA((32,))]
    cfg = (mode, first, last, za, zb, depth, members, across, pieces)
    return call(
        functools.partial(sweep_kernel, cfg),
        "sweep",
        out_shape,
        [ANY] * len(operands),
        [ANY] * len(out_shape),
        scratch,
        after=after,
    )(*operands)


WAITS = {1: ("patches",), 2: ("partial",)}
CUTS = (None,)
ORDER = (
    "planes",
    "gather",
    (1,),
    (1, "post"),
    "local",
    (2,),
    (2, "post"),
    (3,),
    "update",
    (3, "post"),
)


def exact_pick(x, onehot):
    top = x.astype(jnp.bfloat16)
    rest = x - top.astype(F32)
    mid = rest.astype(jnp.bfloat16)
    low = (rest - mid.astype(F32)).astype(jnp.bfloat16)
    out = jnp.dot(low, onehot, preferred_element_type=F32)
    out = out + jnp.dot(mid, onehot, preferred_element_type=F32)
    return out + jnp.dot(top, onehot, preferred_element_type=F32)


def columns_of(cells, start, count, width, lanes, depth, across):
    lane = lax.broadcasted_iota(jnp.int32, (1, lanes), 1)
    at = lax.rem(lane, width)
    cell = jnp.zeros((1, lanes), jnp.int32)
    for o in range(count):
        cell = jnp.where((at >= o * SLOT) & (at < (o + 1) * SLOT), cells[start + o], cell)
    slot = lax.rem(lane, SLOT)
    y = lax.rem(cell, across) + slot - REACH
    y = jnp.where((slot < SIDE) & (at < count * SLOT), y, -1)
    line = lax.div(cell, across)
    return lax.div(line, depth), lax.rem(line, depth), y


def gather_kernel(slabs, wells, rates, cells, head, storage, own, *refs):
    outs = refs[:slabs]
    forcing, field, picked, held_p, held_e, packed, sems, sem_out = refs[slabs:]
    out = held_p
    planes, depth, across = head.shape
    members, lanes = picked.shape[2:]
    _, _, slab = spot()
    step = 16
    copies = []
    for b in range(depth // step):
        rows = pl.ds(b * step, step)
        copy = pltpu.make_async_copy(own.at[:, rows], field.at[:, rows], sems.at[b])
        copy.start()
        copies.append(copy)

    forcing[...] = storage[...] * head[...]
    lane = lax.broadcasted_iota(jnp.int32, (1, across), 1)

    def add_well(k, carry):
        cell = wells[k] - slab * (planes * depth * across)

        @pl.when((cell >= 0) & (cell < planes * depth * across))
        def _():
            line = lax.div(cell, across)
            x = lax.div(line, depth)
            z = lax.rem(line, depth)
            row = forcing[x, pl.ds(z, 1), :]
            here = lane == lax.rem(cell, across)
            forcing[x, pl.ds(z, 1), :] = row + jnp.where(here, rates[k], 0.0)

        return carry

    lax.fori_loop(0, wells.shape[0], add_well, 0)
    _, zcol, ycol = columns_of(cells, 0, lanes // SLOT, lanes, lanes, depth, across)
    across_ids = lax.broadcasted_iota(jnp.int32, (across, lanes), 0)
    onehot = jnp.where(across_ids == ycol, 1.0, 0.0).astype(jnp.bfloat16)
    held_p[...] = jnp.zeros_like(held_p)
    held_e[...] = jnp.zeros_like(held_e)
    depth_ids = lax.broadcasted_iota(jnp.int32, (depth, lanes), 0)
    for a, ref in enumerate((head, storage, forcing)):
        for i in range(planes):
            lines = exact_pick(ref[i], onehot)
            for d in range(SIDE):
                here = zcol + (d - REACH) == depth_ids
                line = jnp.sum(jnp.where(here, lines, 0.0), axis=0, keepdims=True)
                held_e[i, d, pl.ds(a, 1), :] = line
    results = []
    for b in range(depth // step):
        copies[b].wait()
        some = pl.ds(step * b, step)
        for i in range(planes):
            rows = field[i, some].reshape(step * members, across)
            picked[i, some] = exact_pick(rows, onehot).reshape(step, members, lanes)

        def body(k, carry):
            for i in range(planes):
                held = [out[i, d, pl.ds(0, members), :] for d in range(SIDE)]
                for e in range(8):
                    z = b * step + k * 8 + e
                    value = picked[i, z]
                    for d in range(SIDE):
                        held[d] = jnp.where(zcol + (d - REACH) == z, value, held[d])
                for d in range(SIDE):
                    out[i, d, pl.ds(0, members), :] = held[d]
            return carry

        lax.fori_loop(0, step // 8, body, 0)

    width = lanes // slabs
    first = lax.broadcasted_iota(jnp.int32, (members, 128), 1) < 64
    for t in range(slabs):
        tile = pl.ds(width * t // 128 * 128, 128)
        shift = width * t % 128
        for i in range(planes):
            for d in range(SIDE):
                p = pltpu.roll(held_p[i, d, :, tile], (128 - shift) % 128, 1)
                e = pltpu.roll(held_e[i, d, :, tile], (192 - shift) % 128, 1)
                packed[t, i, d] = jnp.where(first, p, e)
    for k in range(slabs):
        copy = pltpu.make_async_copy(packed.at[slab ^ k], outs[k], sem_out.at[k])
        copy.start()
        results.append(copy)
    for copy in results:
        copy.wait()


def gather_of(wells, rates, cells, head, storage, own, slabs, after=()):
    planes, depth, members, across = own.shape
    lanes = cells.shape[0] * SLOT
    held = (planes, SIDE, members, lanes)
    packed = (planes, SIDE, members, 128)
    return call(
        functools.partial(gather_kernel, slabs),
        "gather",
        [jax.ShapeDtypeStruct(packed, F32)] * slabs
        + [jax.ShapeDtypeStruct(head.shape, F32)],
        [SMEM] * 3 + [VMEM] * 2 + [ANY],
        [ANY] * slabs + [VMEM],
        [
            pltpu.VMEM(own.shape, F32),
            pltpu.VMEM((planes, depth, members, lanes), F32),
            pltpu.VMEM(held, F32),
            pltpu.VMEM(held, F32),
            pltpu.VMEM((slabs,) + packed, F32),
            pltpu.SemaphoreType.DMA((depth // 16,)),
            pltpu.SemaphoreType.DMA((slabs,)),
        ],
        after=after,
    )(wells, rates, cells, head, storage, own)


def local_kernel(nz, ny, nobs, slabs, peers, cells, *refs):
    blocks = refs[:slabs]
    out, R, RM, RP, H, HM, HP, ST, FO, W, NEW = refs[slabs:]
    members, lanes = R.shape[2:]
    _, block, slab = spot()
    share = nobs // slabs
    x0, zcol, ycol = columns_of(cells, slab * share, share, 64, lanes, nz, ny)

    def spread(ref, minus, plus, i, d, value):
        ref[i, d] = value
        minus[i, d] = pltpu.roll(value, 1, 1)
        plus[i, d] = pltpu.roll(value, lanes - 1, 1)

    def select(i, carry):
        x = x0 + (i - REACH)
        masks = [x == 2 * (slab ^ (g // 2)) + g % 2 for g in range(2 * slabs)]
        for d in range(SIDE):
            z = zcol + (d - REACH)
            inside = (x >= 0) & (x < 2 * slabs) & (z >= 0) & (z < nz)
            inside = inside & (ycol >= 0) & (ycol < ny)
            both = jnp.zeros((members, lanes), F32)
            for g in range(2 * slabs):
                both = jnp.where(masks[g], blocks[g // 2][g % 2, d], both)
            perm = both
            rest = pltpu.roll(both, 64, 1)
            r = jnp.where(inside, jnp.exp(-perm), jnp.inf)
            spread(R, RM, RP, i, d, r)
            head = jnp.broadcast_to(jnp.where(inside, rest[0:1], 0.0), (members, lanes))
            spread(H, HM, HP, i, d, head)
            ST[i, d] = jnp.where(inside, rest[1:2], 1.0)
            FO[i, d] = jnp.where(inside, rest[2:3], 0.0)
        return carry

    lax.fori_loop(0, SIDE, select, 0)
    rs, hs = (RM, R, RP), (HM, H, HP)

    def update(i, d, first):
        mine = R[i, d]
        total = {}
        weight = {}
        for a in (-1, 0, 1):
            for b in (-1, 0, 1):
                for c in (-1, 0, 1):
                    n = abs(a) + abs(b) + abs(c)
                    if n == 0:
                        continue
                    u = recip(mine + rs[c + 1][i + a, d + b])
                    t = u * hs[c + 1][i + a, d + b]
                    total[n] = total[n] + t if n in total else t
                    if first:
                        weight[n] = weight[n] + u if n in weight else u
        gathered = 2.0 * total[1] + total[2] + 0.5 * total[3]
        if first:
            diagonal = ST[i, d] + (2.0 * weight[1] + weight[2] + 0.5 * weight[3])
            w = OMEGA * recip(diagonal)
            W[i, d] = w
        else:
            w = W[i, d]
        return (1.0 - OMEGA) * H[i, d] + w * (FO[i, d] + gathered)

    for sweep in range(1, REACH):
        width = SIDE - 2 * sweep

        def body(i, carry):
            for d in range(sweep, SIDE - sweep):
                NEW[i, d] = update(i, d, sweep == 1)
            return carry

        lax.fori_loop(sweep, SIDE - sweep, body, 0)
        for i in range(sweep, SIDE - sweep):
            for d in range(sweep, SIDE - sweep):
                spread(H, HM, HP, i, d, NEW[i, d])
    final = update(REACH, REACH, False)
    lane = lax.broadcasted_iota(jnp.int32, (lanes, 128), 0)
    target = lax.broadcasted_iota(jnp.int32, (lanes, 128), 1) - block * (128 // peers)
    onehot = (lane == target * SLOT + REACH) & (target >= 0) & (target < share)
    out[...] = exact_pick(final, jnp.where(onehot, 1.0, 0.0).astype(jnp.bfloat16))


def local_of(nz, ny, cells, peers, blocks, after=()):
    nobs = cells.shape[0]
    lanes = 128
    members = blocks[0].shape[2]
    slabs = len(blocks)
    full = pltpu.VMEM((SIDE, SIDE, members, lanes), F32)
    line = pltpu.VMEM((SIDE, SIDE, 1, lanes), F32)
    return call(
        functools.partial(local_kernel, nz, ny, nobs, slabs, peers),
        "local_heads",
        jax.ShapeDtypeStruct((members, 128), F32),
        [SMEM] + [VMEM] * slabs,
        VMEM,
        [full] * 6 + [line] * 2 + [full] * 2,
        after=after,
    )(cells, *blocks)


def mixing_rows(nobs, peers, values, noise, step, perturb, seen, aug):
    _, block, slab = spot()
    members = perturb.shape[0]
    total = peers * members
    width = 128 // peers
    share = nobs // len(seen)
    row = lax.broadcasted_iota(jnp.int32, (total, 128), 0)
    lane = lax.broadcasted_iota(jnp.int32, (total, 128), 1)
    mine = lax.div(row, members) == lax.div(lane, width)
    source = lax.broadcasted_iota(jnp.int32, (128, nobs), 0)
    target = lax.broadcasted_iota(jnp.int32, (128, nobs), 1)
    spot_of = lax.rem(source, width)
    heads = jnp.zeros((total, nobs), F32)
    for k, ref in enumerate(seen):
        line = jnp.where(mine, jnp.concatenate([ref[...]] * peers, 0), 0.0)
        onehot = (spot_of < share) & (target == (slab ^ k) * share + spot_of)
        heads = heads + exact_pick(line, jnp.where(onehot, 1.0, 0.0).astype(jnp.bfloat16))
    aug[pl.ds(0, total), pl.ds(0, nobs)] = heads
    mean = jnp.sum(heads, axis=0, keepdims=True) * (1.0 / total)
    dev = heads - mean
    contract = (((0,), (0,)), ((), ()))
    cov = lax.dot_general(dev, dev, contract, precision=HIGHEST, preferred_element_type=F32)
    cov = cov * (1.0 / (total - 1))
    row = lax.broadcasted_iota(jnp.int32, (nobs, nobs), 0)
    col = lax.broadcasted_iota(jnp.int32, (nobs, nobs), 1)
    system = cov + jnp.where(row == col, noise[...] * (1.0 / step[0]), 0.0)
    identity = jnp.where(row == col, 1.0, 0.0)
    work = jnp.concatenate([system, identity], 1)
    line = lax.broadcasted_iota(jnp.int32, work.shape, 0)
    for k in range(nobs):
        pivot = work[k : k + 1, :] * (1.0 / work[k : k + 1, k : k + 1])
        work = jnp.where(line == k, pivot, work - work[:, k : k + 1] * pivot)
    own = aug[pl.ds(pl.multiple_of(block * members, members), members), pl.ds(0, nobs)]
    inverse = work[:, nobs:]
    residual = values[...] + perturb[...] - own
    gain = jnp.dot(residual, inverse, precision=HIGHEST, preferred_element_type=F32)
    nt = (((1,), (1,)), ((), ()))
    mixing = lax.dot_general(gain, dev, nt, precision=HIGHEST, preferred_element_type=F32)
    return mixing * (1.0 / (total - 1))


def update_kernel(step, nobs, values, noise, size, perturb, *refs):
    *seen, every, out, x, a, aug, sem_in, sem_out = refs
    members, planes, depth, across = out.shape
    peers = every.shape[0]
    _, me, _ = spot()
    blocks = [(b, i) for b in range(depth // step) for i in range(planes)]
    ahead = a.shape[0]
    ins, outs = [], []
    for n, (b, i) in enumerate(blocks):
        rows = pl.ds(b * step, step)
        ins.append(
            pltpu.make_async_copy(every.at[:, i, rows], a.at[n % ahead], sem_in.at[n])
        )
        outs.append(
            pltpu.make_async_copy(x.at[:, i, rows, :], out.at[:, i, rows, :], sem_out.at[n])
        )
    for n in range(ahead):
        ins[n].start()
    m = mixing_rows(nobs, peers, values, noise, size, perturb, seen, aug)
    m_top = m.astype(jnp.bfloat16)
    m_low = (m - m_top.astype(F32)).astype(jnp.bfloat16)
    left = jnp.concatenate([m_top, m_top], 1)
    right = jnp.concatenate([m_low, jnp.zeros_like(m_low)], 1)
    left = jnp.concatenate([left, right], 0)
    for n, (b, i) in enumerate(blocks):
        ins[n].wait()
        for g in range(step // 8):
            lines = []
            for z in range(8 * g, 8 * g + 8):
                f = jnp.concatenate([a[n % ahead, k, z] for k in range(peers)], 0)
                top = f.astype(jnp.bfloat16)
                low = (f - top.astype(F32)).astype(jnp.bfloat16)
                both = jnp.concatenate([top, low], 0)
                y = jnp.dot(left, both, preferred_element_type=F32)
                lines.append(a[n % ahead, me, z] + (y[:members] + y[members:]))
            some = pl.ds(b * step + 8 * g, 8)
            x[:, i, some, :] = jnp.swapaxes(jnp.stack(lines, 0), 0, 1)
        outs[n].start()
        if n + ahead < len(blocks):
            ins[n + ahead].start()
    for copy in outs:
        copy.wait()


def update_of(seen, values, noise, size, perturb, every, after=()):
    peers, planes, depth, members, across = every.shape
    nobs = values.shape[0]
    step = 8
    ahead = 12
    count = planes * depth // step
    shape = (members, planes, depth, across)
    return call(
        functools.partial(update_kernel, step, nobs),
        "update",
        jax.ShapeDtypeStruct(shape, F32),
        [VMEM, VMEM, SMEM, VMEM] + [VMEM] * len(seen) + [ANY],
        ANY,
        [
            pltpu.VMEM(shape, F32),
            pltpu.VMEM((ahead, peers, step, members, across), F32),
            pltpu.VMEM((peers * members, 128), F32),
            pltpu.SemaphoreType.DMA((count,)),
            pltpu.SemaphoreType.DMA((count,)),
        ],
        after=after,
    )(values[None], noise[None], size, perturb, *seen, every)


def swap(x, axis, bit):
    return lax.ppermute(x, axis, [(i, i ^ bit) for i in range(lax.axis_size(axis))])


def swaps(parts, axis):
    return [parts[0]] + [swap(parts[k], axis, k) for k in range(1, lax.axis_size(axis))]


def halo(x, side):
    pairs = [(i, i + 1) for i in range(side, lax.axis_size("space") - 1, 2)]
    return lax.ppermute(x, "space", pairs + [(b, a) for a, b in pairs])


def shards(
    log_perm,
    storage,
    head_init,
    well_cells,
    well_rates,
    obs_cells,
    obs_values,
    noise_var,
    step_size,
    perturb,
):
    shape = log_perm.shape
    members, planes, depth, across = shape
    slabs = lax.axis_size("space")
    peers = lax.axis_size("ens")
    names = ("a", "b", "ra", "rb")
    state = {"token": ()}

    def after(*refs):
        state["token"] = refs

    def span(parts, cut):
        return [(x, lo, hi) for x, (lo, hi) in zip(parts, row_spans(depth, cut))]

    def planes_step():
        side_a, side_b, own = planes_of(log_perm, head_init, CUTS[0])
        far_a = [halo(x, 0) for x in side_a]
        far_b = [halo(x, 1) for x in side_b]
        sides = (side_a, side_b, far_a, far_b)
        state["perms"] = {("p", n): span(v, CUTS[0]) for n, v in zip(names, sides)}
        state["own"] = own
        state["every"] = lax.all_gather(own, "ens", axis=0)

    def gather_step():
        *patch, state["forcing"] = gather_of(
            well_cells, well_rates, obs_cells, head_init, storage, state["own"], slabs
        )
        state["patches"] = swaps(patch, "space")
        after(patch[0])

    def local_step():
        seen = local_of(
            depth, across, obs_cells, peers, state["patches"], after=state["token"]
        )
        after(seen)
        bit = 1
        while bit < peers:
            seen = seen + swap(seen, "ens", bit)
            bit *= 2
        state["partial"] = swaps([seen] * slabs, "space")

    def update_step():
        state["updated"] = update_of(
            state["partial"],
            obs_values,
            noise_var,
            step_size,
            perturb,
            state["every"],
            after=state["token"],
        )
        after(state["updated"])

    def whole(ref):
        return [(ref, 0, depth)]

    def pre_step(sweep):
        first = sweep == 1
        perms = state["perms"]
        fields = {k: perms[k] for k in (("p", "a"), ("p", "b"))}
        if first:
            lines = [head_init]
        else:
            lines = [state["forcing"]]
            fields["h", "a"], fields["h", "b"] = (whole(x) for x in state["new"][:2])
            fields["w", "w"] = whole(state["weights"])
        state["pre"] = sweep_of(
            "pre", first, sweep == 3, shape, lines, fields, after=state["token"]
        )
        after(state["pre"][0])

    def sweep_step(sweep, mode):
        first, last = sweep == 1, sweep == 3
        post = mode == "post"
        lines = [head_init] if first else []
        if first or not post:
            lines.append(state["forcing"])
        if first:
            lines.append(storage)
        fields = dict(state["perms"])
        if not first:
            fields["w", "w"] = whole(state["weights"])
            for k, n in enumerate(names):
                if k >= 2 or not post:
                    fields["h", n] = whole(state["new"][k])
        if post:
            fields["t", "t"] = whole(state["pre"][0])
            if first:
                fields["u", "u"] = whole(state["pre"][1])
        token = state["token"]
        for key in WAITS.get(sweep, ()):
            token = token + tuple(state[key])
        out = sweep_of(mode, first, last, shape, lines, fields, after=token)
        if last:
            state["head"] = out[0]
        else:
            if first:
                state["weights"] = out[2]
            state["new"] = (out[0], out[1], halo(out[0], 0), halo(out[1], 1))
        after(out[0])

    steps = dict(
        planes=planes_step,
        gather=gather_step,
        local=local_step,
        update=update_step,
    )
    for step in ORDER:
        if isinstance(step, tuple):
            (pre_step if len(step) == 1 else sweep_step)(*step)
        else:
            steps[step]()
    return (state["head"], state["updated"])


def solution(mesh):
    return jax.shard_map(
        shards,
        mesh=mesh,
        in_specs=(
            P("ens", "space", None, None),
            P("space", None, None),
            P("space", None, None),
            P(),
            P(),
            P(),
            P(),
            P(),
            P(),
            P("ens", None),
        ),
        out_specs=(P("ens", "space", None, None), P("ens", "space", None, None)),
        check_vma=False,
    )
```

```python
import functools

import jax
import jax.numpy as jnp
from jax import lax
from jax.experimental import pallas as pl
from jax.experimental.pallas import tpu as pltpu
from jax.sharding import PartitionSpec as P

OMEGA = 0.8
HIGHEST = lax.Precision.HIGHEST
F32 = jnp.float32
MIB = 1 << 20
VMEM = pl.BlockSpec(memory_space=pltpu.VMEM)
SMEM = pl.BlockSpec(memory_space=pltpu.SMEM)
ANY = pl.BlockSpec(memory_space=pl.ANY)
REACH = 3
DEEP = 3
MICROSECOND = 3.0e6
EXPECTED = dict(planes=4, gather=6, sweep=13, local_heads=5, solve=5, mix=4, update=4)
SLOT = 8
SIDE = 2 * REACH + 1


def spot():
    slab = lax.axis_index("space")
    return lax.rem(slab, 2), lax.axis_index("ens"), slab


def recip(x):
    return pltpu.reciprocal(x, approx=True)


def call(kernel, name, out_shape, in_specs, out_specs, scratch=(), after=(), alias={}):
    tokens = len(after)

    def entry(*refs):
        kernel(*refs[tokens:])

    run = pl.pallas_call(
        entry,
        name=name,
        out_shape=out_shape,
        in_specs=[ANY] * tokens + list(in_specs),
        out_specs=out_specs,
        scratch_shapes=list(scratch),
        input_output_aliases={k + tokens: v for k, v in alias.items()},
        compiler_params=pltpu.CompilerParams(vmem_limit_bytes=64 * MIB),
        cost_estimate=pl.CostEstimate(
            flops=0, bytes_accessed=int(EXPECTED[name] * MICROSECOND), transcendentals=0
        ),
    )
    return functools.partial(run, *after)


def row_spans(depth, cut):
    return [(0, depth)] if cut is None else [(0, cut), (cut, depth)]


def planes_kernel(step, cut, lp, head, *refs):
    members, planes, depth, across = lp.shape
    spans = row_spans(depth, cut)
    parts = len(spans)
    sides = (refs[:parts], refs[parts : 2 * parts])
    own, raw, turned, perm, sem_in, sem_out = refs[2 * parts :]
    count = depth // step
    lines = depth // 8
    ins = []
    for b in range(count):
        rows = pl.ds(b * step, step)
        ins.append(
            pltpu.make_async_copy(lp.at[:, :, rows, :], raw.at[:, :, rows, :], sem_in.at[b])
        )
        ins[-1].start()
    odd, _, _ = spot()
    outs = []

    def send(src, dst):
        copy = pltpu.make_async_copy(src, dst, sem_out.at[len(outs)])
        copy.start()
        outs.append(copy)

    for i in range(planes):
        for k in range(lines):
            perm[i, depth + k] = head[i, pl.ds(8 * k, 8), :]
    plane = (1 - odd, odd)
    for s in range(2):
        send(
            perm.at[plane[s], pl.ds(depth, lines)],
            sides[s][0].at[pl.ds(spans[0][1], lines)],
        )
    sent = 0
    for b in range(count):
        ins[b].wait()

        def turn(k, carry):
            some = pl.ds(pl.multiple_of(b * step + 8 * k, 8), 8)
            for i in range(planes):
                x = jnp.swapaxes(raw[:, i, some, :], 0, 1)
                turned[i, some] = x
                perm[i, some] = jnp.exp(x)
            return carry

        lax.fori_loop(0, step // 8, turn, 0)
        rows = pl.ds(b * step, step)
        send(turned.at[:, rows], own.at[:, rows])
        while sent < parts and spans[sent][1] <= (b + 1) * step:
            lo, hi = spans[sent]
            for s in range(2):
                send(perm.at[plane[s], pl.ds(lo, hi - lo)], sides[s][sent].at[pl.ds(0, hi - lo)])
            sent += 1
    for copy in outs:
        copy.wait()


def planes_of(lp, head, cut, after=()):
    members, planes, depth, across = lp.shape
    step = 16
    lines = depth // 8
    spans = row_spans(depth, cut)
    sides = [
        jax.ShapeDtypeStruct((hi - lo + (lines if lo == 0 else 0), members, across), F32)
        for lo, hi in spans
    ]
    turned = (planes, depth, members, across)
    out = call(
        functools.partial(planes_kernel, step, cut),
        "planes",
        sides * 2 + [jax.ShapeDtypeStruct(turned, F32)],
        [ANY, VMEM],
        [ANY] * (2 * len(spans) + 1),
        [
            pltpu.VMEM(lp.shape, F32),
            pltpu.VMEM(turned, F32),
            pltpu.VMEM((planes, depth + lines, members, across), F32),
            pltpu.SemaphoreType.DMA((depth // step,)),
            pltpu.SemaphoreType.DMA((2 * len(spans) + depth // step + 2,)),
        ],
        after=after,
    )(lp, head)
    parts = len(spans)
    return out[:parts], out[parts : 2 * parts], out[2 * parts]


def sweep_kernel(cfg, *refs):
    mode, first, last, za, zb, depth, members, across, pieces = cfg
    pre, post = mode == "pre", mode == "post"
    refs = list(refs)
    odd, _, _ = spot()
    lines = {}
    if first:
        lines["d"] = refs.pop(0)
    if not (pre and first or post and not first):
        lines["f"] = refs.pop(0)
    if first and not pre:
        lines["s"] = refs.pop(0)
    named = {}
    for key, spans in pieces:
        named[key] = [(refs.pop(0), lo, hi) for lo, hi in spans]
    if pre:
        outs = [refs.pop(0)]
        w_out = refs.pop(0) if first else None
    elif last:
        refs.pop(0)
        natural = refs.pop(0)
    else:
        outs = [refs.pop(0), refs.pop(0)]
        w_out = refs.pop(0) if first else None
    R, RP, H, HP, S, A, O, W, forcing = refs[:9]
    refs = refs[9:]
    dests = {"p": R, "h": H, "f": forcing}
    flat = {"w": W}
    if post:
        flat["t"] = refs.pop(0)
        flat["u"] = refs.pop(0)
    if first:
        DS, DA, HH, storage, head = refs[:5]
        refs = refs[5:]
        dests.update({"s": storage, "d": head})
    if last and not pre:
        NAT = refs.pop(0)
    sem_in, sem_out = refs
    zlo = max(za - 1, 0)
    zhi = min(zb, depth - 1)
    own = (1, 2)
    tiles = across // 128
    slots = {"a": 2 - odd, "b": 1 + odd, "ra": 3 - 3 * odd, "rb": 3 * odd}

    ends = []
    at = zlo
    for width in (4, 8, 12, 12, 12, 12, 12):
        if at >= zhi + 1:
            break
        ends.append(min(at + width, zhi + 1))
        at = ends[-1]
    if len(ends) > 1 and ends[-1] - ends[-2] < 4:
        ends.pop(-2)
    groups = []
    used = 0

    def copy_in(batch, src, dst):
        batch.append(pltpu.make_async_copy(src, dst, sem_in.at[len(batch) + used]))

    start = zlo
    for end in ends:
        batch = []
        for (kind, name), spans in named.items():
            low_row = za if kind in flat else zlo
            high_row = zb if kind in flat else zhi + 1
            for ref, lo, hi in spans:
                s, e = max(start, lo, low_row), min(end, hi, high_row)
                if s < e:
                    src, dst = pl.ds(s - lo, e - s), pl.ds(s - low_row, e - s)
                    if kind in flat:
                        copy_in(batch, ref.at[:, src], flat[kind].at[:, dst])
                    else:
                        copy_in(batch, ref.at[src], dests[kind].at[slots[name], dst])
        if start == zlo:
            for kind, ref in lines.items():
                copy_in(batch, ref, dests[kind])
            if first and not pre:
                for q, name in enumerate(("ra", "rb")):
                    ref, lo, hi = named["p", name][0]
                    some = pl.ds(hi - lo, depth // 8)
                    copy_in(batch, ref.at[some], HH.at[odd if q == 1 else 1 - odd])
        groups.append(batch)
        used += len(batch)
        start = end
    for batch in groups[:DEEP]:
        for copy in batch:
            copy.start()

    lane = lax.broadcasted_iota(jnp.int32, (members, 128), 1)
    final_lane = lane == 127
    first_lane = lane == 0

    def ahead(parts, beyond):
        turned = [pltpu.roll(x, 127, 1) for x in parts]
        out = [jnp.where(final_lane, turned[t + 1], turned[t]) for t in range(tiles - 1)]
        last_part = turned[-1]
        if beyond is not None:
            last_part = jnp.where(final_lane, beyond, last_part)
        return out + [last_part]

    def behind(parts):
        turned = [pltpu.roll(x, 1, 1) for x in parts]
        out = [jnp.where(first_lane, 0.0, turned[0])]
        return out + [jnp.where(first_lane, turned[t - 1], turned[t]) for t in range(1, tiles)]

    tile = [pl.ds(t * 128, 128) for t in range(tiles)]

    used_planes = own if pre else range(4)

    def load_row(z, chosen=used_planes):
        q = z - zlo
        for i in chosen:
            r = [recip(R[i, q, :, ys]) for ys in tile]
            rp = ahead(r, jnp.inf)
            for t, ys in enumerate(tile):
                R[i, q, :, ys] = r[t]
                RP[i, q, :, ys] = rp[t]
            if post and i in own:
                continue
            if first:
                if i in own:
                    row = head[i - 1, pl.ds(z, 1), :]
                else:
                    row = HH[i // 3, z // 8, pl.ds(lax.rem(z, 8), 1), :]
                row = jnp.broadcast_to(row, (members, across))
                h = [row[:, t * 128 : (t + 1) * 128] for t in range(tiles)]
            else:
                h = [H[i, q, :, ys] for ys in tile]
            hp = ahead(h, None)
            for t, ys in enumerate(tile):
                if first:
                    H[i, q, :, ys] = h[t]
                HP[i, q, :, ys] = hp[t]

    def process(z, emit=True, inner=True, load=False):
        c = z - zlo
        both = (c, c + 1) if inner else (c,)
        done = {}
        for t, ys in enumerate(tile):

            def get(ref):
                return {i: [ref[i, q, :, ys] for q in both] for i in used_planes}

            r, rp = get(R), get(RP)
            h, hp = ({}, {}) if post else (get(H), get(HP))
            if post:
                for i in (0, 3):
                    h[i] = [H[i, q, :, ys] for q in both]
                    hp[i] = [HP[i, q, :, ys] for q in both]
            total = {}
            for k, i in enumerate(own):
                total["s", i, 0] = S[k, :, ys]
                total["a", i, 0] = A[k, :, ys]
                if first:
                    total["ds", i, 0] = DS[k, :, ys]
                    total["da", i, 0] = DA[k, :, ys]

            def add(key, value):
                total[key] = total[key] + value if key in total else value

            def pair(scale, i, q, j, p, ahead):
                x = r[i][q] + (rp[j][p] if ahead else r[j][p])
                u = recip(x if scale == 1.0 else x * scale)
                if i in own:
                    add(("s", i, q), u * (hp[j][p] if ahead else h[j][p]))
                    if first:
                        add(("ds", i, q), u)
                if j in own:
                    add(("a" if ahead else "s", j, p), u * h[i][q])
                    if first:
                        add(("da" if ahead else "ds", j, p), u)

            w1, w2, w3 = 0.5, 1.0, 2.0
            sides = ((0, 1), (1, 2), (2, 3))
            if mode != "full":
                sides = sides[1:2] if pre else sides[::2]
            inside = () if post else own
            for i in inside:
                pair(w1, i, 0, i, 0, True)
            for i, j in sides:
                pair(w1, i, 0, j, 0, False)
                pair(w2, i, 0, j, 0, True)
                pair(w2, j, 0, i, 0, True)
            if inner:
                for i in inside:
                    pair(w1, i, 0, i, 1, False)
                    pair(w2, i, 0, i, 1, True)
                    pair(w2, i, 1, i, 0, True)
                for i, j in sides:
                    pair(w2, i, 0, j, 1, False)
                    pair(w2, i, 1, j, 0, False)
                    pair(w3, i, 0, j, 1, True)
                    pair(w3, i, 1, j, 0, True)
                    pair(w3, j, 0, i, 1, True)
                    pair(w3, j, 1, i, 0, True)
                for k, i in enumerate(own):
                    S[k, :, ys] = total["s", i, 1]
                    A[k, :, ys] = total["a", i, 1]
                    if first:
                        DS[k, :, ys] = total["ds", i, 1]
                        DA[k, :, ys] = total["da", i, 1]
            for key, value in total.items():
                if key[2] == 0:
                    done.setdefault(key[:2], []).append(value)
            if load:
                count = len(used_planes)
                load_row(z + 2, used_planes[t * count // tiles : (t + 1) * count // tiles])
        if not emit:
            return
        o = z - za
        for k, i in enumerate(own):
            moved = behind(done["a", i])
            if "f" in lines:
                source = forcing[k, pl.ds(z, 1), :]
            if first:
                da = behind(done["da", i])
                old_row = head[k, pl.ds(z, 1), :]
                if not pre:
                    store = storage[k, pl.ds(z, 1), :]
            for t, ys in enumerate(tile):
                cut = slice(t * 128, (t + 1) * 128)
                gathered = done["s", i][t] + moved[t]
                if first:
                    weight = done["ds", i][t] + da[t]
                    old = old_row[:, cut]
                elif not post:
                    old = H[i, c, :, ys]
                if pre and first:
                    O[k, o, :, ys] = gathered
                    W[k, o, :, ys] = weight
                    continue
                if first:
                    if post:
                        gathered = gathered + flat["t"][k, o, :, ys]
                        weight = weight + flat["u"][k, o, :, ys]
                    w = OMEGA * recip(store[:, cut] + weight)
                    W[k, o, :, ys] = w
                else:
                    w = W[k, o, :, ys]
                if post and not first:
                    O[k, o, :, ys] = flat["t"][k, o, :, ys] + w * gathered
                else:
                    O[k, o, :, ys] = (1.0 - OMEGA) * old + w * (source[:, cut] + gathered)

    results = []

    def start_out(src, dst):
        copy = pltpu.make_async_copy(src, dst, sem_out.at[len(results)])
        copy.start()
        results.append(copy)

    progress = [za]

    def flush(upto):
        if last and not pre:
            upto = upto // 8 * 8
        begin = progress[0]
        if upto <= begin:
            return
        progress[0] = upto
        rows = pl.ds(begin - za, upto - begin)
        if pre:
            start_out(O.at[:, rows], outs[0].at[:, rows])
            if first:
                start_out(W.at[:, rows], w_out.at[:, rows])
            return
        if last:

            def turn(b, carry):
                some = pl.ds(pl.multiple_of(b * 8, 8), 8)
                for k in range(2):
                    NAT[:, k, some, :] = jnp.swapaxes(O[k, some], 0, 1)
                return carry

            lax.fori_loop((begin - za) // 8, (upto - za) // 8, turn, 0)
            start_out(
                NAT.at[:, :, rows, :], natural.at[:, :, pl.ds(begin, upto - begin), :]
            )
            return
        start_out(O.at[1 - odd, rows], outs[0].at[rows])
        start_out(O.at[odd, rows], outs[1].at[rows])
        if first:
            start_out(W.at[:, rows], w_out.at[:, rows])

    S[...] = jnp.zeros_like(S)
    A[...] = jnp.zeros_like(A)
    if first:
        DS[...] = jnp.zeros_like(DS)
        DA[...] = jnp.zeros_like(DA)
    at = zlo
    for g, end in enumerate(ends):
        for copy in groups[g]:
            copy.wait()
        if g + DEEP < len(groups):
            for copy in groups[g + DEEP]:
                copy.start()
        if g == 0:
            load_row(zlo)
            load_row(zlo + 1)
            if zlo < za:
                load_row(zlo + 2)
                process(zlo, emit=False)
                at = za

        def body(z, carry):
            process(z, load=True)
            return carry

        lax.fori_loop(at, end - 2, body, 0, unroll=2)
        at = end - 2
        flush(at)
    process(zhi - 1)
    if zb == depth:
        process(zhi, inner=False)
    flush(zb)
    for copy in results:
        copy.wait()


def sweep_of(mode, first, last, shape, lines, fields, after=()):
    members, planes, depth, across = shape
    za, zb = 0, depth
    pieces = tuple((key, tuple((lo, hi) for _, lo, hi in spans)) for key, spans in fields.items())
    operands = list(lines)
    for spans in fields.values():
        operands += [ref for ref, _, _ in spans]
    copies = sum(len(spans) for spans in fields.values()) * 8 + 8
    field = pltpu.VMEM((4, depth, members, across), F32)
    line = pltpu.VMEM((2, members, across), F32)
    flat = pltpu.VMEM((2, depth, across), F32)
    both = pltpu.VMEM((2, depth, members, across), F32)
    scratch = [field] * 4 + [line] * 2 + [both] * 2 + [flat]
    if mode == "post":
        scratch += [both] * 2
    if first:
        scratch += [line] * 2 + [pltpu.VMEM((2, depth // 8, 8, across), F32)] + [flat] * 2
    pair = jax.ShapeDtypeStruct((2, depth, members, across), F32)
    if mode == "pre":
        out_shape = [pair] * (2 if first else 1)
    elif last:
        scratch += [pltpu.VMEM((members, 2, depth, across), F32)]
        out_shape = [jax.ShapeDtypeStruct(shape, F32)]
        operands.append(operands[0])
    else:
        out_shape = [jax.ShapeDtypeStruct((depth, members, across), F32)] * 2
        if first:
            out_shape += [pair]
    scratch += [pltpu.SemaphoreType.DMA((copies,)), pltpu.SemaphoreType.DMA((32,))]
    cfg = (mode, first, last, za, zb, depth, members, across, pieces)
    return call(
        functools.partial(sweep_kernel, cfg),
        "sweep",
        out_shape,
        [ANY] * len(operands),
        [ANY] * len(out_shape),
        scratch,
        after=after,
    )(*operands)


WAITS = {2: ("partial",)}
CUTS = (None,)
ORDER = (
    "planes",
    "gather",
    (1,),
    (1, "post"),
    "local",
    (2,),
    (2, "post"),
    (3,),
    "update",
    (3, "post"),
)


def exact_pick(x, onehot):
    top = x.astype(jnp.bfloat16)
    rest = x - top.astype(F32)
    mid = rest.astype(jnp.bfloat16)
    low = (rest - mid.astype(F32)).astype(jnp.bfloat16)
    out = jnp.dot(low, onehot, preferred_element_type=F32)
    out = out + jnp.dot(mid, onehot, preferred_element_type=F32)
    return out + jnp.dot(top, onehot, preferred_element_type=F32)


def columns_of(cells, start, count, width, lanes, depth, across):
    lane = lax.broadcasted_iota(jnp.int32, (1, lanes), 1)
    at = lax.rem(lane, width)
    cell = jnp.zeros((1, lanes), jnp.int32)
    for o in range(count):
        cell = jnp.where((at >= o * SLOT) & (at < (o + 1) * SLOT), cells[start + o], cell)
    slot = lax.rem(lane, SLOT)
    y = lax.rem(cell, across) + slot - REACH
    y = jnp.where((slot < SIDE) & (at < count * SLOT), y, -1)
    line = lax.div(cell, across)
    return lax.div(line, depth), lax.rem(line, depth), y


def gather_kernel(slabs, wells, rates, cells, head, storage, own, *refs):
    outs = refs[:slabs]
    forcing, field, picked, held_p, held_e, packed, sems, sem_out = refs[slabs:]
    out = held_p
    planes, depth, across = head.shape
    members, lanes = picked.shape[2:]
    _, _, slab = spot()
    step = 16
    copies = []
    for b in range(depth // step):
        rows = pl.ds(b * step, step)
        copy = pltpu.make_async_copy(own.at[:, rows], field.at[:, rows], sems.at[b])
        copy.start()
        copies.append(copy)

    forcing[...] = storage[...] * head[...]
    lane = lax.broadcasted_iota(jnp.int32, (1, across), 1)

    def add_well(k, carry):
        cell = wells[k] - slab * (planes * depth * across)

        @pl.when((cell >= 0) & (cell < planes * depth * across))
        def _():
            line = lax.div(cell, across)
            x = lax.div(line, depth)
            z = lax.rem(line, depth)
            row = forcing[x, pl.ds(z, 1), :]
            here = lane == lax.rem(cell, across)
            forcing[x, pl.ds(z, 1), :] = row + jnp.where(here, rates[k], 0.0)

        return carry

    lax.fori_loop(0, wells.shape[0], add_well, 0)
    _, zcol, ycol = columns_of(cells, 0, lanes // SLOT, lanes, lanes, depth, across)
    across_ids = lax.broadcasted_iota(jnp.int32, (across, lanes), 0)
    onehot = jnp.where(across_ids == ycol, 1.0, 0.0).astype(jnp.bfloat16)
    held_p[...] = jnp.zeros_like(held_p)
    held_e[...] = jnp.zeros_like(held_e)
    depth_ids = lax.broadcasted_iota(jnp.int32, (depth, lanes), 0)
    for a, ref in enumerate((head, storage, forcing)):
        for i in range(planes):
            lines = exact_pick(ref[i], onehot)
            for d in range(SIDE):
                here = zcol + (d - REACH) == depth_ids
                line = jnp.sum(jnp.where(here, lines, 0.0), axis=0, keepdims=True)
                held_e[i, d, pl.ds(a, 1), :] = line
    results = []
    for b in range(depth // step):
        copies[b].wait()
        some = pl.ds(step * b, step)
        for i in range(planes):
            rows = field[i, some].reshape(step * members, across)
            picked[i, some] = exact_pick(rows, onehot).reshape(step, members, lanes)

        def body(k, carry):
            for i in range(planes):
                held = [out[i, d, pl.ds(0, members), :] for d in range(SIDE)]
                for e in range(8):
                    z = b * step + k * 8 + e
                    value = picked[i, z]
                    for d in range(SIDE):
                        held[d] = jnp.where(zcol + (d - REACH) == z, value, held[d])
                for d in range(SIDE):
                    out[i, d, pl.ds(0, members), :] = held[d]
            return carry

        lax.fori_loop(0, step // 8, body, 0)

    width = lanes // slabs
    first = lax.broadcasted_iota(jnp.int32, (members, 128), 1) < 64
    for t in range(slabs):
        tile = pl.ds(width * t // 128 * 128, 128)
        shift = width * t % 128
        for i in range(planes):
            for d in range(SIDE):
                p = pltpu.roll(held_p[i, d, :, tile], (128 - shift) % 128, 1)
                e = pltpu.roll(held_e[i, d, :, tile], (192 - shift) % 128, 1)
                packed[t, i, d] = jnp.where(first, p, e)
    for k in range(slabs):
        copy = pltpu.make_async_copy(packed.at[slab ^ k], outs[k], sem_out.at[k])
        copy.start()
        results.append(copy)
    for copy in results:
        copy.wait()


def gather_of(wells, rates, cells, head, storage, own, slabs, after=()):
    planes, depth, members, across = own.shape
    lanes = cells.shape[0] * SLOT
    held = (planes, SIDE, members, lanes)
    packed = (planes, SIDE, members, 128)
    return call(
        functools.partial(gather_kernel, slabs),
        "gather",
        [jax.ShapeDtypeStruct(packed, F32)] * slabs
        + [jax.ShapeDtypeStruct(head.shape, F32)],
        [SMEM] * 3 + [VMEM] * 2 + [ANY],
        [ANY] * slabs + [VMEM],
        [
            pltpu.VMEM(own.shape, F32),
            pltpu.VMEM((planes, depth, members, lanes), F32),
            pltpu.VMEM(held, F32),
            pltpu.VMEM(held, F32),
            pltpu.VMEM((slabs,) + packed, F32),
            pltpu.SemaphoreType.DMA((depth // 16,)),
            pltpu.SemaphoreType.DMA((slabs,)),
        ],
        after=after,
    )(wells, rates, cells, head, storage, own)


def local_kernel(nz, ny, nobs, slabs, peers, cells, *refs):
    blocks = refs[:slabs]
    out, R, RM, RP, H, HM, HP, ST, FO, W, NEW = refs[slabs:]
    members, lanes = R.shape[2:]
    _, block, slab = spot()
    share = nobs // slabs
    x0, zcol, ycol = columns_of(cells, slab * share, share, 64, lanes, nz, ny)

    def spread(ref, minus, plus, i, d, value):
        ref[i, d] = value
        minus[i, d] = pltpu.roll(value, 1, 1)
        plus[i, d] = pltpu.roll(value, lanes - 1, 1)

    def select(i, carry):
        x = x0 + (i - REACH)
        masks = [x == 2 * (slab ^ (g // 2)) + g % 2 for g in range(2 * slabs)]
        for d in range(SIDE):
            z = zcol + (d - REACH)
            inside = (x >= 0) & (x < 2 * slabs) & (z >= 0) & (z < nz)
            inside = inside & (ycol >= 0) & (ycol < ny)
            both = jnp.zeros((members, lanes), F32)
            for g in range(2 * slabs):
                both = jnp.where(masks[g], blocks[g // 2][g % 2, d], both)
            perm = both
            rest = pltpu.roll(both, 64, 1)
            r = jnp.where(inside, jnp.exp(-perm), jnp.inf)
            spread(R, RM, RP, i, d, r)
            head = jnp.broadcast_to(jnp.where(inside, rest[0:1], 0.0), (members, lanes))
            spread(H, HM, HP, i, d, head)
            ST[i, d] = jnp.where(inside, rest[1:2], 1.0)
            FO[i, d] = jnp.where(inside, rest[2:3], 0.0)
        return carry

    lax.fori_loop(0, SIDE, select, 0, unroll=True)
    rs, hs = (RM, R, RP), (HM, H, HP)

    def update(i, d, first):
        mine = R[i, d]
        total = {}
        weight = {}
        for a in (-1, 0, 1):
            for b in (-1, 0, 1):
                for c in (-1, 0, 1):
                    n = abs(a) + abs(b) + abs(c)
                    if n == 0:
                        continue
                    u = recip(mine + rs[c + 1][i + a, d + b])
                    t = u * hs[c + 1][i + a, d + b]
                    total[n] = total[n] + t if n in total else t
                    if first:
                        weight[n] = weight[n] + u if n in weight else u
        gathered = 2.0 * total[1] + total[2] + 0.5 * total[3]
        if first:
            diagonal = ST[i, d] + (2.0 * weight[1] + weight[2] + 0.5 * weight[3])
            w = OMEGA * recip(diagonal)
            W[i, d] = w
        else:
            w = W[i, d]
        return (1.0 - OMEGA) * H[i, d] + w * (FO[i, d] + gathered)

    for sweep in range(1, REACH):
        width = SIDE - 2 * sweep

        def body(i, carry):
            for d in range(sweep, SIDE - sweep):
                NEW[i, d] = update(i, d, sweep == 1)
            return carry

        lax.fori_loop(sweep, SIDE - sweep, body, 0, unroll=True)
        for i in range(sweep, SIDE - sweep):
            for d in range(sweep, SIDE - sweep):
                spread(H, HM, HP, i, d, NEW[i, d])
    final = update(REACH, REACH, False)
    lane = lax.broadcasted_iota(jnp.int32, (lanes, 128), 0)
    target = lax.broadcasted_iota(jnp.int32, (lanes, 128), 1) - block * (128 // peers)
    onehot = (lane == target * SLOT + REACH) & (target >= 0) & (target < share)
    out[...] = exact_pick(final, jnp.where(onehot, 1.0, 0.0).astype(jnp.bfloat16))


def local_of(nz, ny, cells, peers, blocks, after=()):
    nobs = cells.shape[0]
    lanes = 128
    members = blocks[0].shape[2]
    slabs = len(blocks)
    full = pltpu.VMEM((SIDE, SIDE, members, lanes), F32)
    line = pltpu.VMEM((SIDE, SIDE, 1, lanes), F32)
    return call(
        functools.partial(local_kernel, nz, ny, nobs, slabs, peers),
        "local_heads",
        jax.ShapeDtypeStruct((members, 128), F32),
        [SMEM] + [VMEM] * slabs,
        VMEM,
        [full] * 6 + [line] * 2 + [full] * 2,
        after=after,
    )(cells, *blocks)


def mixing_rows(nobs, peers, values, noise, step, perturb, seen, aug):
    _, block, slab = spot()
    members = perturb.shape[0]
    total = peers * members
    width = 128 // peers
    share = nobs // len(seen)
    row = lax.broadcasted_iota(jnp.int32, (total, 128), 0)
    lane = lax.broadcasted_iota(jnp.int32, (total, 128), 1)
    mine = lax.div(row, members) == lax.div(lane, width)
    source = lax.broadcasted_iota(jnp.int32, (128, nobs), 0)
    target = lax.broadcasted_iota(jnp.int32, (128, nobs), 1)
    spot_of = lax.rem(source, width)
    heads = jnp.zeros((total, nobs), F32)
    for k, ref in enumerate(seen):
        line = jnp.where(mine, jnp.concatenate([ref[...]] * peers, 0), 0.0)
        onehot = (spot_of < share) & (target == (slab ^ k) * share + spot_of)
        heads = heads + exact_pick(line, jnp.where(onehot, 1.0, 0.0).astype(jnp.bfloat16))
    aug[pl.ds(0, total), pl.ds(0, nobs)] = heads
    mean = jnp.sum(heads, axis=0, keepdims=True) * (1.0 / total)
    dev = heads - mean
    contract = (((0,), (0,)), ((), ()))
    cov = lax.dot_general(dev, dev, contract, precision=HIGHEST, preferred_element_type=F32)
    cov = cov * (1.0 / (total - 1))
    row = lax.broadcasted_iota(jnp.int32, (nobs, nobs), 0)
    col = lax.broadcasted_iota(jnp.int32, (nobs, nobs), 1)
    system = cov + jnp.where(row == col, noise[...] * (1.0 / step[0]), 0.0)
    identity = jnp.where(row == col, 1.0, 0.0)
    work = jnp.concatenate([system, identity], 1)
    line = lax.broadcasted_iota(jnp.int32, work.shape, 0)
    for k in range(nobs):
        pivot = work[k : k + 1, :] * (1.0 / work[k : k + 1, k : k + 1])
        work = jnp.where(line == k, pivot, work - work[:, k : k + 1] * pivot)
    own = aug[pl.ds(pl.multiple_of(block * members, members), members), pl.ds(0, nobs)]
    inverse = work[:, nobs:]
    residual = values[...] + perturb[...] - own
    gain = jnp.dot(residual, inverse, precision=HIGHEST, preferred_element_type=F32)
    nt = (((1,), (1,)), ((), ()))
    mixing = lax.dot_general(gain, dev, nt, precision=HIGHEST, preferred_element_type=F32)
    return mixing * (1.0 / (total - 1))


def update_kernel(step, nobs, values, noise, size, perturb, *refs):
    *seen, every, out, x, a, aug, sem_in, sem_out = refs
    members, planes, depth, across = out.shape
    peers = every.shape[0]
    _, me, _ = spot()
    blocks = [(b, i) for b in range(depth // step) for i in range(planes)]
    ahead = a.shape[0]
    ins, outs = [], []
    for n, (b, i) in enumerate(blocks):
        rows = pl.ds(b * step, step)
        ins.append(
            pltpu.make_async_copy(every.at[:, i, rows], a.at[n % ahead], sem_in.at[n])
        )
        outs.append(
            pltpu.make_async_copy(x.at[:, i, rows, :], out.at[:, i, rows, :], sem_out.at[n])
        )
    for n in range(ahead):
        ins[n].start()
    m = mixing_rows(nobs, peers, values, noise, size, perturb, seen, aug)
    m_top = m.astype(jnp.bfloat16)
    m_low = (m - m_top.astype(F32)).astype(jnp.bfloat16)
    left = jnp.concatenate([m_top, m_top], 1)
    right = jnp.concatenate([m_low, jnp.zeros_like(m_low)], 1)
    left = jnp.concatenate([left, right], 0)
    for n, (b, i) in enumerate(blocks):
        ins[n].wait()
        for g in range(step // 8):
            lines = []
            for z in range(8 * g, 8 * g + 8):
                f = jnp.concatenate([a[n % ahead, k, z] for k in range(peers)], 0)
                top = f.astype(jnp.bfloat16)
                low = (f - top.astype(F32)).astype(jnp.bfloat16)
                both = jnp.concatenate([top, low], 0)
                y = jnp.dot(left, both, preferred_element_type=F32)
                lines.append(a[n % ahead, me, z] + (y[:members] + y[members:]))
            some = pl.ds(b * step + 8 * g, 8)
            x[:, i, some, :] = jnp.swapaxes(jnp.stack(lines, 0), 0, 1)
        outs[n].start()
        if n + ahead < len(blocks):
            ins[n + ahead].start()
    for copy in outs:
        copy.wait()


def update_of(seen, values, noise, size, perturb, every, after=()):
    peers, planes, depth, members, across = every.shape
    nobs = values.shape[0]
    step = 8
    ahead = 12
    count = planes * depth // step
    shape = (members, planes, depth, across)
    return call(
        functools.partial(update_kernel, step, nobs),
        "update",
        jax.ShapeDtypeStruct(shape, F32),
        [VMEM, VMEM, SMEM, VMEM] + [VMEM] * len(seen) + [ANY],
        ANY,
        [
            pltpu.VMEM(shape, F32),
            pltpu.VMEM((ahead, peers, step, members, across), F32),
            pltpu.VMEM((peers * members, 128), F32),
            pltpu.SemaphoreType.DMA((count,)),
            pltpu.SemaphoreType.DMA((count,)),
        ],
        after=after,
    )(values[None], noise[None], size, perturb, *seen, every)


def swap(x, axis, bit):
    return lax.ppermute(x, axis, [(i, i ^ bit) for i in range(lax.axis_size(axis))])


def swaps(parts, axis):
    return [parts[0]] + [swap(parts[k], axis, k) for k in range(1, lax.axis_size(axis))]


def halo(x, side):
    pairs = [(i, i + 1) for i in range(side, lax.axis_size("space") - 1, 2)]
    return lax.ppermute(x, "space", pairs + [(b, a) for a, b in pairs])


def shards(
    log_perm,
    storage,
    head_init,
    well_cells,
    well_rates,
    obs_cells,
    obs_values,
    noise_var,
    step_size,
    perturb,
):
    shape = log_perm.shape
    members, planes, depth, across = shape
    slabs = lax.axis_size("space")
    peers = lax.axis_size("ens")
    names = ("a", "b", "ra", "rb")
    state = {"token": ()}

    def after(*refs):
        state["token"] = refs

    def span(parts, cut):
        return [(x, lo, hi) for x, (lo, hi) in zip(parts, row_spans(depth, cut))]

    def planes_step():
        side_a, side_b, own = planes_of(log_perm, head_init, CUTS[0])
        far_a = [halo(x, 0) for x in side_a]
        far_b = [halo(x, 1) for x in side_b]
        sides = (side_a, side_b, far_a, far_b)
        state["perms"] = {("p", n): span(v, CUTS[0]) for n, v in zip(names, sides)}
        state["own"] = own
        state["every"] = lax.all_gather(own, "ens", axis=0)

    def gather_step():
        *patch, state["forcing"] = gather_of(
            well_cells, well_rates, obs_cells, head_init, storage, state["own"], slabs
        )
        state["patches"] = swaps(patch, "space")
        after(patch[0])

    def local_step():
        seen = local_of(
            depth, across, obs_cells, peers, state["patches"], after=state["token"]
        )
        after(seen)
        bit = 1
        while bit < peers:
            seen = seen + swap(seen, "ens", bit)
            bit *= 2
        state["partial"] = swaps([seen] * slabs, "space")

    def update_step():
        state["updated"] = update_of(
            state["partial"],
            obs_values,
            noise_var,
            step_size,
            perturb,
            state["every"],
            after=state["token"],
        )
        after(state["updated"])

    def whole(ref):
        return [(ref, 0, depth)]

    def pre_step(sweep):
        first = sweep == 1
        perms = state["perms"]
        fields = {k: perms[k] for k in (("p", "a"), ("p", "b"))}
        if first:
            lines = [head_init]
        else:
            lines = [state["forcing"]]
            fields["h", "a"], fields["h", "b"] = (whole(x) for x in state["new"][:2])
            fields["w", "w"] = whole(state["weights"])
        state["pre"] = sweep_of(
            "pre", first, sweep == 3, shape, lines, fields, after=state["token"]
        )
        after(state["pre"][0])

    def sweep_step(sweep, mode):
        first, last = sweep == 1, sweep == 3
        post = mode == "post"
        lines = [head_init] if first else []
        if first or not post:
            lines.append(state["forcing"])
        if first:
            lines.append(storage)
        fields = dict(state["perms"])
        if not first:
            fields["w", "w"] = whole(state["weights"])
            for k, n in enumerate(names):
                if k >= 2 or not post:
                    fields["h", n] = whole(state["new"][k])
        if post:
            fields["t", "t"] = whole(state["pre"][0])
            if first:
                fields["u", "u"] = whole(state["pre"][1])
        token = state["token"]
        for key in WAITS.get(sweep, ()):
            token = token + tuple(state[key])
        out = sweep_of(mode, first, last, shape, lines, fields, after=token)
        if last:
            state["head"] = out[0]
        else:
            if first:
                state["weights"] = out[2]
            sent = out[:2]
            if first:
                held = lax.optimization_barrier((*sent, *state["patches"]))
                sent, state["patches"] = held[:2], list(held[2:])
            state["new"] = (out[0], out[1], halo(sent[0], 0), halo(sent[1], 1))
        after(out[0])

    steps = dict(
        planes=planes_step,
        gather=gather_step,
        local=local_step,
        update=update_step,
    )
    for step in ORDER:
        if isinstance(step, tuple):
            (pre_step if len(step) == 1 else sweep_step)(*step)
        else:
            steps[step]()
    return (state["head"], state["updated"])


def solution(mesh):
    return jax.shard_map(
        shards,
        mesh=mesh,
        in_specs=(
            P("ens", "space", None, None),
            P("space", None, None),
            P("space", None, None),
            P(),
            P(),
            P(),
            P(),
            P(),
            P(),
            P("ens", None),
        ),
        out_specs=(P("ens", "space", None, None), P("ens", "space", None, None)),
        check_vma=False,
    )
```

```python
import functools

import jax
import jax.numpy as jnp
from jax import lax
from jax.experimental import pallas as pl
from jax.experimental.pallas import tpu as pltpu
from jax.sharding import PartitionSpec as P

OMEGA = 0.8
HIGHEST = lax.Precision.HIGHEST
F32 = jnp.float32
MIB = 1 << 20
VMEM = pl.BlockSpec(memory_space=pltpu.VMEM)
SMEM = pl.BlockSpec(memory_space=pltpu.SMEM)
ANY = pl.BlockSpec(memory_space=pl.ANY)
REACH = 3
DEEP = 4
MICROSECOND = 3.0e6
EXPECTED = dict(planes=4, gather=6, sweep=13, local_heads=5, solve=5, mix=4, update=4)
SLOT = 8
SIDE = 2 * REACH + 1


def spot():
    slab = lax.axis_index("space")
    return lax.rem(slab, 2), lax.axis_index("ens"), slab


def recip(x):
    return pltpu.reciprocal(x, approx=True)


def call(kernel, name, out_shape, in_specs, out_specs, scratch=(), after=(), alias={}):
    tokens = len(after)

    def entry(*refs):
        kernel(*refs[tokens:])

    run = pl.pallas_call(
        entry,
        name=name,
        out_shape=out_shape,
        in_specs=[ANY] * tokens + list(in_specs),
        out_specs=out_specs,
        scratch_shapes=list(scratch),
        input_output_aliases={k + tokens: v for k, v in alias.items()},
        compiler_params=pltpu.CompilerParams(vmem_limit_bytes=64 * MIB),
        cost_estimate=pl.CostEstimate(
            flops=0, bytes_accessed=int(EXPECTED[name] * MICROSECOND), transcendentals=0
        ),
    )
    return functools.partial(run, *after)


def row_spans(depth, cut):
    return [(0, depth)] if cut is None else [(0, cut), (cut, depth)]


def planes_kernel(step, cut, lp, head, *refs):
    members, planes, depth, across = lp.shape
    spans = row_spans(depth, cut)
    parts = len(spans)
    sides = (refs[:parts], refs[parts : 2 * parts])
    own, raw, turned, perm, sem_in, sem_out = refs[2 * parts :]
    count = depth // step
    lines = depth // 8
    ins = []
    for b in range(count):
        rows = pl.ds(b * step, step)
        ins.append(
            pltpu.make_async_copy(lp.at[:, :, rows, :], raw.at[:, :, rows, :], sem_in.at[b])
        )
        ins[-1].start()
    odd, _, _ = spot()
    outs = []

    def send(src, dst):
        copy = pltpu.make_async_copy(src, dst, sem_out.at[len(outs)])
        copy.start()
        outs.append(copy)

    for i in range(planes):
        for k in range(lines):
            perm[i, depth + k] = head[i, pl.ds(8 * k, 8), :]
    plane = (1 - odd, odd)
    for s in range(2):
        send(
            perm.at[plane[s], pl.ds(depth, lines)],
            sides[s][0].at[pl.ds(spans[0][1], lines)],
        )
    sent = 0
    for b in range(count):
        ins[b].wait()

        def turn(k, carry):
            some = pl.ds(pl.multiple_of(b * step + 8 * k, 8), 8)
            for i in range(planes):
                x = jnp.swapaxes(raw[:, i, some, :], 0, 1)
                turned[i, some] = x
                perm[i, some] = jnp.exp(x)
            return carry

        lax.fori_loop(0, step // 8, turn, 0)
        rows = pl.ds(b * step, step)
        send(turned.at[:, rows], own.at[:, rows])
        while sent < parts and spans[sent][1] <= (b + 1) * step:
            lo, hi = spans[sent]
            for s in range(2):
                send(perm.at[plane[s], pl.ds(lo, hi - lo)], sides[s][sent].at[pl.ds(0, hi - lo)])
            sent += 1
    for copy in outs:
        copy.wait()


def planes_of(lp, head, cut, after=()):
    members, planes, depth, across = lp.shape
    step = 8
    lines = depth // 8
    spans = row_spans(depth, cut)
    sides = [
        jax.ShapeDtypeStruct((hi - lo + (lines if lo == 0 else 0), members, across), F32)
        for lo, hi in spans
    ]
    turned = (planes, depth, members, across)
    out = call(
        functools.partial(planes_kernel, step, cut),
        "planes",
        sides * 2 + [jax.ShapeDtypeStruct(turned, F32)],
        [ANY, VMEM],
        [ANY] * (2 * len(spans) + 1),
        [
            pltpu.VMEM(lp.shape, F32),
            pltpu.VMEM(turned, F32),
            pltpu.VMEM((planes, depth + lines, members, across), F32),
            pltpu.SemaphoreType.DMA((depth // step,)),
            pltpu.SemaphoreType.DMA((2 * len(spans) + depth // step + 2,)),
        ],
        after=after,
    )(lp, head)
    parts = len(spans)
    return out[:parts], out[parts : 2 * parts], out[2 * parts]


def sweep_kernel(cfg, *refs):
    mode, first, last, za, zb, depth, members, across, pieces = cfg
    pre, post = mode == "pre", mode == "post"
    refs = list(refs)
    odd, _, _ = spot()
    lines = {}
    if first:
        lines["d"] = refs.pop(0)
    if not (pre and first or post and not first):
        lines["f"] = refs.pop(0)
    if first and not pre:
        lines["s"] = refs.pop(0)
    named = {}
    for key, spans in pieces:
        named[key] = [(refs.pop(0), lo, hi) for lo, hi in spans]
    if pre:
        outs = [refs.pop(0)]
        w_out = refs.pop(0) if first else None
    elif last:
        refs.pop(0)
        natural = refs.pop(0)
    else:
        outs = [refs.pop(0), refs.pop(0)]
        w_out = refs.pop(0) if first else None
    R, RP, H, HP, S, A, O, W, forcing = refs[:9]
    refs = refs[9:]
    dests = {"p": R, "h": H, "f": forcing}
    flat = {"w": W}
    if post:
        flat["t"] = refs.pop(0)
        flat["u"] = refs.pop(0)
    if first:
        DS, DA, HH, storage, head = refs[:5]
        refs = refs[5:]
        dests.update({"s": storage, "d": head})
    if last and not pre:
        NAT = refs.pop(0)
    sem_in, sem_out = refs
    zlo = max(za - 1, 0)
    zhi = min(zb, depth - 1)
    own = (1, 2)
    tiles = across // 128
    slots = {"a": 2 - odd, "b": 1 + odd, "ra": 3 - 3 * odd, "rb": 3 * odd}

    ends = []
    at = zlo
    for width in (4, 4, 8, 8, 8, 8, 8, 8, 8):
        if at >= zhi + 1:
            break
        ends.append(min(at + width, zhi + 1))
        at = ends[-1]
    if len(ends) > 1 and ends[-1] - ends[-2] < 4:
        ends.pop(-2)
    groups = []
    used = 0

    def copy_in(batch, src, dst):
        batch.append(pltpu.make_async_copy(src, dst, sem_in.at[len(batch) + used]))

    start = zlo
    for end in ends:
        batch = []
        for (kind, name), spans in named.items():
            low_row = za if kind in flat else zlo
            high_row = zb if kind in flat else zhi + 1
            for ref, lo, hi in spans:
                s, e = max(start, lo, low_row), min(end, hi, high_row)
                if s < e:
                    src, dst = pl.ds(s - lo, e - s), pl.ds(s - low_row, e - s)
                    if kind in flat:
                        copy_in(batch, ref.at[:, src], flat[kind].at[:, dst])
                    else:
                        copy_in(batch, ref.at[src], dests[kind].at[slots[name], dst])
        if start == zlo:
            for kind, ref in lines.items():
                copy_in(batch, ref, dests[kind])
            if first and not pre:
                for q, name in enumerate(("ra", "rb")):
                    ref, lo, hi = named["p", name][0]
                    some = pl.ds(hi - lo, depth // 8)
                    copy_in(batch, ref.at[some], HH.at[odd if q == 1 else 1 - odd])
        groups.append(batch)
        used += len(batch)
        start = end
    for batch in groups[:DEEP]:
        for copy in batch:
            copy.start()

    lane = lax.broadcasted_iota(jnp.int32, (members, 128), 1)
    final_lane = lane == 127
    first_lane = lane == 0

    def ahead(parts, beyond):
        turned = [pltpu.roll(x, 127, 1) for x in parts]
        out = [jnp.where(final_lane, turned[t + 1], turned[t]) for t in range(tiles - 1)]
        last_part = turned[-1]
        if beyond is not None:
            last_part = jnp.where(final_lane, beyond, last_part)
        return out + [last_part]

    def behind(parts):
        turned = [pltpu.roll(x, 1, 1) for x in parts]
        out = [jnp.where(first_lane, 0.0, turned[0])]
        return out + [jnp.where(first_lane, turned[t - 1], turned[t]) for t in range(1, tiles)]

    tile = [pl.ds(t * 128, 128) for t in range(tiles)]

    used_planes = own if pre else range(4)

    def load_row(z, chosen=used_planes):
        q = z - zlo
        for i in chosen:
            r = [recip(R[i, q, :, ys]) for ys in tile]
            rp = ahead(r, jnp.inf)
            for t, ys in enumerate(tile):
                R[i, q, :, ys] = r[t]
                RP[i, q, :, ys] = rp[t]
            if post and i in own:
                continue
            if first:
                if i in own:
                    row = head[i - 1, pl.ds(z, 1), :]
                else:
                    row = HH[i // 3, z // 8, pl.ds(lax.rem(z, 8), 1), :]
                row = jnp.broadcast_to(row, (members, across))
                h = [row[:, t * 128 : (t + 1) * 128] for t in range(tiles)]
            else:
                h = [H[i, q, :, ys] for ys in tile]
            hp = ahead(h, None)
            for t, ys in enumerate(tile):
                if first:
                    H[i, q, :, ys] = h[t]
                HP[i, q, :, ys] = hp[t]

    def process(z, emit=True, inner=True, load=False):
        c = z - zlo
        both = (c, c + 1) if inner else (c,)
        done = {}
        for t, ys in enumerate(tile):

            def get(ref):
                return {i: [ref[i, q, :, ys] for q in both] for i in used_planes}

            r, rp = get(R), get(RP)
            h, hp = ({}, {}) if post else (get(H), get(HP))
            if post:
                for i in (0, 3):
                    h[i] = [H[i, q, :, ys] for q in both]
                    hp[i] = [HP[i, q, :, ys] for q in both]
            total = {}
            for k, i in enumerate(own):
                total["s", i, 0] = S[k, :, ys]
                total["a", i, 0] = A[k, :, ys]
                if first:
                    total["ds", i, 0] = DS[k, :, ys]
                    total["da", i, 0] = DA[k, :, ys]

            def add(key, value):
                total[key] = total[key] + value if key in total else value

            def pair(scale, i, q, j, p, ahead):
                x = r[i][q] + (rp[j][p] if ahead else r[j][p])
                u = recip(x if scale == 1.0 else x * scale)
                if i in own:
                    add(("s", i, q), u * (hp[j][p] if ahead else h[j][p]))
                    if first:
                        add(("ds", i, q), u)
                if j in own:
                    add(("a" if ahead else "s", j, p), u * h[i][q])
                    if first:
                        add(("da" if ahead else "ds", j, p), u)

            w1, w2, w3 = 0.5, 1.0, 2.0
            sides = ((0, 1), (1, 2), (2, 3))
            if mode != "full":
                sides = sides[1:2] if pre else sides[::2]
            inside = () if post else own
            for i in inside:
                pair(w1, i, 0, i, 0, True)
            for i, j in sides:
                pair(w1, i, 0, j, 0, False)
                pair(w2, i, 0, j, 0, True)
                pair(w2, j, 0, i, 0, True)
            if inner:
                for i in inside:
                    pair(w1, i, 0, i, 1, False)
                    pair(w2, i, 0, i, 1, True)
                    pair(w2, i, 1, i, 0, True)
                for i, j in sides:
                    pair(w2, i, 0, j, 1, False)
                    pair(w2, i, 1, j, 0, False)
                    pair(w3, i, 0, j, 1, True)
                    pair(w3, i, 1, j, 0, True)
                    pair(w3, j, 0, i, 1, True)
                    pair(w3, j, 1, i, 0, True)
                for k, i in enumerate(own):
                    S[k, :, ys] = total["s", i, 1]
                    A[k, :, ys] = total["a", i, 1]
                    if first:
                        DS[k, :, ys] = total["ds", i, 1]
                        DA[k, :, ys] = total["da", i, 1]
            for key, value in total.items():
                if key[2] == 0:
                    done.setdefault(key[:2], []).append(value)
            if load:
                count = len(used_planes)
                load_row(z + 2, used_planes[t * count // tiles : (t + 1) * count // tiles])
        if not emit:
            return
        o = z - za
        for k, i in enumerate(own):
            moved = behind(done["a", i])
            if "f" in lines:
                source = forcing[k, pl.ds(z, 1), :]
            if first:
                da = behind(done["da", i])
                old_row = head[k, pl.ds(z, 1), :]
                if not pre:
                    store = storage[k, pl.ds(z, 1), :]
            for t, ys in enumerate(tile):
                cut = slice(t * 128, (t + 1) * 128)
                gathered = done["s", i][t] + moved[t]
                if first:
                    weight = done["ds", i][t] + da[t]
                    old = old_row[:, cut]
                elif not post:
                    old = H[i, c, :, ys]
                if pre and first:
                    O[k, o, :, ys] = gathered
                    W[k, o, :, ys] = weight
                    continue
                if first:
                    if post:
                        gathered = gathered + flat["t"][k, o, :, ys]
                        weight = weight + flat["u"][k, o, :, ys]
                    w = OMEGA * recip(store[:, cut] + weight)
                    W[k, o, :, ys] = w
                else:
                    w = W[k, o, :, ys]
                if post and not first:
                    O[k, o, :, ys] = flat["t"][k, o, :, ys] + w * gathered
                else:
                    O[k, o, :, ys] = (1.0 - OMEGA) * old + w * (source[:, cut] + gathered)

    results = []

    def start_out(src, dst):
        copy = pltpu.make_async_copy(src, dst, sem_out.at[len(results)])
        copy.start()
        results.append(copy)

    progress = [za]

    def flush(upto):
        if last and not pre:
            upto = upto // 8 * 8
        begin = progress[0]
        if upto <= begin:
            return
        progress[0] = upto
        rows = pl.ds(begin - za, upto - begin)
        if pre:
            start_out(O.at[:, rows], outs[0].at[:, rows])
            if first:
                start_out(W.at[:, rows], w_out.at[:, rows])
            return
        if last:

            def turn(b, carry):
                some = pl.ds(pl.multiple_of(b * 8, 8), 8)
                for k in range(2):
                    NAT[:, k, some, :] = jnp.swapaxes(O[k, some], 0, 1)
                return carry

            lax.fori_loop((begin - za) // 8, (upto - za) // 8, turn, 0)
            start_out(
                NAT.at[:, :, rows, :], natural.at[:, :, pl.ds(begin, upto - begin), :]
            )
            return
        start_out(O.at[1 - odd, rows], outs[0].at[rows])
        start_out(O.at[odd, rows], outs[1].at[rows])
        if first:
            start_out(W.at[:, rows], w_out.at[:, rows])

    S[...] = jnp.zeros_like(S)
    A[...] = jnp.zeros_like(A)
    if first:
        DS[...] = jnp.zeros_like(DS)
        DA[...] = jnp.zeros_like(DA)
    at = zlo
    for g, end in enumerate(ends):
        for copy in groups[g]:
            copy.wait()
        if g + DEEP < len(groups):
            for copy in groups[g + DEEP]:
                copy.start()
        if g == 0:
            load_row(zlo)
            load_row(zlo + 1)
            if zlo < za:
                load_row(zlo + 2)
                process(zlo, emit=False)
                at = za

        def body(z, carry):
            process(z, load=True)
            return carry

        lax.fori_loop(at, end - 2, body, 0, unroll=2)
        at = end - 2
        flush(at)
    process(zhi - 1)
    if zb == depth:
        process(zhi, inner=False)
    flush(zb)
    for copy in results:
        copy.wait()


def sweep_of(mode, first, last, shape, lines, fields, after=()):
    members, planes, depth, across = shape
    za, zb = 0, depth
    pieces = tuple((key, tuple((lo, hi) for _, lo, hi in spans)) for key, spans in fields.items())
    operands = list(lines)
    for spans in fields.values():
        operands += [ref for ref, _, _ in spans]
    copies = sum(len(spans) for spans in fields.values()) * 10 + 8
    field = pltpu.VMEM((4, depth, members, across), F32)
    line = pltpu.VMEM((2, members, across), F32)
    flat = pltpu.VMEM((2, depth, across), F32)
    both = pltpu.VMEM((2, depth, members, across), F32)
    scratch = [field] * 4 + [line] * 2 + [both] * 2 + [flat]
    if mode == "post":
        scratch += [both] * 2
    if first:
        scratch += [line] * 2 + [pltpu.VMEM((2, depth // 8, 8, across), F32)] + [flat] * 2
    pair = jax.ShapeDtypeStruct((2, depth, members, across), F32)
    if mode == "pre":
        out_shape = [pair] * (2 if first else 1)
    elif last:
        scratch += [pltpu.VMEM((members, 2, depth, across), F32)]
        out_shape = [jax.ShapeDtypeStruct(shape, F32)]
        operands.append(operands[0])
    else:
        out_shape = [jax.ShapeDtypeStruct((depth, members, across), F32)] * 2
        if first:
            out_shape += [pair]
    scratch += [pltpu.SemaphoreType.DMA((copies,)), pltpu.SemaphoreType.DMA((32,))]
    cfg = (mode, first, last, za, zb, depth, members, across, pieces)
    return call(
        functools.partial(sweep_kernel, cfg),
        "sweep",
        out_shape,
        [ANY] * len(operands),
        [ANY] * len(out_shape),
        scratch,
        after=after,
    )(*operands)


WAITS = {2: ("partial",)}
CUTS = (None,)
ORDER = (
    "planes",
    "gather",
    (1,),
    (1, "post"),
    "local",
    (2,),
    (2, "post"),
    (3,),
    "update",
    (3, "post"),
)


def exact_pick(x, onehot):
    top = x.astype(jnp.bfloat16)
    rest = x - top.astype(F32)
    mid = rest.astype(jnp.bfloat16)
    low = (rest - mid.astype(F32)).astype(jnp.bfloat16)
    out = jnp.dot(low, onehot, preferred_element_type=F32)
    out = out + jnp.dot(mid, onehot, preferred_element_type=F32)
    return out + jnp.dot(top, onehot, preferred_element_type=F32)


def columns_of(cells, start, count, width, lanes, depth, across):
    lane = lax.broadcasted_iota(jnp.int32, (1, lanes), 1)
    at = lax.rem(lane, width)
    cell = jnp.zeros((1, lanes), jnp.int32)
    for o in range(count):
        cell = jnp.where((at >= o * SLOT) & (at < (o + 1) * SLOT), cells[start + o], cell)
    slot = lax.rem(lane, SLOT)
    y = lax.rem(cell, across) + slot - REACH
    y = jnp.where((slot < SIDE) & (at < count * SLOT), y, -1)
    line = lax.div(cell, across)
    return lax.div(line, depth), lax.rem(line, depth), y


def gather_kernel(slabs, wells, rates, cells, head, storage, own, *refs):
    outs = refs[:slabs]
    forcing, field, picked, held_p, held_e, packed, sems, sem_out = refs[slabs:]
    out = held_p
    planes, depth, across = head.shape
    members, lanes = picked.shape[2:]
    _, _, slab = spot()
    step = 16
    copies = []
    for b in range(depth // step):
        rows = pl.ds(b * step, step)
        copy = pltpu.make_async_copy(own.at[:, rows], field.at[:, rows], sems.at[b])
        copy.start()
        copies.append(copy)

    forcing[...] = storage[...] * head[...]
    lane = lax.broadcasted_iota(jnp.int32, (1, across), 1)

    def add_well(k, carry):
        cell = wells[k] - slab * (planes * depth * across)

        @pl.when((cell >= 0) & (cell < planes * depth * across))
        def _():
            line = lax.div(cell, across)
            x = lax.div(line, depth)
            z = lax.rem(line, depth)
            row = forcing[x, pl.ds(z, 1), :]
            here = lane == lax.rem(cell, across)
            forcing[x, pl.ds(z, 1), :] = row + jnp.where(here, rates[k], 0.0)

        return carry

    lax.fori_loop(0, wells.shape[0], add_well, 0)
    _, zcol, ycol = columns_of(cells, 0, lanes // SLOT, lanes, lanes, depth, across)
    across_ids = lax.broadcasted_iota(jnp.int32, (across, lanes), 0)
    onehot = jnp.where(across_ids == ycol, 1.0, 0.0).astype(jnp.bfloat16)
    held_p[...] = jnp.zeros_like(held_p)
    held_e[...] = jnp.zeros_like(held_e)
    depth_ids = lax.broadcasted_iota(jnp.int32, (depth, lanes), 0)
    for a, ref in enumerate((head, storage, forcing)):
        for i in range(planes):
            lines = exact_pick(ref[i], onehot)
            for d in range(SIDE):
                here = zcol + (d - REACH) == depth_ids
                line = jnp.sum(jnp.where(here, lines, 0.0), axis=0, keepdims=True)
                held_e[i, d, pl.ds(a, 1), :] = line
    results = []
    for b in range(depth // step):
        copies[b].wait()
        some = pl.ds(step * b, step)
        for i in range(planes):
            rows = field[i, some].reshape(step * members, across)
            picked[i, some] = exact_pick(rows, onehot).reshape(step, members, lanes)

        def body(k, carry):
            for i in range(planes):
                held = [out[i, d, pl.ds(0, members), :] for d in range(SIDE)]
                for e in range(8):
                    z = b * step + k * 8 + e
                    value = picked[i, z]
                    for d in range(SIDE):
                        held[d] = jnp.where(zcol + (d - REACH) == z, value, held[d])
                for d in range(SIDE):
                    out[i, d, pl.ds(0, members), :] = held[d]
            return carry

        lax.fori_loop(0, step // 8, body, 0)

    width = lanes // slabs
    first = lax.broadcasted_iota(jnp.int32, (members, 128), 1) < 64
    for t in range(slabs):
        tile = pl.ds(width * t // 128 * 128, 128)
        shift = width * t % 128
        for i in range(planes):
            for d in range(SIDE):
                p = pltpu.roll(held_p[i, d, :, tile], (128 - shift) % 128, 1)
                e = pltpu.roll(held_e[i, d, :, tile], (192 - shift) % 128, 1)
                packed[t, i, d] = jnp.where(first, p, e)
    for k in range(slabs):
        copy = pltpu.make_async_copy(packed.at[slab ^ k], outs[k], sem_out.at[k])
        copy.start()
        results.append(copy)
    for copy in results:
        copy.wait()


def gather_of(wells, rates, cells, head, storage, own, slabs, after=()):
    planes, depth, members, across = own.shape
    lanes = cells.shape[0] * SLOT
    held = (planes, SIDE, members, lanes)
    packed = (planes, SIDE, members, 128)
    return call(
        functools.partial(gather_kernel, slabs),
        "gather",
        [jax.ShapeDtypeStruct(packed, F32)] * slabs
        + [jax.ShapeDtypeStruct(head.shape, F32)],
        [SMEM] * 3 + [VMEM] * 2 + [ANY],
        [ANY] * slabs + [VMEM],
        [
            pltpu.VMEM(own.shape, F32),
            pltpu.VMEM((planes, depth, members, lanes), F32),
            pltpu.VMEM(held, F32),
            pltpu.VMEM(held, F32),
            pltpu.VMEM((slabs,) + packed, F32),
            pltpu.SemaphoreType.DMA((depth // 16,)),
            pltpu.SemaphoreType.DMA((slabs,)),
        ],
        after=after,
    )(wells, rates, cells, head, storage, own)


def local_kernel(nz, ny, nobs, slabs, peers, cells, *refs):
    blocks = refs[:slabs]
    out, R, RM, RP, H, HM, HP, ST, FO, W, NEW = refs[slabs:]
    members, lanes = R.shape[2:]
    _, block, slab = spot()
    share = nobs // slabs
    x0, zcol, ycol = columns_of(cells, slab * share, share, 64, lanes, nz, ny)

    def spread(ref, minus, plus, i, d, value):
        ref[i, d] = value
        minus[i, d] = pltpu.roll(value, 1, 1)
        plus[i, d] = pltpu.roll(value, lanes - 1, 1)

    def select(i, carry):
        x = x0 + (i - REACH)
        masks = [x == 2 * (slab ^ (g // 2)) + g % 2 for g in range(2 * slabs)]
        for d in range(SIDE):
            z = zcol + (d - REACH)
            inside = (x >= 0) & (x < 2 * slabs) & (z >= 0) & (z < nz)
            inside = inside & (ycol >= 0) & (ycol < ny)
            both = jnp.zeros((members, lanes), F32)
            for g in range(2 * slabs):
                both = jnp.where(masks[g], blocks[g // 2][g % 2, d], both)
            perm = both
            rest = pltpu.roll(both, 64, 1)
            r = jnp.where(inside, jnp.exp(-perm), jnp.inf)
            spread(R, RM, RP, i, d, r)
            head = jnp.broadcast_to(jnp.where(inside, rest[0:1], 0.0), (members, lanes))
            spread(H, HM, HP, i, d, head)
            ST[i, d] = jnp.where(inside, rest[1:2], 1.0)
            FO[i, d] = jnp.where(inside, rest[2:3], 0.0)
        return carry

    lax.fori_loop(0, SIDE, select, 0, unroll=True)
    rs, hs = (RM, R, RP), (HM, H, HP)

    def update(i, d, first):
        mine = R[i, d]
        total = {}
        weight = {}
        for a in (-1, 0, 1):
            for b in (-1, 0, 1):
                for c in (-1, 0, 1):
                    n = abs(a) + abs(b) + abs(c)
                    if n == 0:
                        continue
                    u = recip(mine + rs[c + 1][i + a, d + b])
                    t = u * hs[c + 1][i + a, d + b]
                    total[n] = total[n] + t if n in total else t
                    if first:
                        weight[n] = weight[n] + u if n in weight else u
        gathered = 2.0 * total[1] + total[2] + 0.5 * total[3]
        if first:
            diagonal = ST[i, d] + (2.0 * weight[1] + weight[2] + 0.5 * weight[3])
            w = OMEGA * recip(diagonal)
            W[i, d] = w
        else:
            w = W[i, d]
        return (1.0 - OMEGA) * H[i, d] + w * (FO[i, d] + gathered)

    for sweep in range(1, REACH):
        width = SIDE - 2 * sweep

        def body(i, carry):
            for d in range(sweep, SIDE - sweep):
                NEW[i, d] = update(i, d, sweep == 1)
            return carry

        lax.fori_loop(sweep, SIDE - sweep, body, 0, unroll=True)
        for i in range(sweep, SIDE - sweep):
            for d in range(sweep, SIDE - sweep):
                spread(H, HM, HP, i, d, NEW[i, d])
    final = update(REACH, REACH, False)
    lane = lax.broadcasted_iota(jnp.int32, (lanes, 128), 0)
    target = lax.broadcasted_iota(jnp.int32, (lanes, 128), 1) - block * (128 // peers)
    onehot = (lane == target * SLOT + REACH) & (target >= 0) & (target < share)
    out[...] = exact_pick(final, jnp.where(onehot, 1.0, 0.0).astype(jnp.bfloat16))


def local_of(nz, ny, cells, peers, blocks, after=()):
    nobs = cells.shape[0]
    lanes = 128
    members = blocks[0].shape[2]
    slabs = len(blocks)
    full = pltpu.VMEM((SIDE, SIDE, members, lanes), F32)
    line = pltpu.VMEM((SIDE, SIDE, 1, lanes), F32)
    return call(
        functools.partial(local_kernel, nz, ny, nobs, slabs, peers),
        "local_heads",
        jax.ShapeDtypeStruct((members, 128), F32),
        [SMEM] + [VMEM] * slabs,
        VMEM,
        [full] * 6 + [line] * 2 + [full] * 2,
        after=after,
    )(cells, *blocks)


def mixing_rows(nobs, peers, values, noise, step, perturb, seen, aug):
    _, block, slab = spot()
    members = perturb.shape[0]
    total = peers * members
    width = 128 // peers
    share = nobs // len(seen)
    row = lax.broadcasted_iota(jnp.int32, (total, 128), 0)
    lane = lax.broadcasted_iota(jnp.int32, (total, 128), 1)
    mine = lax.div(row, members) == lax.div(lane, width)
    source = lax.broadcasted_iota(jnp.int32, (128, nobs), 0)
    target = lax.broadcasted_iota(jnp.int32, (128, nobs), 1)
    spot_of = lax.rem(source, width)
    heads = jnp.zeros((total, nobs), F32)
    for k, ref in enumerate(seen):
        line = jnp.where(mine, jnp.concatenate([ref[...]] * peers, 0), 0.0)
        onehot = (spot_of < share) & (target == (slab ^ k) * share + spot_of)
        heads = heads + exact_pick(line, jnp.where(onehot, 1.0, 0.0).astype(jnp.bfloat16))
    aug[pl.ds(0, total), pl.ds(0, nobs)] = heads
    mean = jnp.sum(heads, axis=0, keepdims=True) * (1.0 / total)
    dev = heads - mean
    contract = (((0,), (0,)), ((), ()))
    cov = lax.dot_general(dev, dev, contract, precision=HIGHEST, preferred_element_type=F32)
    cov = cov * (1.0 / (total - 1))
    row = lax.broadcasted_iota(jnp.int32, (nobs, nobs), 0)
    col = lax.broadcasted_iota(jnp.int32, (nobs, nobs), 1)
    system = cov + jnp.where(row == col, noise[...] * (1.0 / step[0]), 0.0)
    identity = jnp.where(row == col, 1.0, 0.0)
    work = jnp.concatenate([system, identity], 1)
    line = lax.broadcasted_iota(jnp.int32, work.shape, 0)
    for k in range(nobs):
        pivot = work[k : k + 1, :] * (1.0 / work[k : k + 1, k : k + 1])
        work = jnp.where(line == k, pivot, work - work[:, k : k + 1] * pivot)
    own = aug[pl.ds(pl.multiple_of(block * members, members), members), pl.ds(0, nobs)]
    inverse = work[:, nobs:]
    residual = values[...] + perturb[...] - own
    gain = jnp.dot(residual, inverse, precision=HIGHEST, preferred_element_type=F32)
    nt = (((1,), (1,)), ((), ()))
    mixing = lax.dot_general(gain, dev, nt, precision=HIGHEST, preferred_element_type=F32)
    return mixing * (1.0 / (total - 1))


def update_kernel(step, nobs, values, noise, size, perturb, *refs):
    *seen, every, out, x, a, aug, sem_in, sem_out = refs
    members, planes, depth, across = out.shape
    peers = every.shape[0]
    _, me, _ = spot()
    blocks = [(b, i) for b in range(depth // step) for i in range(planes)]
    ahead = a.shape[0]
    ins, outs = [], []
    for n, (b, i) in enumerate(blocks):
        rows = pl.ds(b * step, step)
        ins.append(
            pltpu.make_async_copy(every.at[:, i, rows], a.at[n % ahead], sem_in.at[n])
        )
        outs.append(
            pltpu.make_async_copy(x.at[:, i, rows, :], out.at[:, i, rows, :], sem_out.at[n])
        )
    for n in range(ahead):
        ins[n].start()
    m = mixing_rows(nobs, peers, values, noise, size, perturb, seen, aug)
    m_top = m.astype(jnp.bfloat16)
    m_low = (m - m_top.astype(F32)).astype(jnp.bfloat16)
    left = jnp.concatenate([m_top, m_top], 1)
    right = jnp.concatenate([m_low, jnp.zeros_like(m_low)], 1)
    left = jnp.concatenate([left, right], 0)
    for n, (b, i) in enumerate(blocks):
        ins[n].wait()
        for g in range(step // 8):
            lines = []
            for z in range(8 * g, 8 * g + 8):
                f = jnp.concatenate([a[n % ahead, k, z] for k in range(peers)], 0)
                top = f.astype(jnp.bfloat16)
                low = (f - top.astype(F32)).astype(jnp.bfloat16)
                both = jnp.concatenate([top, low], 0)
                y = jnp.dot(left, both, preferred_element_type=F32)
                lines.append(a[n % ahead, me, z] + (y[:members] + y[members:]))
            some = pl.ds(b * step + 8 * g, 8)
            x[:, i, some, :] = jnp.swapaxes(jnp.stack(lines, 0), 0, 1)
        outs[n].start()
        if n + ahead < len(blocks):
            ins[n + ahead].start()
    for copy in outs:
        copy.wait()


def update_of(seen, values, noise, size, perturb, every, after=()):
    peers, planes, depth, members, across = every.shape
    nobs = values.shape[0]
    step = 8
    ahead = 12
    count = planes * depth // step
    shape = (members, planes, depth, across)
    return call(
        functools.partial(update_kernel, step, nobs),
        "update",
        jax.ShapeDtypeStruct(shape, F32),
        [VMEM, VMEM, SMEM, VMEM] + [VMEM] * len(seen) + [ANY],
        ANY,
        [
            pltpu.VMEM(shape, F32),
            pltpu.VMEM((ahead, peers, step, members, across), F32),
            pltpu.VMEM((peers * members, 128), F32),
            pltpu.SemaphoreType.DMA((count,)),
            pltpu.SemaphoreType.DMA((count,)),
        ],
        after=after,
    )(values[None], noise[None], size, perturb, *seen, every)


def swap(x, axis, bit):
    return lax.ppermute(x, axis, [(i, i ^ bit) for i in range(lax.axis_size(axis))])


def swaps(parts, axis):
    return [parts[0]] + [swap(parts[k], axis, k) for k in range(1, lax.axis_size(axis))]


def halo(x, side):
    pairs = [(i, i + 1) for i in range(side, lax.axis_size("space") - 1, 2)]
    return lax.ppermute(x, "space", pairs + [(b, a) for a, b in pairs])


def shards(
    log_perm,
    storage,
    head_init,
    well_cells,
    well_rates,
    obs_cells,
    obs_values,
    noise_var,
    step_size,
    perturb,
):
    shape = log_perm.shape
    members, planes, depth, across = shape
    slabs = lax.axis_size("space")
    peers = lax.axis_size("ens")
    names = ("a", "b", "ra", "rb")
    state = {"token": ()}

    def after(*refs):
        state["token"] = refs

    def span(parts, cut):
        return [(x, lo, hi) for x, (lo, hi) in zip(parts, row_spans(depth, cut))]

    def planes_step():
        side_a, side_b, own = planes_of(log_perm, head_init, CUTS[0])
        far_a = [halo(x, 0) for x in side_a]
        far_b = [halo(x, 1) for x in side_b]
        sides = (side_a, side_b, far_a, far_b)
        state["perms"] = {("p", n): span(v, CUTS[0]) for n, v in zip(names, sides)}
        state["own"] = own
        state["every"] = lax.all_gather(own, "ens", axis=0)

    def gather_step():
        *patch, state["forcing"] = gather_of(
            well_cells, well_rates, obs_cells, head_init, storage, state["own"], slabs
        )
        state["patches"] = swaps(patch, "space")
        after(patch[0])

    def local_step():
        seen = local_of(
            depth, across, obs_cells, peers, state["patches"], after=state["token"]
        )
        after(seen)
        bit = 1
        while bit < peers:
            seen = seen + swap(seen, "ens", bit)
            bit *= 2
        state["partial"] = swaps([seen] * slabs, "space")

    def update_step():
        state["updated"] = update_of(
            state["partial"],
            obs_values,
            noise_var,
            step_size,
            perturb,
            state["every"],
            after=state["token"],
        )
        after(state["updated"])

    def whole(ref):
        return [(ref, 0, depth)]

    def pre_step(sweep):
        first = sweep == 1
        perms = state["perms"]
        fields = {k: perms[k] for k in (("p", "a"), ("p", "b"))}
        if first:
            lines = [head_init]
        else:
            lines = [state["forcing"]]
            fields["h", "a"], fields["h", "b"] = (whole(x) for x in state["new"][:2])
            fields["w", "w"] = whole(state["weights"])
        state["pre"] = sweep_of(
            "pre", first, sweep == 3, shape, lines, fields, after=state["token"]
        )
        after(state["pre"][0])

    def sweep_step(sweep, mode):
        first, last = sweep == 1, sweep == 3
        post = mode == "post"
        lines = [head_init] if first else []
        if first or not post:
            lines.append(state["forcing"])
        if first:
            lines.append(storage)
        fields = dict(state["perms"])
        if not first:
            fields["w", "w"] = whole(state["weights"])
            for k, n in enumerate(names):
                if k >= 2 or not post:
                    fields["h", n] = whole(state["new"][k])
        if post:
            fields["t", "t"] = whole(state["pre"][0])
            if first:
                fields["u", "u"] = whole(state["pre"][1])
        token = state["token"]
        for key in WAITS.get(sweep, ()):
            token = token + tuple(state[key])
        out = sweep_of(mode, first, last, shape, lines, fields, after=token)
        if last:
            state["head"] = out[0]
        else:
            if first:
                state["weights"] = out[2]
            sent = out[:2]
            if first:
                held = lax.optimization_barrier((*sent, *state["patches"]))
                sent, state["patches"] = held[:2], list(held[2:])
            state["new"] = (out[0], out[1], halo(sent[0], 0), halo(sent[1], 1))
        after(out[0])

    steps = dict(
        planes=planes_step,
        gather=gather_step,
        local=local_step,
        update=update_step,
    )
    for step in ORDER:
        if isinstance(step, tuple):
            (pre_step if len(step) == 1 else sweep_step)(*step)
        else:
            steps[step]()
    return (state["head"], state["updated"])


def solution(mesh):
    return jax.shard_map(
        shards,
        mesh=mesh,
        in_specs=(
            P("ens", "space", None, None),
            P("space", None, None),
            P("space", None, None),
            P(),
            P(),
            P(),
            P(),
            P(),
            P(),
            P("ens", None),
        ),
        out_specs=(P("ens", "space", None, None), P("ens", "space", None, None)),
        check_vma=False,
    )
```
